32 devices in a mesh: row: 4 (over y, core), col: 8 (over z, x).
Axes of the slice: x: 2, y: 2, z: 4, core: 2. Of those that a mesh axis runs over, the one named last changes fastest.
Arguments:
- stored_inverse: bfloat16 [6, 4, 3, 8, 256, 256], P(None, 'row', None, 'col'), may hold values from -6 to 6
- panel_first: bfloat16 [6, 4, 256, 256], P(None, 'row', 'col'), may hold values from -0.09375 to 0.09375
- panel_second: bfloat16 [6, 4, 256, 256], P(None, 'row', 'col'), may hold values from -0.109375 to 0.109375
- panel_link: bfloat16 [256, 256], replicated, may hold values from -0.375 to 0.375
- inv_first: float32 [256, 256], replicated, as said below
- inv_second: float32 [256, 256], replicated, as said below
- struct_first: int32 [18], replicated, may hold values from 0 to 23, as said below
- struct_second: int32 [12], replicated, may hold values from 0 to 23, as said below
Outputs:
- column_first: float32 [6, 4, 256, 256], P(None, 'row', 'col')
- column_second: float32 [6, 4, 256, 256], P(None, 'row', 'col')
- diag_first: float32 [256, 256], P('col')
- link_block: float32 [256, 256], P('col')
- diag_second: float32 [256, 256], P('col')
The draws below stay inside these ranges and needn't reach their ends.
Inputs may be any that keep to these rules, and one draw needn't show every extreme that they name: `struct_first`: 18 distinct block indices in increasing order; the last is always 24 - 1. `struct_second`: 12 distinct block indices in increasing order, each also listed in struct_first; the last is always 24 - 1; the second supernode's whole structure is the first supernode together with these blocks. `inv_first`: lower triangular with a positive diagonal. `inv_second`: lower triangular with a positive diagonal.
All inputs are finite; a program needn't handle non-finite values.
Results may differ from the reference program's by a relative error of at most 0.0041.
Values may be sent and summed in bfloat16 or wider, within the bound.
No kernel may reach another device: no remote copies, remote signals or barrier semaphores. Data moves between devices by JAX's collectives and lax.ppermute only.
A program may use at most 64 MiB of HBM per device.

```python
import math
import jax
import jax.numpy as jnp
from jax import lax

B = 256
CB = 3
NB = 24
RB = 6
P1 = 18
P2 = 12
N_ROW = 4
N_COL = 8


def lower_factor(key):
    first, second = jax.random.split(key)
    row_index = jnp.arange(B)[:, None]
    col_index = jnp.arange(B)[None, :]
    lower_part = jax.random.normal(first, (B, B), jnp.float32) * (0.8 / math.sqrt(B))
    diagonal = jax.random.uniform(second, (B,), jnp.float32, 0.5, 2.0)
    return jnp.where(row_index > col_index, lower_part, 0.0) + jnp.where(row_index == col_index, diagonal[:, None], 0.0)


def draw_inv_first(key, part):
    return lower_factor(jax.random.fold_in(key, 11))


def draw_inv_second(key, part):
    return lower_factor(jax.random.fold_in(key, 12))


def structure(key):
    shuffled = jax.random.permutation(jax.random.fold_in(key, 5), NB - 1).astype(jnp.int32)
    root_block = jnp.full((1,), NB - 1, jnp.int32)
    return (shuffled, root_block)


def draw_struct_first(key, part):
    shuffled, root_block = structure(key)
    return jnp.sort(jnp.concatenate([shuffled[:P1 - 1], root_block]))


def draw_struct_second(key, part):
    shuffled, root_block = structure(key)
    return jnp.sort(jnp.concatenate([shuffled[:P2 - 1], root_block]))


def levels(own_key, dims, shards, least, largest):
    level = 1.0
    for position, blocks in shards:
        draws = jax.random.uniform(jax.random.fold_in(jax.random.fold_in(own_key, 6), position), (blocks,), jnp.float32, least / len(shards), largest / len(shards))
        level = level * jnp.repeat(jnp.exp(draws), dims[position] // blocks).reshape((-1,) + (1,) * (len(dims) - 1 - position))
    return level


def noise(key, dims, deviation, most, cuts=(), kind=jnp.bfloat16):
    values = deviation * jax.random.normal(key, dims, jnp.float32)
    if cuts:
        values = values * levels(key, dims, cuts, -0.22, 0.18)
    return jnp.clip(values, -most, most).astype(kind)


def setup_inputs(seed: int = 0) -> dict:
    splits = jax.random.split(jax.random.key(seed), 9)
    return {
        "stored_inverse": noise(splits[0], (RB, N_ROW, CB, N_COL, B, B), 1.0, 6.0, ((1, 4), (3, 8))),
        "panel_first": noise(splits[1], (RB, N_ROW, B, B), (P1 * B) ** -0.5, 0.09375, ((1, 4), (2, 8))),
        "panel_second": noise(splits[2], (RB, N_ROW, B, B), (P2 * B) ** -0.5, 0.109375, ((1, 4), (2, 8))),
        "panel_link": noise(splits[3], (B, B), B ** -0.5, 0.375),
        "inv_first": draw_inv_first(jax.random.fold_in(splits[8], 71), 0),
        "inv_second": draw_inv_second(jax.random.fold_in(splits[8], 71), 0),
        "struct_first": draw_struct_first(jax.random.fold_in(splits[8], 71), 0),
        "struct_second": draw_struct_second(jax.random.fold_in(splits[8], 71), 0),
    }


precise = lax.Precision.HIGHEST


def member(struct):
    block_ids = jnp.arange(NB, dtype=jnp.int32)
    return jnp.any(block_ids[:, None] == struct[None, :], axis=1)


def block_products(blocks, factors):
    factors_wide = factors.astype(jnp.float32)

    def one_row(block_row):
        return jnp.einsum("kij,kjl->il", block_row.astype(jnp.float32), factors_wide, precision=precise)

    return lax.map(one_row, blocks)


def factor_blocks(panel, inverse, mask):
    product = jnp.einsum("kij,jl->kil", panel.astype(jnp.float32), inverse, precision=precise)
    return jnp.where(mask[:, None, None], product, 0.0).astype(jnp.bfloat16)


def reference(stored_inverse, panel_first, panel_second, panel_link, inv_first, inv_second, struct_first, struct_second):
    blocks = stored_inverse.reshape(NB, NB, B, B)
    mask_first = member(struct_first)
    mask_second = member(struct_second)
    factor_first = factor_blocks(panel_first.reshape(NB, B, B), inv_first, mask_first)
    column_first = jnp.where(mask_first[:, None, None], -block_products(blocks, factor_first), 0.0)
    diag_first = jnp.dot(inv_first.T, inv_first, precision=precise) - jnp.einsum(
        "kij,kil->jl", factor_first.astype(jnp.float32), column_first, precision=precise)
    factor_second = factor_blocks(panel_second.reshape(NB, B, B), inv_second, mask_second)
    link_wide = jnp.dot(panel_link.astype(jnp.float32), inv_second, precision=precise)
    link_block = -(jnp.einsum("kij,kil->jl", column_first, factor_second.astype(jnp.float32), precision=precise)
                   + jnp.dot(diag_first, link_wide, precision=precise))
    carried = jnp.einsum("kij,jl->kil", column_first, link_wide, precision=precise)
    column_second = jnp.where(mask_second[:, None, None], -(block_products(blocks, factor_second) + carried), 0.0)
    diag_second = (jnp.dot(inv_second.T, inv_second, precision=precise)
                   - jnp.einsum("kij,kil->jl", factor_second.astype(jnp.float32), column_second, precision=precise)
                   - jnp.dot(link_wide.T, link_block, precision=precise))
    return (column_first.reshape(RB, N_ROW, B, B), column_second.reshape(RB, N_ROW, B, B),
            diag_first, link_block, diag_second)
```

```python
import functools

import jax
import jax.numpy as jnp
from jax import lax
from jax.experimental import pallas as pl
from jax.experimental.pallas import tpu as pltpu
from jax.sharding import PartitionSpec as P

precise = lax.Precision.HIGHEST
SMEM = pl.BlockSpec(memory_space=pltpu.SMEM)
VMEM = pl.BlockSpec(memory_space=pltpu.VMEM)


def exact_dot(left, right, left_dim=1):
    dims = (((left_dim,), (0,)), ((), ()))
    return lax.dot_general(left, right, dims, precision=precise, preferred_element_type=jnp.float32)


def listed(struct_ref, blocks, n_row):
    ids = lax.broadcasted_iota(jnp.int32, (blocks, 1, 1), 0) * n_row + lax.axis_index("row")

    def look(place, found):
        return jnp.where(ids == struct_ref[place], 1, found)

    found = lax.fori_loop(0, struct_ref.shape[0], look, jnp.zeros((blocks, 1, 1), jnp.int32))
    return found == 1


def factor_kernel(n_row, cycle, struct1, struct2, panel1, panel2, link, inv1, inv2, own, linked, *parts):
    blocks, slab, width = panel1.shape
    for p, (struct, panel, inverse) in enumerate(((struct1, panel1, inv1), (struct2, panel2, inv2))):
        rows = panel[...].astype(jnp.float32).reshape(blocks * slab, width)
        product = exact_dot(rows, inverse[...]).reshape(blocks, slab, width)
        keep = listed(struct, blocks, n_row)
        own[p] = jnp.where(keep, product, 0.0).astype(jnp.bfloat16)
    turn = lax.rem(lax.axis_index("col"), cycle)
    for s, part in enumerate(parts):
        pick = lax.rem(s - turn + cycle, cycle)
        for p in range(2):
            for b in range(blocks // cycle):
                part[p, b] = own[p, b * cycle + pick]
    linked[...] = exact_dot(link[...].astype(jnp.float32), inv2[...])


def product_kernel(n_row, n_col, first_bits, stored, *rest):
    cycle = n_col // n_row
    pieces = rest[: n_row * cycle]
    keeps = rest[n_row * cycle : n_row * cycle + 2]
    sends = rest[n_row * cycle + 2 : n_row * cycle + 4]
    loose, factor = rest[n_row * cycle + 4 :]
    col_blocks, _, slab, double = loose.shape
    width = double // 2
    here_row, here_col = lax.axis_index("row"), lax.axis_index("col")

    @pl.when(pl.program_id(0) == 0)
    def _():
        group = here_col // n_row
        for m in range(n_row):
            for s in range(cycle):
                piece = pieces[m * cycle + s]
                slot = (here_row ^ m) * cycle + lax.rem(s - group + cycle, cycle)
                for p in range(2):
                    for b in range(col_blocks):
                        loose[b, slot, :, p * width : (p + 1) * width] = piece[p, b].astype(jnp.float32)
        for b in range(col_blocks):
            factor[b] = loose[b].reshape(n_col * slab, double).astype(jnp.bfloat16)

    total = jnp.dot(stored[0, 0], factor[0], preferred_element_type=jnp.float32)
    for b in range(1, col_blocks):
        total += jnp.dot(stored[0, b], factor[b], preferred_element_type=jnp.float32)
    for p in range(2):
        bit = first_bits[p]
        upper = ((here_col >> bit) & 1) == 1
        for j in range(n_col // 2):
            low = ((j >> bit) << (bit + 1)) | (j & ((1 << bit) - 1))
            high = low | (1 << bit)
            a = total[low * slab : (low + 1) * slab, p * width : (p + 1) * width]
            b = total[high * slab : (high + 1) * slab, p * width : (p + 1) * width]
            keeps[p][j, 0] = jnp.where(upper, b, a)
            sends[p][j, 0] = jnp.where(upper, a, b).astype(jnp.bfloat16)


def column_kernel(n_row, struct1, struct2, kept1, came1, kept2, came2, own, linked, column1, column2, mine, *others):
    sums, sends = others[-1], others[:-1]
    blocks, slab, width = column1.shape
    here_col = lax.axis_index("col")
    flat = (blocks * slab, width)
    sum1 = kept1[...] + came1[...].astype(jnp.float32)
    sum2 = kept2[...] + came2[...].astype(jnp.float32)
    link = linked[...]
    col1 = jnp.where(listed(struct1, blocks, n_row), -sum1, 0.0)
    column1[...] = col1
    col1 = col1.reshape(flat)
    carried = exact_dot(col1, link).reshape(sum2.shape)
    col2 = jnp.where(listed(struct2, blocks, n_row), -(sum2 + carried), 0.0)
    column2[...] = col2
    col2 = col2.reshape(flat)
    u1 = own[0].astype(jnp.float32).reshape(flat)
    u2 = own[1].astype(jnp.float32).reshape(flat)
    first = exact_dot(u1, col1, 0)
    top = exact_dot(col1, u2, 0) - exact_dot(first, link)
    second = exact_dot(u2, col2, 0) - exact_dot(link, top, 0)
    sums[0] = first
    sums[1] = top
    sums[2] = second
    for m, out in enumerate((mine,) + sends):
        place = pl.ds(pl.multiple_of((here_col ^ m) * slab, slab), slab)
        out[...] = sums[:, place, :].astype(out.dtype)


def gram_kernel(inv1, inv2, linked, out, whole):
    slab = out.shape[1]
    link = linked[...]
    gram1 = exact_dot(inv1[...], inv1[...], 0)
    across = exact_dot(gram1, link)
    whole[0] = gram1
    whole[1] = -across
    whole[2] = exact_dot(inv2[...], inv2[...], 0) + exact_dot(link, across, 0)
    place = pl.ds(pl.multiple_of(lax.axis_index("col") * slab, slab), slab)
    out[...] = whole[:, place, :]


def swapped(value, axis, size, mask):
    return lax.ppermute(value, axis, [(i, i ^ mask) for i in range(size)])


def body(stored_inverse, panel_first, panel_second, panel_link, inv_first, inv_second, struct_first, struct_second):
    n_row, n_col = lax.axis_size("row"), lax.axis_size("col")
    here_col = lax.axis_index("col")
    row_blocks, _, col_blocks, _, width, _ = stored_inverse.shape
    slab = width // n_col
    cycle = n_col // n_row
    f32, bf16 = jnp.float32, jnp.bfloat16
    shape = jax.ShapeDtypeStruct
    big = pltpu.CompilerParams(vmem_limit_bytes=24 * 1024 * 1024)
    stored = stored_inverse.reshape(row_blocks, col_blocks, width, width)

    made = pl.pallas_call(
        functools.partial(factor_kernel, n_row, cycle),
        out_shape=[shape((2, row_blocks, slab, width), bf16), shape((width, width), f32)]
        + [shape((2, col_blocks, slab, width), bf16)] * cycle,
        in_specs=[SMEM, SMEM] + [VMEM] * 5,
        out_specs=[VMEM] * (2 + cycle),
        compiler_params=big,
        name="factors",
    )(
        struct_first,
        struct_second,
        panel_first.reshape(row_blocks, slab, width),
        panel_second.reshape(row_blocks, slab, width),
        panel_link,
        inv_first,
        inv_second,
    )
    own, linked, parts = made[0], made[1], made[2:]

    got = []
    for s, part in enumerate(parts):
        moves = []
        for r in range(n_row):
            for c in range(n_col):
                j = (s - c) % cycle
                moves.append((r * n_col + c, (c // cycle) * n_col + r + j * n_row))
        got.append(lax.ppermute(part, ("row", "col"), moves))
    pieces = list(got)
    for m in range(1, n_row):
        pieces += [swapped(g, "row", n_row, m) for g in got]

    consts = pl.pallas_call(
        gram_kernel,
        out_shape=shape((3, slab, width), f32),
        scratch_shapes=[pltpu.VMEM((3, width, width), f32)],
        compiler_params=big,
        name="grams",
        cost_estimate=pl.CostEstimate(flops=6 * 8 * width**3, bytes_accessed=8 * width**2, transcendentals=0),
    )(inv_first, inv_second, linked)

    n_bits = n_col.bit_length() - 1
    orders = (list(range(n_bits)), [1, 0] + list(range(2, n_bits)))
    half = (n_col // 2, row_blocks, slab, width)
    whole_piece = pl.BlockSpec((2, col_blocks, slab, width), lambda a: (0, 0, 0, 0))
    out_block = pl.BlockSpec((n_col // 2, 1, slab, width), lambda a: (0, a, 0, 0))
    split = pl.pallas_call(
        functools.partial(product_kernel, n_row, n_col, (orders[0][0], orders[1][0])),
        grid=(row_blocks,),
        out_shape=[shape(half, f32)] * 2 + [shape(half, bf16)] * 2,
        in_specs=[pl.BlockSpec((1, col_blocks, width, width), lambda a: (a, 0, 0, 0))] + [whole_piece] * len(pieces),
        out_specs=[out_block] * 4,
        scratch_shapes=[
            pltpu.VMEM((col_blocks, n_col, slab, 2 * width), f32),
            pltpu.VMEM((col_blocks, width, 2 * width), bf16),
        ],
        compiler_params=big,
        name="products",
    )(stored, *pieces)

    done = []
    for p in range(2):
        keep, send = split[p], split[2 + p]
        left = sorted(set(range(n_bits)) - {orders[p][0]})
        came = swapped(send, "col", n_col, 1 << orders[p][0])
        for bit in orders[p][1:]:
            low = 1 << left.index(bit)
            left.remove(bit)
            view = (-1, 2, low, row_blocks, slab, width)
            total = (keep + came.astype(f32)).reshape(view)
            mine = (here_col >> bit) & 1
            rest = (-1, row_blocks, slab, width)
            send = lax.dynamic_index_in_dim(total, 1 - mine, 1, keepdims=False).astype(bf16).reshape(rest)
            keep = lax.dynamic_index_in_dim(total, mine, 1, keepdims=False).reshape(rest)
            came = swapped(send, "col", n_col, 1 << bit)
        done += [keep[0], came[0]]

    column = shape((row_blocks, slab, width), f32)
    sliver = (3, slab, width)
    results = pl.pallas_call(
        functools.partial(column_kernel, n_row),
        out_shape=[column, column, shape(sliver, f32)] + [shape(sliver, bf16)] * (n_col - 1),
        in_specs=[SMEM, SMEM] + [VMEM] * 6,
        out_specs=[VMEM] * (n_col + 2),
        scratch_shapes=[pltpu.VMEM((3, width, width), f32)],
        compiler_params=big,
        name="columns",
    )(struct_first, struct_second, *done, own, linked)
    column_first, column_second, total = results[:3]
    for m, send in enumerate(results[3:], 1):
        total = total + swapped(send, "col", n_col, m).astype(f32)
    send = total.astype(bf16)
    for m in range(1, n_row):
        total = total + swapped(send, "row", n_row, m).astype(f32)
    diag_first, link_block, diag_second = consts - total
    out = (row_blocks, 1, slab, width)
    return column_first.reshape(out), column_second.reshape(out), diag_first, link_block, diag_second


def solution(mesh):
    placed = (
        P(None, "row", None, "col", None, None),
        P(None, "row", "col", None),
        P(None, "row", "col", None),
        P(),
        P(),
        P(),
        P(),
        P(),
    )
    return jax.shard_map(
        body,
        mesh=mesh,
        in_specs=placed,
        out_specs=(
            P(None, "row", "col", None),
            P(None, "row", "col", None),
            P("col", None),
            P("col", None),
            P("col", None),
        ),
        check_vma=False,
    )
```

```python
import functools

import jax
import jax.numpy as jnp
from jax import lax
from jax.experimental import pallas as pl
from jax.experimental.pallas import tpu as pltpu
from jax.sharding import PartitionSpec as P

precise = lax.Precision.HIGHEST
SMEM = pl.BlockSpec(memory_space=pltpu.SMEM)
VMEM = pl.BlockSpec(memory_space=pltpu.VMEM)
HBM = pl.BlockSpec(memory_space=pltpu.HBM)


def exact_dot(left, right, left_dim=1):
    dims = (((left_dim,), (0,)), ((), ()))
    return lax.dot_general(left, right, dims, precision=precise, preferred_element_type=jnp.float32)


def split_dot(left, right, left_dim=1):
    def halves(value):
        if value.dtype == jnp.bfloat16:
            return [value]
        high = value.astype(jnp.bfloat16)
        return [high, (value - high.astype(jnp.float32)).astype(jnp.bfloat16)]

    dims = (((left_dim,), (0,)), ((), ()))
    total = None
    for i, a in enumerate(halves(left)):
        for j, b in enumerate(halves(right)):
            if i + j < 2:
                term = lax.dot_general(a, b, dims, preferred_element_type=jnp.float32)
                total = term if total is None else total + term
    return total


def listed(struct_ref, blocks, n_row):
    ids = lax.broadcasted_iota(jnp.int32, (blocks, 1, 1), 0) * n_row + lax.axis_index("row")

    def look(place, found):
        return jnp.where(ids == struct_ref[place], 1, found)

    found = lax.fori_loop(0, struct_ref.shape[0], look, jnp.zeros((blocks, 1, 1), jnp.int32))
    return found == 1


def factor_kernel(n_row, cycle, struct1, struct2, *refs):
    sources, (own, linked, *parts) = refs[:5], refs[5 : 7 + cycle]
    held, sems = refs[7 + cycle : 12 + cycle], refs[12 + cycle]
    copies = [pltpu.make_async_copy(a, b, sems.at[i]) for i, (a, b) in enumerate(zip(sources, held))]
    for copy in copies:
        copy.start()
    panel1, panel2, link, inv1, inv2 = held
    blocks, slab, width = panel1.shape
    keep = [listed(struct, blocks, n_row) for struct in (struct1, struct2)]
    turn = lax.rem(lax.axis_index("col"), cycle)
    for copy in copies:
        copy.wait()
    for p, (panel, inverse) in enumerate(((panel1, inv1), (panel2, inv2))):
        rows = panel[...].astype(jnp.float32).reshape(blocks * slab, width)
        product = exact_dot(rows, inverse[...]).reshape(blocks, slab, width)
        own[p] = jnp.where(keep[p], product, 0.0).astype(jnp.bfloat16)
    for s, part in enumerate(parts):
        pick = lax.rem(s - turn + cycle, cycle)
        for p in range(2):
            for b in range(blocks // cycle):
                part[p, b] = own[p, b * cycle + pick]
    linked[...] = exact_dot(link[...].astype(jnp.float32), inv2[...])


def product_kernel(n_row, n_col, first_bits, stored, pieces, *rest):
    cycle = n_col // n_row
    keeps, sends = rest[:2], rest[2:4]
    held, loose, factor, sems = rest[4:]
    row_blocks = held.shape[0]
    col_blocks, _, slab, double = loose.shape
    width = double // 2
    here_row, here_col = lax.axis_index("row"), lax.axis_index("col")
    copies = [pltpu.make_async_copy(stored.at[a], held.at[a], sems.at[a]) for a in range(row_blocks)]
    for copy in copies:
        copy.start()

    group = here_col // n_row
    for m in range(n_row):
        for s in range(cycle):
            slot = (here_row ^ m) * cycle + lax.rem(s - group + cycle, cycle)
            for p in range(2):
                for b in range(col_blocks):
                    loose[b, slot, :, p * width : (p + 1) * width] = pieces[m, s, p, b].astype(jnp.float32)
    for b in range(col_blocks):
        factor[b] = loose[b].reshape(n_col * slab, double).astype(jnp.bfloat16)

    for a in range(row_blocks):
        copies[a].wait()
        total = jnp.dot(held[a, 0], factor[0], preferred_element_type=jnp.float32)
        for b in range(1, col_blocks):
            total += jnp.dot(held[a, b], factor[b], preferred_element_type=jnp.float32)
        for p in range(2):
            bit = first_bits[p]
            upper = ((here_col >> bit) & 1) == 1
            for j in range(n_col // 2):
                low = ((j >> bit) << (bit + 1)) | (j & ((1 << bit) - 1))
                high = low | (1 << bit)
                x = total[low * slab : (low + 1) * slab, p * width : (p + 1) * width]
                y = total[high * slab : (high + 1) * slab, p * width : (p + 1) * width]
                keeps[p][j, a] = jnp.where(upper, y, x)
                sends[p][j, a] = jnp.where(upper, x, y).astype(jnp.bfloat16)


def sum_kernel(own, other, mine1, theirs1, mine2, theirs2, linked, out):
    blocks, slab, width = mine1.shape
    flat = (blocks * slab, width)

    def both(a, b):
        return jnp.concatenate([a.reshape(flat), b.reshape(flat)], axis=0)

    def factor(p):
        return both(own[p].astype(jnp.float32), other[p].astype(jnp.float32)).astype(jnp.bfloat16)

    link = linked[...]
    sum1 = both(mine1[...], theirs1[...])
    u2 = factor(1)
    first = split_dot(factor(0), sum1, 0)
    cross = split_dot(u2, sum1, 0)
    top = cross.T - split_dot(first, link)
    second = split_dot(u2, both(mine2[...], theirs2[...]), 0) - split_dot(cross, link) - split_dot(link, top, 0)
    n_col = width // slab
    out[0] = first.reshape(n_col, slab, width)
    out[1] = top.reshape(n_col, slab, width)
    out[2] = second.reshape(n_col, slab, width)


def column_kernel(n_row, struct1, struct2, kept1, came1, kept2, came2, linked, column1, column2):
    blocks, slab, width = column1.shape
    sum1 = kept1[...] + came1[...].astype(jnp.float32)
    sum2 = kept2[...] + came2[...].astype(jnp.float32)
    col1 = jnp.where(listed(struct1, blocks, n_row), -sum1, 0.0)
    column1[...] = col1
    carried = split_dot(col1.reshape(blocks * slab, width), linked[...]).reshape(sum2.shape)
    column2[...] = jnp.where(listed(struct2, blocks, n_row), -(sum2 + carried), 0.0)


def gram_kernel(inv1, inv2, linked, out, held1, held2, whole, sems):
    copies = [pltpu.make_async_copy(inv1, held1, sems.at[0]), pltpu.make_async_copy(inv2, held2, sems.at[1])]
    for copy in copies:
        copy.start()
    for copy in copies:
        copy.wait()
    slab = out.shape[1]
    link = linked[...]
    gram1 = exact_dot(held1[...], held1[...], 0)
    across = exact_dot(gram1, link)
    whole[0] = gram1
    whole[1] = -across
    whole[2] = exact_dot(held2[...], held2[...], 0) + exact_dot(link, across, 0)
    place = pl.ds(pl.multiple_of(lax.axis_index("col") * slab, slab), slab)
    out[...] = whole[:, place, :]


def swapped(value, axis, size, mask):
    return lax.ppermute(value, axis, [(i, i ^ mask) for i in range(size)])


def halves(value, axis, mine):
    kept = lax.dynamic_index_in_dim(value, mine, axis, keepdims=False)
    sent = lax.dynamic_index_in_dim(value, 1 - mine, axis, keepdims=False)
    return kept, sent.astype(jnp.bfloat16)


def body(stored_inverse, panel_first, panel_second, panel_link, inv_first, inv_second, struct_first, struct_second):
    n_row, n_col = lax.axis_size("row"), lax.axis_size("col")
    here_col = lax.axis_index("col")
    row_blocks, _, col_blocks, _, width, _ = stored_inverse.shape
    slab = width // n_col
    cycle = n_col // n_row
    n_bits = n_col.bit_length() - 1
    f32, bf16 = jnp.float32, jnp.bfloat16
    shape = jax.ShapeDtypeStruct
    big = pltpu.CompilerParams(vmem_limit_bytes=24 * 1024 * 1024)
    stored = stored_inverse.reshape(row_blocks, col_blocks, width, width)
    panel = (row_blocks, slab, width)
    square = pltpu.VMEM((width, width), f32)

    own, linked, *parts = pl.pallas_call(
        functools.partial(factor_kernel, n_row, cycle),
        out_shape=[shape((2,) + panel, bf16), shape((width, width), f32)]
        + [shape((2, col_blocks, slab, width), bf16)] * cycle,
        in_specs=[SMEM, SMEM] + [HBM] * 5,
        out_specs=[VMEM] * (2 + cycle),
        scratch_shapes=[pltpu.VMEM(panel, bf16)] * 2
        + [pltpu.VMEM((width, width), bf16), square, square, pltpu.SemaphoreType.DMA((5,))],
        compiler_params=big,
        name="factors",
    )(struct_first, struct_second, panel_first.reshape(panel), panel_second.reshape(panel), panel_link, inv_first, inv_second)

    got = []
    for s, part in enumerate(parts):
        moves = []
        for r in range(n_row):
            for c in range(n_col):
                j = (s - c) % cycle
                moves.append((r * n_col + c, (c // cycle) * n_col + r + j * n_row))
        got.append(lax.ppermute(part, ("row", "col"), moves))
    pieces = jnp.stack(got)[None]

    consts = pl.pallas_call(
        gram_kernel,
        out_shape=shape((3, slab, width), f32),
        in_specs=[HBM, HBM, VMEM],
        out_specs=VMEM,
        scratch_shapes=[square, square, pltpu.VMEM((3, width, width), f32), pltpu.SemaphoreType.DMA((2,))],
        compiler_params=big,
        name="grams",
        cost_estimate=pl.CostEstimate(flops=6 * 8 * width**3, bytes_accessed=8 * width**2, transcendentals=0),
    )(inv_first, inv_second, linked)

    order = [0]
    bit = n_row // 2
    while bit:
        pieces = jnp.concatenate([pieces, swapped(pieces, "row", n_row, bit)])
        order += [o ^ bit for o in order]
        bit //= 2
    pieces = jnp.stack([pieces[order.index(m)] for m in range(n_row)])
    pieces, consts, own = lax.optimization_barrier((pieces, consts, own))
    other = swapped(own, "col", n_col, n_col // 2)

    orders = (list(range(n_bits)), [1, 0] + list(range(2, n_bits)))
    half = (n_col // 2,) + panel
    split = pl.pallas_call(
        functools.partial(product_kernel, n_row, n_col, (orders[0][0], orders[1][0])),
        out_shape=[shape(half, f32)] * 2 + [shape(half, bf16)] * 2,
        in_specs=[HBM, VMEM],
        out_specs=[VMEM] * 4,
        scratch_shapes=[
            pltpu.VMEM(stored.shape, bf16),
            pltpu.VMEM((col_blocks, n_col, slab, 2 * width), f32),
            pltpu.VMEM((col_blocks, width, 2 * width), bf16),
            pltpu.SemaphoreType.DMA((row_blocks,)),
        ],
        compiler_params=big,
        name="products",
    )(stored, pieces)

    last = []
    for p in range(2):
        keep, send = split[p], split[2 + p]
        left = sorted(set(range(n_bits)) - {orders[p][0]})
        came = swapped(send, "col", n_col, 1 << orders[p][0])
        for bit in orders[p][1:]:
            low = 1 << left.index(bit)
            left.remove(bit)
            total = (keep + came.astype(f32)).reshape((-1, 2, low) + panel)
            keep, send = halves(total, 1, (here_col >> bit) & 1)
            keep, send = keep.reshape((-1,) + panel), send.reshape((-1,) + panel)
            if left:
                came = swapped(send, "col", n_col, 1 << bit)
        theirs = lax.dynamic_index_in_dim(total, 1 - ((here_col >> bit) & 1), 1, keepdims=False)
        last.append((keep.reshape(panel), theirs.reshape(panel), send))

    sums = pl.pallas_call(
        sum_kernel,
        out_shape=shape((3, n_col, slab, width), f32),
        in_specs=[VMEM] * 7,
        out_specs=VMEM,
        compiler_params=big,
        name="sums",
    )(own, other, last[0][0], last[0][1], last[1][0], last[1][1], linked)
    for bit in range(n_bits):
        keep, send = halves(sums.reshape(3, -1, 2, slab, width), 2, (here_col >> bit) & 1)
        sums = keep + swapped(send, "col", n_col, 1 << bit).astype(f32)

    done = []
    for keep, _, send in last:
        done += [keep, swapped(send, "col", n_col, n_col // 2).reshape(panel)]
    column_first, column_second = pl.pallas_call(
        functools.partial(column_kernel, n_row),
        out_shape=[shape(panel, f32)] * 2,
        in_specs=[SMEM, SMEM] + [VMEM] * 5,
        out_specs=[VMEM] * 2,
        compiler_params=big,
        name="columns",
    )(struct_first, struct_second, *done, linked)

    total = sums.reshape(3, slab, width)
    send = total.astype(bf16)
    for m in range(1, n_row):
        total = total + swapped(send, "row", n_row, m).astype(f32)
    diag_first, link_block, diag_second = consts + total
    out = (row_blocks, 1, slab, width)
    return column_first.reshape(out), column_second.reshape(out), diag_first, link_block, diag_second


def solution(mesh):
    placed = (
        P(None, "row", None, "col", None, None),
        P(None, "row", "col", None),
        P(None, "row", "col", None),
        P(),
        P(),
        P(),
        P(),
        P(),
    )
    return jax.shard_map(
        body,
        mesh=mesh,
        in_specs=placed,
        out_specs=(
            P(None, "row", "col", None),
            P(None, "row", "col", None),
            P("col", None),
            P("col", None),
            P("col", None),
        ),
        check_vma=False,
    )
```

```python
import functools

import jax
import jax.numpy as jnp
from jax import lax
from jax.experimental import pallas as pl
from jax.experimental.pallas import tpu as pltpu
from jax.sharding import PartitionSpec as P

precise = lax.Precision.HIGHEST
SMEM = pl.BlockSpec(memory_space=pltpu.SMEM)
VMEM = pl.BlockSpec(memory_space=pltpu.VMEM)
HBM = pl.BlockSpec(memory_space=pltpu.HBM)
ANY = pl.BlockSpec(memory_space=pl.ANY)


def exact_dot(left, right, left_dim=1):
    dims = (((left_dim,), (0,)), ((), ()))
    return lax.dot_general(left, right, dims, precision=precise, preferred_element_type=jnp.float32)


def split_dot(left, right, left_dim=1):
    def halves(value):
        if value.dtype == jnp.bfloat16:
            return [value]
        high = value.astype(jnp.bfloat16)
        return [high, (value - high.astype(jnp.float32)).astype(jnp.bfloat16)]

    dims = (((left_dim,), (0,)), ((), ()))
    total = None
    for i, a in enumerate(halves(left)):
        for j, b in enumerate(halves(right)):
            if i + j < 2:
                term = lax.dot_general(a, b, dims, preferred_element_type=jnp.float32)
                total = term if total is None else total + term
    return total


def listed(struct_ref, blocks, n_row):
    ids = lax.broadcasted_iota(jnp.int32, (blocks, 1, 1), 0) * n_row + lax.axis_index("row")

    def look(place, found):
        return jnp.where(ids == struct_ref[place], 1, found)

    found = lax.fori_loop(0, struct_ref.shape[0], look, jnp.zeros((blocks, 1, 1), jnp.int32))
    return found == 1


def product_kernel(n_row, n_col, first_bits, struct1, struct2, inv1, inv2, stored, pieces, *rest):
    cycle = n_col // n_row
    keeps, sends = rest[:2], rest[2:4]
    held, loose, factor, sems = rest[4:]
    row_blocks = held.shape[0]
    _, col_blocks, _, slab, width = loose.shape
    here_row, here_col = lax.axis_index("row"), lax.axis_index("col")
    copies = [pltpu.make_async_copy(stored.at[a], held.at[a], sems.at[a]) for a in range(row_blocks)]
    for copy in copies:
        copy.start()

    group = here_col // n_row
    for m in range(n_row):
        for s in range(cycle):
            slot = (here_row ^ m) * cycle + lax.rem(s - group + cycle, cycle)
            for p in range(2):
                for b in range(col_blocks):
                    loose[p, b, slot] = pieces[m, s, p, b].astype(jnp.float32)
    for p, (struct, inverse) in enumerate(((struct1, inv1), (struct2, inv2))):

        def look(place, found):
            return tuple(f | (struct[place] == b * n_col + here_col).astype(jnp.int32) for b, f in enumerate(found))

        found = lax.fori_loop(0, struct.shape[0], look, (jnp.int32(0),) * col_blocks)
        blocks = loose[p].reshape(col_blocks * n_col * slab, width).astype(jnp.bfloat16)
        product = split_dot(blocks, inverse[...])
        for b in range(col_blocks):
            block = product[b * width : (b + 1) * width]
            factor[b, :, p * width : (p + 1) * width] = jnp.where(found[b] == 1, block, 0.0).astype(jnp.bfloat16)

    for a in range(row_blocks):
        copies[a].wait()
        total = jnp.dot(held[a, 0], factor[0], preferred_element_type=jnp.float32)
        for b in range(1, col_blocks):
            total += jnp.dot(held[a, b], factor[b], preferred_element_type=jnp.float32)
        for p in range(2):
            bit = first_bits[p]
            upper = ((here_col >> bit) & 1) == 1
            for j in range(n_col // 2):
                low = ((j >> bit) << (bit + 1)) | (j & ((1 << bit) - 1))
                high = low | (1 << bit)
                x = total[low * slab : (low + 1) * slab, p * width : (p + 1) * width]
                y = total[high * slab : (high + 1) * slab, p * width : (p + 1) * width]
                keeps[p][j, a] = jnp.where(upper, y, x)
                sends[p][j, a] = jnp.where(upper, x, y).astype(jnp.bfloat16)


def prepare_kernel(n_row, struct1, struct2, mine1, mine2, other1, other2, link, inv1, inv2, after, rows, linked, out, whole):
    blocks, slab, width = mine1.shape
    for p, (struct, inverse, parts) in enumerate(((struct1, inv1, (mine1, other1)), (struct2, inv2, (mine2, other2)))):
        keep = listed(struct, blocks, n_row)
        for i, part in enumerate(parts):
            flat = part[...].astype(jnp.float32).reshape(blocks * slab, width).astype(jnp.bfloat16)
            product = split_dot(flat, inverse[...]).reshape(blocks, slab, width)
            rows[p, i] = jnp.where(keep, product, 0.0).astype(jnp.bfloat16)
    linked[...] = exact_dot(link[...].astype(jnp.float32), inv2[...])
    link = linked[...]
    gram1 = exact_dot(inv1[...], inv1[...], 0)
    across = exact_dot(gram1, link)
    whole[0] = gram1
    whole[1] = -across
    whole[2] = exact_dot(inv2[...], inv2[...], 0) + exact_dot(link, across, 0)
    place = pl.ds(pl.multiple_of(lax.axis_index("col") * slab, slab), slab)
    out[...] = whole[:, place, :]


def sum_kernel(rows, mine1, theirs1, mine2, theirs2, linked, after, out):
    blocks, slab, width = mine1.shape
    flat = (blocks * slab, width)

    def both(a, b):
        return jnp.concatenate([a.reshape(flat), b.reshape(flat)], axis=0)

    def factor(p):
        return rows[p].astype(jnp.float32).reshape(2 * blocks * slab, width).astype(jnp.bfloat16)

    link = linked[...]
    sum1 = both(mine1[...], theirs1[...])
    u2 = factor(1)
    first = split_dot(factor(0), sum1, 0)
    cross = split_dot(u2, sum1, 0)
    top = cross.T - split_dot(first, link)
    second = split_dot(u2, both(mine2[...], theirs2[...]), 0) - split_dot(cross, link) - split_dot(link, top, 0)
    n_col = width // slab
    out[0] = first.reshape(n_col, slab, width)
    out[1] = top.reshape(n_col, slab, width)
    out[2] = second.reshape(n_col, slab, width)


def column_kernel(n_row, struct1, struct2, kept1, came1, kept2, came2, linked, column1, column2):
    blocks, slab, width = column1.shape
    sum1 = kept1[...] + came1[...].astype(jnp.float32)
    sum2 = kept2[...] + came2[...].astype(jnp.float32)
    col1 = jnp.where(listed(struct1, blocks, n_row), -sum1, 0.0)
    column1[...] = col1
    carried = split_dot(col1.reshape(blocks * slab, width), linked[...]).reshape(sum2.shape)
    column2[...] = jnp.where(listed(struct2, blocks, n_row), -(sum2 + carried), 0.0)


def swapped(value, axis, size, mask):
    return lax.ppermute(value, axis, [(i, i ^ mask) for i in range(size)])


def halves(value, axis, mine):
    kept = lax.dynamic_index_in_dim(value, mine, axis, keepdims=False)
    sent = lax.dynamic_index_in_dim(value, 1 - mine, axis, keepdims=False)
    return kept, sent.astype(jnp.bfloat16)


def body(stored_inverse, panel_first, panel_second, panel_link, inv_first, inv_second, struct_first, struct_second):
    n_row, n_col = lax.axis_size("row"), lax.axis_size("col")
    here_col = lax.axis_index("col")
    row_blocks, _, col_blocks, _, width, _ = stored_inverse.shape
    slab = width // n_col
    cycle = n_col // n_row
    n_bits = n_col.bit_length() - 1
    f32, bf16 = jnp.float32, jnp.bfloat16
    shape = jax.ShapeDtypeStruct
    big = pltpu.CompilerParams(vmem_limit_bytes=24 * 1024 * 1024)
    stored = stored_inverse.reshape(row_blocks, col_blocks, width, width)
    panel = (row_blocks, slab, width)

    panels = [panel_first.reshape(panel), panel_second.reshape(panel)]

    turns = [p.reshape(col_blocks, cycle, slab, width) for p in panels]
    got = []
    for s in range(cycle):
        moves = []
        for r in range(n_row):
            for c in range(n_col):
                j = (s - c) % cycle
                moves.append((r * n_col + c, (c // cycle) * n_col + r + j * n_row))
        pick = (s - here_col) % cycle
        part = jnp.stack([lax.dynamic_index_in_dim(t, pick, 1, keepdims=False) for t in turns])
        got.append(lax.ppermute(part, ("row", "col"), moves))
    pieces = jnp.stack(got)[None]
    others = [swapped(p, "col", n_col, n_col // 2) for p in panels]

    order = [0]
    bit = n_row // 2
    while bit:
        if bit == 1:
            pieces, others[0] = lax.optimization_barrier((pieces, others[0]))
        pieces = jnp.concatenate([pieces, swapped(pieces, "row", n_row, bit)])
        order += [o ^ bit for o in order]
        bit //= 2
    pieces = jnp.stack([pieces[order.index(m)] for m in range(n_row)])
    pieces, others[1] = lax.optimization_barrier((pieces, others[1]))

    orders = (list(range(n_bits)), [1, 0] + list(range(2, n_bits)))
    half = (n_col // 2,) + panel
    split = pl.pallas_call(
        functools.partial(product_kernel, n_row, n_col, (orders[0][0], orders[1][0])),
        out_shape=[shape(half, f32)] * 2 + [shape(half, bf16)] * 2,
        in_specs=[SMEM, SMEM, VMEM, VMEM, HBM, VMEM],
        out_specs=[VMEM] * 4,
        scratch_shapes=[
            pltpu.VMEM(stored.shape, bf16),
            pltpu.VMEM((2, col_blocks, n_col, slab, width), f32),
            pltpu.VMEM((col_blocks, width, 2 * width), bf16),
            pltpu.SemaphoreType.DMA((row_blocks,)),
        ],
        compiler_params=big,
        name="products",
    )(struct_first, struct_second, inv_first, inv_second, stored, pieces)

    rows, linked, consts = pl.pallas_call(
        functools.partial(prepare_kernel, n_row),
        out_shape=[shape((2, 2) + panel, bf16), shape((width, width), f32), shape((3, slab, width), f32)],
        in_specs=[SMEM, SMEM] + [VMEM] * 7 + [ANY],
        out_specs=[VMEM] * 3,
        scratch_shapes=[pltpu.VMEM((3, width, width), f32)],
        compiler_params=big,
        name="prepare",
        cost_estimate=pl.CostEstimate(flops=6 * 10 * width**3, bytes_accessed=8 * width**2, transcendentals=0),
    )(struct_first, struct_second, *panels, *others, panel_link, inv_first, inv_second, split[0])

    last = []
    for p in range(2):
        keep, send = split[p], split[2 + p]
        left = sorted(set(range(n_bits)) - {orders[p][0]})
        came = swapped(send, "col", n_col, 1 << orders[p][0])
        for bit in orders[p][1:]:
            low = 1 << left.index(bit)
            left.remove(bit)
            total = (keep + came.astype(f32)).reshape((-1, 2, low) + panel)
            keep, send = halves(total, 1, (here_col >> bit) & 1)
            keep, send = keep.reshape((-1,) + panel), send.reshape((-1,) + panel)
            if left:
                came = swapped(send, "col", n_col, 1 << bit)
        theirs = lax.dynamic_index_in_dim(total, 1 - ((here_col >> bit) & 1), 1, keepdims=False)
        last.append((keep.reshape(panel), theirs.reshape(panel), send))

    sums = pl.pallas_call(
        sum_kernel,
        out_shape=shape((3, n_col, slab, width), f32),
        in_specs=[VMEM] * 6 + [ANY],
        out_specs=VMEM,
        compiler_params=big,
        name="sums",
    )(rows, last[0][0], last[0][1], last[1][0], last[1][1], linked, consts)
    done = []
    for keep, _, send in last:
        done += [keep, swapped(send, "col", n_col, n_col // 2).reshape(panel)]
    for bit in range(n_bits):
        if bit == n_bits - 1:
            sums, done = lax.optimization_barrier((sums, done))
        keep, send = halves(sums.reshape(3, -1, 2, slab, width), 2, (here_col >> bit) & 1)
        sums = keep + swapped(send, "col", n_col, 1 << bit).astype(f32)

    column_first, column_second = pl.pallas_call(
        functools.partial(column_kernel, n_row),
        out_shape=[shape(panel, f32)] * 2,
        in_specs=[SMEM, SMEM] + [VMEM] * 5,
        out_specs=[VMEM] * 2,
        compiler_params=big,
        name="columns",
    )(struct_first, struct_second, *done, linked)

    total = sums.reshape(3, slab, width)
    send = total.astype(bf16)
    for m in range(1, n_row):
        total = total + swapped(send, "row", n_row, m).astype(f32)
    diag_first, link_block, diag_second = consts + total
    out = (row_blocks, 1, slab, width)
    return column_first.reshape(out), column_second.reshape(out), diag_first, link_block, diag_second


def solution(mesh):
    placed = (
        P(None, "row", None, "col", None, None),
        P(None, "row", "col", None),
        P(None, "row", "col", None),
        P(),
        P(),
        P(),
        P(),
        P(),
    )
    return jax.shard_map(
        body,
        mesh=mesh,
        in_specs=placed,
        out_specs=(
            P(None, "row", "col", None),
            P(None, "row", "col", None),
            P("col", None),
            P("col", None),
            P("col", None),
        ),
        check_vma=False,
    )
```

```python
import functools

import jax
import jax.numpy as jnp
from jax import lax
from jax.experimental import pallas as pl
from jax.experimental.pallas import tpu as pltpu
from jax.sharding import PartitionSpec as P

precise = lax.Precision.HIGHEST
SMEM = pl.BlockSpec(memory_space=pltpu.SMEM)
VMEM = pl.BlockSpec(memory_space=pltpu.VMEM)
HBM = pl.BlockSpec(memory_space=pltpu.HBM)
ANY = pl.BlockSpec(memory_space=pl.ANY)


def exact_dot(left, right, left_dim=1):
    dims = (((left_dim,), (0,)), ((), ()))
    return lax.dot_general(left, right, dims, precision=precise, preferred_element_type=jnp.float32)


def split_dot(left, right, left_dim=1):
    def halves(value):
        if value.dtype == jnp.bfloat16:
            return [value]
        high = value.astype(jnp.bfloat16)
        return [high, (value - high.astype(jnp.float32)).astype(jnp.bfloat16)]

    dims = (((left_dim,), (0,)), ((), ()))
    total = None
    for i, a in enumerate(halves(left)):
        for j, b in enumerate(halves(right)):
            if i + j < 2:
                term = lax.dot_general(a, b, dims, preferred_element_type=jnp.float32)
                total = term if total is None else total + term
    return total


def listed(struct_ref, blocks, n_row):
    ids = lax.broadcasted_iota(jnp.int32, (blocks, 1, 1), 0) * n_row + lax.axis_index("row")

    def look(place, found):
        return jnp.where(ids == struct_ref[place], 1, found)

    found = lax.fori_loop(0, struct_ref.shape[0], look, jnp.zeros((blocks, 1, 1), jnp.int32))
    return found == 1


def slice_of(row, turn, n_row):
    half = n_row // 2
    return 2 * (turn * half + lax.rem(row, half)) + row // half


def place_of(piece, n_row):
    half = n_row // 2
    return (piece % 2) * half + piece // 2 % half, piece // 2 // half


def product_kernel(n_row, n_col, first_bits, struct1, struct2, inv1, inv2, stored, pieces, *rest):
    cycle = n_col // n_row
    keeps, sends = rest[:2], rest[2:4]
    loose, factor = rest[4:]
    row_blocks = stored.shape[0]
    _, col_blocks, _, slab, width = loose.shape
    here_row, here_col = lax.axis_index("row"), lax.axis_index("col")

    group = here_col // n_row
    for m in range(n_row):
        row = here_row ^ m
        for s in range(cycle):
            slot = slice_of(row, lax.rem(s - group + cycle, cycle), n_row)
            for p in range(2):
                for b in range(col_blocks):
                    loose[p, b, slot] = pieces[m, s, p, b].astype(loose.dtype)
    for p, (struct, inverse) in enumerate(((struct1, inv1), (struct2, inv2))):

        def look(place, found):
            return tuple(f | (struct[place] == b * n_col + here_col).astype(jnp.int32) for b, f in enumerate(found))

        found = lax.fori_loop(0, struct.shape[0], look, (jnp.int32(0),) * col_blocks)
        blocks = loose[p].reshape(col_blocks * width, width).astype(jnp.bfloat16)
        product = split_dot(blocks, inverse[...])
        for b in range(col_blocks):
            place = slice(b * width, (b + 1) * width)
            factor[place, p * width : (p + 1) * width] = jnp.where(found[b] == 1, product[place], 0.0).astype(jnp.bfloat16)

    step = 2 if row_blocks % 2 == 0 else 1
    for a in range(0, row_blocks, step):
        wide = [jnp.concatenate([stored[a + i, b] for b in range(col_blocks)], axis=1) for i in range(step)]
        totals = jnp.dot(jnp.concatenate(wide, axis=0), factor[...], preferred_element_type=jnp.float32)
        for i in range(step):
            total = totals[i * width : (i + 1) * width]
            for p in range(2):
                bit = first_bits[p]
                upper = ((here_col >> bit) & 1) == 1
                for j in range(n_col // 2):
                    low = ((j >> bit) << (bit + 1)) | (j & ((1 << bit) - 1))
                    high = low | (1 << bit)
                    x = total[low * slab : (low + 1) * slab, p * width : (p + 1) * width]
                    y = total[high * slab : (high + 1) * slab, p * width : (p + 1) * width]
                    keeps[p][j, a + i] = jnp.where(upper, y, x)
                    sends[p][j, a + i] = jnp.where(upper, x, y).astype(jnp.bfloat16)


def prepare_kernel(n_row, struct1, struct2, mine1, mine2, other, link, inv1, inv2, after, rows, linked, out, whole):
    blocks, slab, width = mine1.shape
    for p, (struct, inverse, parts) in enumerate(((struct1, inv1, (mine1, other.at[0])), (struct2, inv2, (mine2, other.at[1])))):
        keep = listed(struct, blocks, n_row)
        for i, part in enumerate(parts):
            flat = part[...].astype(jnp.float32).reshape(blocks * slab, width).astype(jnp.bfloat16)
            product = split_dot(flat, inverse[...]).reshape(blocks, slab, width)
            rows[p, i] = jnp.where(keep, product, 0.0).astype(jnp.bfloat16)
    linked[...] = exact_dot(link[...].astype(jnp.float32), inv2[...])
    link = linked[...]
    gram1 = exact_dot(inv1[...], inv1[...], 0)
    across = exact_dot(gram1, link)
    whole[0] = gram1
    whole[1] = -across
    whole[2] = exact_dot(inv2[...], inv2[...], 0) + exact_dot(link, across, 0)
    place = pl.ds(pl.multiple_of(lax.axis_index("col") * slab, slab), slab)
    out[...] = whole[:, place, :]


def sum_kernel(rows, mine1, theirs1, mine2, theirs2, linked, after, out):
    blocks, slab, width = mine1.shape
    flat = (blocks * slab, width)

    def both(a, b):
        return jnp.concatenate([a.reshape(flat), b.reshape(flat)], axis=0)

    def factor(p):
        return rows[p].astype(jnp.float32).reshape(2 * blocks * slab, width).astype(jnp.bfloat16)

    link = linked[...]
    sum1 = both(mine1[...], theirs1[...])
    u2 = factor(1)
    first = split_dot(factor(0), sum1, 0)
    cross = split_dot(u2, sum1, 0)
    top = cross.T - split_dot(first, link)
    second = split_dot(u2, both(mine2[...], theirs2[...]), 0) - split_dot(cross, link) - split_dot(link, top, 0)
    n_col = width // slab
    out[0] = first.reshape(n_col, slab, width)
    out[1] = top.reshape(n_col, slab, width)
    out[2] = second.reshape(n_col, slab, width)


def column_kernel(n_row, struct1, struct2, kept1, came1, kept2, came2, linked, column1, column2):
    blocks, slab, width = column1.shape
    sum1 = kept1[...] + came1[...].astype(jnp.float32)
    sum2 = kept2[...] + came2[...].astype(jnp.float32)
    col1 = jnp.where(listed(struct1, blocks, n_row), -sum1, 0.0)
    column1[...] = col1
    carried = split_dot(col1.reshape(blocks * slab, width), linked[...]).reshape(sum2.shape)
    column2[...] = jnp.where(listed(struct2, blocks, n_row), -(sum2 + carried), 0.0)


def swapped(value, axis, size, mask):
    return lax.ppermute(value, axis, [(i, i ^ mask) for i in range(size)])


def halves(value, axis, mine):
    kept = lax.dynamic_index_in_dim(value, mine, axis, keepdims=False)
    sent = lax.dynamic_index_in_dim(value, 1 - mine, axis, keepdims=False)
    return kept, sent.astype(jnp.bfloat16)


def body(stored_inverse, panel_first, panel_second, panel_link, inv_first, inv_second, struct_first, struct_second):
    n_row, n_col = lax.axis_size("row"), lax.axis_size("col")
    here_col = lax.axis_index("col")
    row_blocks, _, col_blocks, _, width, _ = stored_inverse.shape
    slab = width // n_col
    cycle = n_col // n_row
    n_bits = n_col.bit_length() - 1
    f32, bf16 = jnp.float32, jnp.bfloat16
    shape = jax.ShapeDtypeStruct
    big = pltpu.CompilerParams(vmem_limit_bytes=12 * 1024 * 1024)
    stored = stored_inverse.reshape(row_blocks, col_blocks, width, width)
    panel = (row_blocks, slab, width)

    panels = [panel_first.reshape(panel), panel_second.reshape(panel)]

    turns = jnp.stack(panels).reshape(2, col_blocks, cycle, slab, width)
    _, turn = place_of(here_col, n_row)
    got = []
    for s in range(cycle):
        moves = []
        for r in range(n_row):
            for c in range(n_col):
                row, t = place_of(c, n_row)
                moves.append((r * n_col + c, row * n_col + r + (s - t) % cycle * n_row))
        part = lax.dynamic_index_in_dim(turns, (s - turn) % cycle, 2, keepdims=False)
        got.append(lax.ppermute(part, ("row", "col"), moves))
    pieces = jnp.stack(got)[None]

    order = [0]
    bit = n_row // 2
    while bit:
        pieces = jnp.concatenate([pieces, swapped(pieces, "row", n_row, bit)])
        order += [o ^ bit for o in order]
        bit //= 2
    pieces = jnp.stack([pieces[order.index(m)] for m in range(n_row)])

    orders = (list(range(n_bits)), [1, 0] + list(range(2, n_bits)))
    half = (n_col // 2,) + panel
    split = pl.pallas_call(
        functools.partial(product_kernel, n_row, n_col, (orders[0][0], orders[1][0])),
        out_shape=[shape(half, f32)] * 2 + [shape(half, bf16)] * 2,
        in_specs=[SMEM, SMEM] + [VMEM] * 4,
        out_specs=[VMEM] * 4,
        scratch_shapes=[
            pltpu.VMEM((2, col_blocks, n_col, slab, width), bf16 if slab % 16 == 0 else f32),
            pltpu.VMEM((col_blocks * width, 2 * width), bf16),
        ],
        compiler_params=big,
        name="products",
    )(struct_first, struct_second, inv_first, inv_second, stored, pieces)

    panels, pieces = lax.optimization_barrier((panels, pieces))
    other = swapped(jnp.stack(panels), "col", n_col, n_col // 2)
    rows, linked, consts = pl.pallas_call(
        functools.partial(prepare_kernel, n_row),
        out_shape=[shape((2, 2) + panel, bf16), shape((width, width), f32), shape((3, slab, width), f32)],
        in_specs=[SMEM, SMEM] + [VMEM] * 6 + [ANY],
        out_specs=[VMEM] * 3,
        scratch_shapes=[pltpu.VMEM((3, width, width), f32)],
        compiler_params=big,
        name="prepare",
        cost_estimate=pl.CostEstimate(flops=6 * 10 * width**3, bytes_accessed=8 * width**2, transcendentals=0),
    )(struct_first, struct_second, *panels, other, panel_link, inv_first, inv_second, split[0])

    last = []
    for p in range(2):
        keep, send = split[p], split[2 + p]
        left = sorted(set(range(n_bits)) - {orders[p][0]})
        came = swapped(send, "col", n_col, 1 << orders[p][0])
        for bit in orders[p][1:]:
            low = 1 << left.index(bit)
            left.remove(bit)
            total = (keep + came.astype(f32)).reshape((-1, 2, low) + panel)
            keep, send = halves(total, 1, (here_col >> bit) & 1)
            keep, send = keep.reshape((-1,) + panel), send.reshape((-1,) + panel)
            if left:
                came = swapped(send, "col", n_col, 1 << bit)
        theirs = lax.dynamic_index_in_dim(total, 1 - ((here_col >> bit) & 1), 1, keepdims=False)
        last.append((keep.reshape(panel), theirs.reshape(panel), send))

    sums = pl.pallas_call(
        sum_kernel,
        out_shape=shape((3, n_col, slab, width), f32),
        in_specs=[VMEM] * 6 + [ANY],
        out_specs=VMEM,
        compiler_params=big,
        name="sums",
    )(rows, last[0][0], last[0][1], last[1][0], last[1][1], linked, consts)
    done = []
    for keep, _, send in last:
        done += [keep, swapped(send, "col", n_col, n_col // 2).reshape(panel)]
    for bit in range(n_bits):
        if bit == n_bits - 1:
            sums, done[1] = lax.optimization_barrier((sums, done[1]))
        keep, send = halves(sums.reshape(3, -1, 2, slab, width), 2, (here_col >> bit) & 1)
        sums = keep + swapped(send, "col", n_col, 1 << bit).astype(f32)

    total = sums.reshape(3, slab, width)
    total, done[3] = lax.optimization_barrier((total, done[3]))
    column_first, column_second = pl.pallas_call(
        functools.partial(column_kernel, n_row),
        out_shape=[shape(panel, f32)] * 2,
        in_specs=[SMEM, SMEM] + [VMEM] * 5,
        out_specs=[VMEM] * 2,
        compiler_params=big,
        name="columns",
    )(struct_first, struct_second, *done, linked)

    send = total.astype(bf16)
    for m in range(1, n_row):
        total = total + swapped(send, "row", n_row, m).astype(f32)
    diag_first, link_block, diag_second = consts + total
    out = (row_blocks, 1, slab, width)
    return column_first.reshape(out), column_second.reshape(out), diag_first, link_block, diag_second


def solution(mesh):
    placed = (
        P(None, "row", None, "col", None, None),
        P(None, "row", "col", None),
        P(None, "row", "col", None),
        P(),
        P(),
        P(),
        P(),
        P(),
    )
    return jax.shard_map(
        body,
        mesh=mesh,
        in_specs=placed,
        out_specs=(
            P(None, "row", "col", None),
            P(None, "row", "col", None),
            P("col", None),
            P("col", None),
            P("col", None),
        ),
        check_vma=False,
    )
```

```python
import functools

import jax
import jax.numpy as jnp
from jax import lax
from jax.experimental import pallas as pl
from jax.experimental.pallas import tpu as pltpu
from jax.sharding import PartitionSpec as P

precise = lax.Precision.HIGHEST
SMEM = pl.BlockSpec(memory_space=pltpu.SMEM)
VMEM = pl.BlockSpec(memory_space=pltpu.VMEM)
HBM = pl.BlockSpec(memory_space=pltpu.HBM)
ANY = pl.BlockSpec(memory_space=pl.ANY)


def exact_dot(left, right, left_dim=1):
    dims = (((left_dim,), (0,)), ((), ()))
    return lax.dot_general(left, right, dims, precision=precise, preferred_element_type=jnp.float32)


def split_dot(left, right, left_dim=1):
    def halves(value):
        if value.dtype == jnp.bfloat16:
            return [value]
        high = value.astype(jnp.bfloat16)
        return [high, (value - high.astype(jnp.float32)).astype(jnp.bfloat16)]

    dims = (((left_dim,), (0,)), ((), ()))
    total = None
    for i, a in enumerate(halves(left)):
        for j, b in enumerate(halves(right)):
            if i + j < 2:
                term = lax.dot_general(a, b, dims, preferred_element_type=jnp.float32)
                total = term if total is None else total + term
    return total


def listed(struct_ref, blocks, n_row):
    ids = lax.broadcasted_iota(jnp.int32, (blocks, 1, 1), 0) * n_row + lax.axis_index("row")

    def look(place, found):
        return jnp.where(ids == struct_ref[place], 1, found)

    found = lax.fori_loop(0, struct_ref.shape[0], look, jnp.zeros((blocks, 1, 1), jnp.int32))
    return found == 1


def slice_of(row, turn, n_row):
    half = n_row // 2
    return 2 * (turn * half + lax.rem(row, half)) + row // half


def place_of(piece, n_row):
    half = n_row // 2
    return (piece % 2) * half + piece // 2 % half, piece // 2 // half


def product_kernel(n_row, n_col, first_bits, struct1, struct2, inv1, inv2, stored, pieces, *rest):
    cycle = n_col // n_row
    keeps, sends = rest[:2], rest[2:4]
    loose, factor = rest[4:]
    row_blocks = stored.shape[0]
    _, col_blocks, _, slab, width = loose.shape
    here_row, here_col = lax.axis_index("row"), lax.axis_index("col")

    group = here_col // n_row
    for m in range(n_row):
        row = here_row ^ m
        for s in range(cycle):
            slot = slice_of(row, lax.rem(s - group + cycle, cycle), n_row)
            for p in range(2):
                for b in range(col_blocks):
                    loose[p, b, slot] = pieces[m, s, p, b].astype(loose.dtype)
    for p, (struct, inverse) in enumerate(((struct1, inv1), (struct2, inv2))):

        def look(place, found):
            return tuple(f | (struct[place] == b * n_col + here_col).astype(jnp.int32) for b, f in enumerate(found))

        found = lax.fori_loop(0, struct.shape[0], look, (jnp.int32(0),) * col_blocks)
        blocks = loose[p].reshape(col_blocks * width, width).astype(jnp.bfloat16)
        product = split_dot(blocks, inverse[...])
        for b in range(col_blocks):
            place = slice(b * width, (b + 1) * width)
            factor[place, p * width : (p + 1) * width] = jnp.where(found[b] == 1, product[place], 0.0).astype(jnp.bfloat16)

    step = 2 if row_blocks % 2 == 0 else 1
    for a in range(0, row_blocks, step):
        wide = [jnp.concatenate([stored[a + i, b] for b in range(col_blocks)], axis=1) for i in range(step)]
        totals = jnp.dot(jnp.concatenate(wide, axis=0), factor[...], preferred_element_type=jnp.float32)
        for i in range(step):
            total = totals[i * width : (i + 1) * width]
            for p in range(2):
                bit = first_bits[p]
                upper = ((here_col >> bit) & 1) == 1
                for j in range(n_col // 2):
                    low = ((j >> bit) << (bit + 1)) | (j & ((1 << bit) - 1))
                    high = low | (1 << bit)
                    x = total[low * slab : (low + 1) * slab, p * width : (p + 1) * width]
                    y = total[high * slab : (high + 1) * slab, p * width : (p + 1) * width]
                    keeps[p][j, a + i] = jnp.where(upper, y, x)
                    sends[p][j, a + i] = jnp.where(upper, x, y).astype(jnp.bfloat16)


def factor_rows(panel, inverse, keep):
    blocks, slab, width = panel.shape
    flat = panel[...].astype(jnp.float32).reshape(blocks * slab, width).astype(jnp.bfloat16)
    product = split_dot(flat, inverse[...]).reshape(blocks, slab, width)
    return jnp.where(keep, product, 0.0)


def prepare_kernel(n_row, struct1, struct2, mine1, mine2, link, inv1, inv2, after, rows, linked, out, whole):
    blocks, slab, width = mine1.shape
    for p, (struct, mine, inverse) in enumerate(((struct1, mine1, inv1), (struct2, mine2, inv2))):
        rows[p] = factor_rows(mine, inverse, listed(struct, blocks, n_row)).astype(jnp.bfloat16)
    linked[...] = exact_dot(link[...].astype(jnp.float32), inv2[...])
    link = linked[...]
    gram1 = exact_dot(inv1[...], inv1[...], 0)
    across = exact_dot(gram1, link)
    whole[0] = gram1
    whole[1] = -across
    whole[2] = exact_dot(inv2[...], inv2[...], 0) + exact_dot(link, across, 0)
    place = pl.ds(pl.multiple_of(lax.axis_index("col") * slab, slab), slab)
    out[...] = whole[:, place, :]


def sum_kernel(n_row, struct1, struct2, rows, other1, other2, inv1, inv2, mine1, theirs1, mine2, theirs2, linked, after, out):
    blocks, slab, width = mine1.shape
    flat = (blocks * slab, width)

    def both(a, b):
        return jnp.concatenate([a.reshape(flat), b.reshape(flat)], axis=0)

    def factor(p, struct, other, inverse):
        theirs = factor_rows(other, inverse, listed(struct, blocks, n_row))
        return both(rows[p].astype(jnp.float32), theirs).astype(jnp.bfloat16)

    link = linked[...]
    sum1 = both(mine1[...], theirs1[...])
    u2 = factor(1, struct2, other2, inv2)
    first = split_dot(factor(0, struct1, other1, inv1), sum1, 0)
    cross = split_dot(u2, sum1, 0)
    top = cross.T - split_dot(first, link)
    second = split_dot(u2, both(mine2[...], theirs2[...]), 0) - split_dot(cross, link) - split_dot(link, top, 0)
    n_col = width // slab
    out[0] = first.reshape(n_col, slab, width)
    out[1] = top.reshape(n_col, slab, width)
    out[2] = second.reshape(n_col, slab, width)


def column_kernel(n_row, struct1, struct2, kept1, came1, kept2, came2, linked, column1, column2):
    blocks, slab, width = column1.shape
    sum1 = kept1[...] + came1[...].astype(jnp.float32)
    sum2 = kept2[...] + came2[...].astype(jnp.float32)
    col1 = jnp.where(listed(struct1, blocks, n_row), -sum1, 0.0)
    column1[...] = col1
    carried = split_dot(col1.reshape(blocks * slab, width), linked[...]).reshape(sum2.shape)
    column2[...] = jnp.where(listed(struct2, blocks, n_row), -(sum2 + carried), 0.0)


def swapped(value, axis, size, mask):
    return lax.ppermute(value, axis, [(i, i ^ mask) for i in range(size)])


def halves(value, axis, ways):
    kept, sent = (lax.dynamic_index_in_dim(value, way, axis, keepdims=False) for way in ways)
    return kept, sent


def body(stored_inverse, panel_first, panel_second, panel_link, inv_first, inv_second, struct_first, struct_second):
    n_row, n_col = lax.axis_size("row"), lax.axis_size("col")
    here_col = lax.axis_index("col")
    row_blocks, _, col_blocks, _, width, _ = stored_inverse.shape
    slab = width // n_col
    cycle = n_col // n_row
    n_bits = n_col.bit_length() - 1
    f32, bf16 = jnp.float32, jnp.bfloat16
    shape = jax.ShapeDtypeStruct
    big = pltpu.CompilerParams(vmem_limit_bytes=12 * 1024 * 1024)
    stored = stored_inverse.reshape(row_blocks, col_blocks, width, width)
    panel = (row_blocks, slab, width)

    panels = [panel_first.reshape(panel), panel_second.reshape(panel)]
    _, turn = place_of(here_col, n_row)
    picks = [((s - turn + cycle) % cycle).astype(jnp.uint32) for s in range(cycle)]
    ways = [(here_col >> bit) & 1 for bit in range(n_bits)]
    ways = [(way.astype(jnp.uint32), (1 - way).astype(jnp.uint32)) for way in ways]
    panels, picks, ways = lax.optimization_barrier((panels, picks, ways))

    turns = jnp.stack(panels).reshape(2, col_blocks, cycle, slab, width)
    got = []
    for s in range(cycle):
        moves = []
        for r in range(n_row):
            for c in range(n_col):
                row, t = place_of(c, n_row)
                moves.append((r * n_col + c, row * n_col + r + (s - t) % cycle * n_row))
        part = lax.dynamic_index_in_dim(turns, picks[s], 2, keepdims=False)
        got.append(lax.ppermute(part, ("row", "col"), moves))
    pieces = jnp.stack(got)[None]

    order = [0]
    bit = n_row // 2
    while bit:
        pieces = jnp.concatenate([pieces, swapped(pieces, "row", n_row, bit)])
        order += [o ^ bit for o in order]
        bit //= 2
    pieces = jnp.stack([pieces[order.index(m)] for m in range(n_row)])

    orders = (list(range(n_bits)), [1, 0] + list(range(2, n_bits)))
    half = (n_col // 2,) + panel
    split = pl.pallas_call(
        functools.partial(product_kernel, n_row, n_col, (orders[0][0], orders[1][0])),
        out_shape=[shape(half, f32)] * 2 + [shape(half, bf16)] * 2,
        in_specs=[SMEM, SMEM] + [VMEM] * 4,
        out_specs=[VMEM] * 4,
        scratch_shapes=[
            pltpu.VMEM((2, col_blocks, n_col, slab, width), bf16 if slab % 16 == 0 else f32),
            pltpu.VMEM((col_blocks * width, 2 * width), bf16),
        ],
        compiler_params=big,
        name="products",
    )(struct_first, struct_second, inv_first, inv_second, stored, pieces)

    rows, linked, consts = pl.pallas_call(
        functools.partial(prepare_kernel, n_row),
        out_shape=[shape((2,) + panel, bf16), shape((width, width), f32), shape((3, slab, width), f32)],
        in_specs=[SMEM, SMEM] + [VMEM] * 5 + [ANY],
        out_specs=[VMEM] * 3,
        scratch_shapes=[pltpu.VMEM((3, width, width), f32)],
        compiler_params=big,
        name="prepare",
        cost_estimate=pl.CostEstimate(flops=6 * 10 * width**3, bytes_accessed=8 * width**2, transcendentals=0),
    )(struct_first, struct_second, *panels, panel_link, inv_first, inv_second, split[0])

    panels, consts = lax.optimization_barrier((panels, consts))
    others = [swapped(p, "col", n_col, n_col // 2) for p in panels]

    last = []
    for p in range(2):
        keep, send = split[p], split[2 + p]
        left = sorted(set(range(n_bits)) - {orders[p][0]})
        came = swapped(send, "col", n_col, 1 << orders[p][0])
        for bit in orders[p][1:]:
            low = 1 << left.index(bit)
            left.remove(bit)
            total = (keep + came.astype(f32)).reshape((-1, 2, low) + panel)
            keep, theirs = halves(total, 1, ways[bit])
            keep, theirs = keep.reshape((-1,) + panel), theirs.reshape((-1,) + panel)
            if left:
                came = swapped(theirs.astype(bf16), "col", n_col, 1 << bit)
        last.append((keep[0], theirs[0]))

    sums = pl.pallas_call(
        functools.partial(sum_kernel, n_row),
        out_shape=shape((3, n_col, slab, width), f32),
        in_specs=[SMEM, SMEM] + [VMEM] * 10 + [ANY],
        out_specs=VMEM,
        compiler_params=big,
        name="sums",
    )(struct_first, struct_second, rows, *others, inv_first, inv_second, last[0][0], last[0][1], last[1][0], last[1][1], linked, consts)
    done = [swapped(theirs.astype(bf16), "col", n_col, n_col // 2) for _, theirs in last]
    for bit in range(n_bits):
        if bit >= n_bits - 2:
            sums, done[bit - n_bits + 2] = lax.optimization_barrier((sums, done[bit - n_bits + 2]))
        keep, send = halves(sums.reshape(3, -1, 2, slab, width), 2, ways[bit])
        sums = keep + swapped(send.astype(bf16), "col", n_col, 1 << bit).astype(f32)

    total = sums.reshape(3, slab, width)
    column_first, column_second = pl.pallas_call(
        functools.partial(column_kernel, n_row),
        out_shape=[shape(panel, f32)] * 2,
        in_specs=[SMEM, SMEM] + [VMEM] * 5,
        out_specs=[VMEM] * 2,
        compiler_params=big,
        name="columns",
    )(struct_first, struct_second, last[0][0], done[0], last[1][0], done[1], linked)

    send = total.astype(bf16)
    for m in range(1, n_row):
        total = total + swapped(send, "row", n_row, m).astype(f32)
    diag_first, link_block, diag_second = consts + total
    out = (row_blocks, 1, slab, width)
    return column_first.reshape(out), column_second.reshape(out), diag_first, link_block, diag_second


def solution(mesh):
    placed = (
        P(None, "row", None, "col", None, None),
        P(None, "row", "col", None),
        P(None, "row", "col", None),
        P(),
        P(),
        P(),
        P(),
        P(),
    )
    return jax.shard_map(
        body,
        mesh=mesh,
        in_specs=placed,
        out_specs=(
            P(None, "row", "col", None),
            P(None, "row", "col", None),
            P("col", None),
            P("col", None),
            P("col", None),
        ),
        check_vma=False,
    )
```

```python
import functools

import jax
import jax.numpy as jnp
from jax import lax
from jax.experimental import pallas as pl
from jax.experimental.pallas import tpu as pltpu
from jax.sharding import PartitionSpec as P

precise = lax.Precision.HIGHEST
SMEM = pl.BlockSpec(memory_space=pltpu.SMEM)
VMEM = pl.BlockSpec(memory_space=pltpu.VMEM)
HBM = pl.BlockSpec(memory_space=pltpu.HBM)
ANY = pl.BlockSpec(memory_space=pl.ANY)


def exact_dot(left, right, left_dim=1):
    dims = (((left_dim,), (0,)), ((), ()))
    return lax.dot_general(left, right, dims, precision=precise, preferred_element_type=jnp.float32)


def split_dot(left, right, left_dim=1):
    def halves(value):
        if value.dtype == jnp.bfloat16:
            return [value]
        high = value.astype(jnp.bfloat16)
        return [high, (value - high.astype(jnp.float32)).astype(jnp.bfloat16)]

    dims = (((left_dim,), (0,)), ((), ()))
    total = None
    for i, a in enumerate(halves(left)):
        for j, b in enumerate(halves(right)):
            if i + j < 2:
                term = lax.dot_general(a, b, dims, preferred_element_type=jnp.float32)
                total = term if total is None else total + term
    return total


def listed(struct_ref, blocks, n_row):
    ids = lax.broadcasted_iota(jnp.int32, (blocks, 1, 1), 0) * n_row + lax.axis_index("row")

    def look(place, found):
        return jnp.where(ids == struct_ref[place], 1, found)

    found = lax.fori_loop(0, struct_ref.shape[0], look, jnp.zeros((blocks, 1, 1), jnp.int32))
    return found == 1


def slice_of(row, turn, n_row):
    return turn * n_row + row


def place_of(piece, n_row):
    return piece % n_row, piece // n_row


def product_kernel(n_row, n_col, first_bits, struct1, struct2, inv1, inv2, stored, pieces, *rest):
    cycle = n_col // n_row
    keeps, sends = rest[:2], rest[2:4]
    loose, factor = rest[4:]
    row_blocks = stored.shape[0]
    _, col_blocks, _, slab, width = loose.shape
    here_row, here_col = lax.axis_index("row"), lax.axis_index("col")

    group = here_col // n_row
    for m in range(n_row):
        row = here_row ^ m
        for s in range(cycle):
            slot = slice_of(row, lax.rem(s - group + cycle, cycle), n_row)
            for p in range(2):
                for b in range(col_blocks):
                    loose[p, b, slot] = pieces[m, s, p, b].astype(loose.dtype)
    for p, (struct, inverse) in enumerate(((struct1, inv1), (struct2, inv2))):

        def look(place, found):
            return tuple(f | (struct[place] == b * n_col + here_col).astype(jnp.int32) for b, f in enumerate(found))

        found = lax.fori_loop(0, struct.shape[0], look, (jnp.int32(0),) * col_blocks)
        blocks = loose[p].reshape(col_blocks * width, width).astype(jnp.bfloat16)
        product = split_dot(blocks, inverse[...])
        for b in range(col_blocks):
            place = slice(b * width, (b + 1) * width)
            factor[place, p * width : (p + 1) * width] = jnp.where(found[b] == 1, product[place], 0.0).astype(jnp.bfloat16)

    step = 2 if row_blocks % 2 == 0 else 1
    for a in range(0, row_blocks, step):
        wide = [jnp.concatenate([stored[a + i, b] for b in range(col_blocks)], axis=1) for i in range(step)]
        totals = jnp.dot(jnp.concatenate(wide, axis=0), factor[...], preferred_element_type=jnp.float32)
        for i in range(step):
            total = totals[i * width : (i + 1) * width]
            for p in range(2):
                bit = first_bits[p]
                upper = ((here_col >> bit) & 1) == 1
                for j in range(n_col // 2):
                    low = ((j >> bit) << (bit + 1)) | (j & ((1 << bit) - 1))
                    high = low | (1 << bit)
                    x = total[low * slab : (low + 1) * slab, p * width : (p + 1) * width]
                    y = total[high * slab : (high + 1) * slab, p * width : (p + 1) * width]
                    keeps[p][j, a + i] = jnp.where(upper, y, x)
                    sends[p][j, a + i] = jnp.where(upper, x, y).astype(jnp.bfloat16)


def factor_rows(panel, inverse, keep):
    blocks, slab, width = panel.shape
    flat = panel[...].astype(jnp.float32).reshape(blocks * slab, width).astype(jnp.bfloat16)
    product = split_dot(flat, inverse[...]).reshape(blocks, slab, width)
    return jnp.where(keep, product, 0.0)


def prepare_kernel(n_row, struct1, struct2, mine1, mine2, link, inv1, inv2, after, rows, linked, out, whole):
    blocks, slab, width = mine1.shape
    for p, (struct, mine, inverse) in enumerate(((struct1, mine1, inv1), (struct2, mine2, inv2))):
        rows[p] = factor_rows(mine, inverse, listed(struct, blocks, n_row)).astype(jnp.bfloat16)
    linked[...] = exact_dot(link[...].astype(jnp.float32), inv2[...])
    link = linked[...]
    gram1 = exact_dot(inv1[...], inv1[...], 0)
    across = exact_dot(gram1, link)
    whole[0] = gram1
    whole[1] = -across
    whole[2] = exact_dot(inv2[...], inv2[...], 0) + exact_dot(link, across, 0)
    place = pl.ds(pl.multiple_of(lax.axis_index("col") * slab, slab), slab)
    out[...] = whole[:, place, :]


def sum_kernel(rows, kept1, came1, kept2, came2, linked, after, out):
    blocks, slab, width = kept1.shape
    flat = (blocks * slab, width)
    sum1 = (kept1[...] + came1[...].astype(jnp.float32)).reshape(flat)
    sum2 = (kept2[...] + came2[...].astype(jnp.float32)).reshape(flat)
    u1, u2 = (rows[p].astype(jnp.float32).reshape(flat).astype(jnp.bfloat16) for p in range(2))
    link = linked[...]
    first = split_dot(u1, sum1, 0)
    cross = split_dot(u2, sum1, 0)
    top = cross.T - split_dot(first, link)
    second = split_dot(u2, sum2, 0) - split_dot(cross, link) - split_dot(link, top, 0)
    for i, part in enumerate((first, top, second)):
        out[:, i] = part.reshape(width // slab, slab, width).astype(out.dtype)


def column_kernel(n_row, struct1, struct2, kept1, came1, kept2, came2, linked, column1, column2):
    blocks, slab, width = column1.shape
    sum1 = kept1[...] + came1[...].astype(jnp.float32)
    sum2 = kept2[...] + came2[...].astype(jnp.float32)
    col1 = jnp.where(listed(struct1, blocks, n_row), -sum1, 0.0)
    column1[...] = col1
    carried = split_dot(col1.reshape(blocks * slab, width), linked[...]).reshape(sum2.shape)
    column2[...] = jnp.where(listed(struct2, blocks, n_row), -(sum2 + carried), 0.0)


def swapped(value, axis, size, mask):
    return lax.ppermute(value, axis, [(i, i ^ mask) for i in range(size)])


def halves(value, axis, ways):
    kept, sent = (lax.dynamic_index_in_dim(value, way, axis, keepdims=False) for way in ways)
    return kept, sent


def body(stored_inverse, panel_first, panel_second, panel_link, inv_first, inv_second, struct_first, struct_second):
    n_row, n_col = lax.axis_size("row"), lax.axis_size("col")
    here_col = lax.axis_index("col")
    row_blocks, _, col_blocks, _, width, _ = stored_inverse.shape
    slab = width // n_col
    cycle = n_col // n_row
    n_bits = n_col.bit_length() - 1
    f32, bf16 = jnp.float32, jnp.bfloat16
    shape = jax.ShapeDtypeStruct
    big = pltpu.CompilerParams(vmem_limit_bytes=12 * 1024 * 1024)
    stored = stored_inverse.reshape(row_blocks, col_blocks, width, width)
    panel = (row_blocks, slab, width)

    panels = [panel_first.reshape(panel), panel_second.reshape(panel)]
    _, turn = place_of(here_col, n_row)
    picks = [((s - turn + cycle) % cycle).astype(jnp.uint32) for s in range(cycle)]
    ways = [(here_col >> bit) & 1 for bit in range(n_bits)]
    ways = [(way.astype(jnp.uint32), (1 - way).astype(jnp.uint32)) for way in ways]
    panels, picks, ways = lax.optimization_barrier((panels, picks, ways))

    turns = jnp.stack(panels).reshape(2, col_blocks, cycle, slab, width)
    got = []
    for s in range(cycle):
        moves = []
        for r in range(n_row):
            for c in range(n_col):
                row, t = place_of(c, n_row)
                moves.append((r * n_col + c, row * n_col + r + (s - t) % cycle * n_row))
        part = lax.dynamic_index_in_dim(turns, picks[s], 2, keepdims=False)
        got.append(lax.ppermute(part, ("row", "col"), moves))
    pieces = jnp.stack(got)[None]

    order = [0]
    bit = n_row // 2
    while bit:
        pieces = jnp.concatenate([pieces, swapped(pieces, "row", n_row, bit)])
        order += [o ^ bit for o in order]
        bit //= 2
    pieces = jnp.stack([pieces[order.index(m)] for m in range(n_row)])

    orders = (list(range(1, n_bits)) + [0], list(range(n_bits)))
    half = (n_col // 2,) + panel
    split = pl.pallas_call(
        functools.partial(product_kernel, n_row, n_col, (orders[0][0], orders[1][0])),
        out_shape=[shape(half, f32)] * 2 + [shape(half, bf16)] * 2,
        in_specs=[SMEM, SMEM] + [VMEM] * 4,
        out_specs=[VMEM] * 4,
        scratch_shapes=[
            pltpu.VMEM((2, col_blocks, n_col, slab, width), bf16 if slab % 16 == 0 else f32),
            pltpu.VMEM((col_blocks * width, 2 * width), bf16),
        ],
        compiler_params=big,
        name="products",
    )(struct_first, struct_second, inv_first, inv_second, stored, pieces)

    rows, linked, consts = pl.pallas_call(
        functools.partial(prepare_kernel, n_row),
        out_shape=[shape((2,) + panel, bf16), shape((width, width), f32), shape((3, slab, width), f32)],
        in_specs=[SMEM, SMEM] + [VMEM] * 5 + [ANY],
        out_specs=[VMEM] * 3,
        scratch_shapes=[pltpu.VMEM((3, width, width), f32)],
        compiler_params=big,
        name="prepare",
        cost_estimate=pl.CostEstimate(flops=6 * 10 * width**3, bytes_accessed=8 * width**2, transcendentals=0),
    )(struct_first, struct_second, *panels, panel_link, inv_first, inv_second, split[0])

    last = []
    for p in range(2):
        keep, came = split[p], swapped(split[2 + p], "col", n_col, 1 << orders[p][0])
        left = sorted(set(range(n_bits)) - {orders[p][0]})
        for bit in orders[p][1:]:
            low = 1 << left.index(bit)
            left.remove(bit)
            total = (keep + came.astype(f32)).reshape((-1, 2, low) + panel)
            keep, send = halves(total, 1, ways[bit])
            keep = keep.reshape((-1,) + panel)
            came = swapped(send.astype(bf16).reshape((-1,) + panel), "col", n_col, 1 << bit)
        last += [keep[0], came[0]]

    sums = pl.pallas_call(
        sum_kernel,
        out_shape=shape((n_col, 3, slab, width), bf16),
        in_specs=[VMEM] * 6 + [ANY],
        out_specs=VMEM,
        compiler_params=big,
        name="sums",
    )(rows, *last, linked, consts)
    sums = lax.all_to_all(sums, "col", 0, 0, tiled=True)

    column_first, column_second = pl.pallas_call(
        functools.partial(column_kernel, n_row),
        out_shape=[shape(panel, f32)] * 2,
        in_specs=[SMEM, SMEM] + [VMEM] * 5,
        out_specs=[VMEM] * 2,
        compiler_params=big,
        name="columns",
    )(struct_first, struct_second, *last, linked)

    total = jnp.sum(sums.astype(f32), axis=0)
    send = total.astype(bf16)
    for m in range(1, n_row):
        total = total + swapped(send, "row", n_row, m).astype(f32)
    diag_first, link_block, diag_second = consts + total
    out = (row_blocks, 1, slab, width)
    return column_first.reshape(out), column_second.reshape(out), diag_first, link_block, diag_second


def solution(mesh):
    placed = (
        P(None, "row", None, "col", None, None),
        P(None, "row", "col", None),
        P(None, "row", "col", None),
        P(),
        P(),
        P(),
        P(),
        P(),
    )
    return jax.shard_map(
        body,
        mesh=mesh,
        in_specs=placed,
        out_specs=(
            P(None, "row", "col", None),
            P(None, "row", "col", None),
            P("col", None),
            P("col", None),
            P("col", None),
        ),
        check_vma=False,
    )
```

```python
import functools

import jax
import jax.numpy as jnp
from jax import lax
from jax.experimental import pallas as pl
from jax.experimental.pallas import tpu as pltpu
from jax.sharding import PartitionSpec as P

precise = lax.Precision.HIGHEST
SMEM = pl.BlockSpec(memory_space=pltpu.SMEM)
VMEM = pl.BlockSpec(memory_space=pltpu.VMEM)
HBM = pl.BlockSpec(memory_space=pltpu.HBM)
ANY = pl.BlockSpec(memory_space=pl.ANY)


def exact_dot(left, right, left_dim=1):
    dims = (((left_dim,), (0,)), ((), ()))
    return lax.dot_general(left, right, dims, precision=precise, preferred_element_type=jnp.float32)


def split_dot(left, right, left_dim=1):
    def halves(value):
        if value.dtype == jnp.bfloat16:
            return [value]
        high = value.astype(jnp.bfloat16)
        return [high, (value - high.astype(jnp.float32)).astype(jnp.bfloat16)]

    dims = (((left_dim,), (0,)), ((), ()))
    total = None
    for i, a in enumerate(halves(left)):
        for j, b in enumerate(halves(right)):
            if i + j < 2:
                term = lax.dot_general(a, b, dims, preferred_element_type=jnp.float32)
                total = term if total is None else total + term
    return total


def listed(struct_ref, blocks, n_row):
    ids = lax.broadcasted_iota(jnp.int32, (blocks, 1, 1), 0) * n_row + lax.axis_index("row")

    def look(place, found):
        return jnp.where(ids == struct_ref[place], 1, found)

    found = lax.fori_loop(0, struct_ref.shape[0], look, jnp.zeros((blocks, 1, 1), jnp.int32))
    return found == 1


def slice_of(row, turn, n_row):
    return turn * n_row + row


def place_of(piece, n_row):
    return piece % n_row, piece // n_row


def product_kernel(n_row, n_col, first_bits, struct1, struct2, inv1, inv2, stored, pieces, *rest):
    cycle = n_col // n_row
    keeps, sends = rest[:2], rest[2:4]
    loose, factor = rest[4:]
    row_blocks = stored.shape[0]
    _, col_blocks, _, slab, width = loose.shape
    here_row, here_col = lax.axis_index("row"), lax.axis_index("col")

    group = here_col // n_row
    for m in range(n_row):
        row = here_row ^ m
        for s in range(cycle):
            slot = slice_of(row, lax.rem(s - group + cycle, cycle), n_row)
            for p in range(2):
                for b in range(col_blocks):
                    loose[p, b, slot] = pieces[m, s, p, b].astype(loose.dtype)
    for p, (struct, inverse) in enumerate(((struct1, inv1), (struct2, inv2))):

        def look(place, found):
            return tuple(f | (struct[place] == b * n_col + here_col).astype(jnp.int32) for b, f in enumerate(found))

        found = lax.fori_loop(0, struct.shape[0], look, (jnp.int32(0),) * col_blocks)
        blocks = loose[p].reshape(col_blocks * width, width).astype(jnp.bfloat16)
        product = split_dot(blocks, inverse[...])
        for b in range(col_blocks):
            place = slice(b * width, (b + 1) * width)
            factor[place, p * width : (p + 1) * width] = jnp.where(found[b] == 1, product[place], 0.0).astype(jnp.bfloat16)

    step = 2 if row_blocks % 2 == 0 else 1
    for a in range(0, row_blocks, step):
        wide = [jnp.concatenate([stored[a + i, b] for b in range(col_blocks)], axis=1) for i in range(step)]
        totals = jnp.dot(jnp.concatenate(wide, axis=0), factor[...], preferred_element_type=jnp.float32)
        for i in range(step):
            total = totals[i * width : (i + 1) * width]
            for p in range(2):
                bit = first_bits[p]
                upper = ((here_col >> bit) & 1) == 1
                for j in range(n_col // 2):
                    low = ((j >> bit) << (bit + 1)) | (j & ((1 << bit) - 1))
                    high = low | (1 << bit)
                    x = total[low * slab : (low + 1) * slab, p * width : (p + 1) * width]
                    y = total[high * slab : (high + 1) * slab, p * width : (p + 1) * width]
                    keeps[p][j, a + i] = jnp.where(upper, y, x)
                    sends[p][j, a + i] = jnp.where(upper, x, y).astype(jnp.bfloat16)


def factor_rows(panel, inverse, keep):
    blocks, slab, width = panel.shape
    flat = panel[...].astype(jnp.float32).reshape(blocks * slab, width).astype(jnp.bfloat16)
    product = split_dot(flat, inverse[...]).reshape(blocks, slab, width)
    return jnp.where(keep, product, 0.0)


def prepare_kernel(n_row, struct1, struct2, mine1, mine2, link, inv1, inv2, after, rows, linked, out, whole):
    blocks, slab, width = mine1.shape
    for p, (struct, mine, inverse) in enumerate(((struct1, mine1, inv1), (struct2, mine2, inv2))):
        rows[p] = factor_rows(mine, inverse, listed(struct, blocks, n_row)).astype(jnp.bfloat16)
    linked[...] = exact_dot(link[...].astype(jnp.float32), inv2[...])
    link = linked[...]
    gram1 = exact_dot(inv1[...], inv1[...], 0)
    across = exact_dot(gram1, link)
    whole[0] = gram1
    whole[1] = -across
    whole[2] = exact_dot(inv2[...], inv2[...], 0) + exact_dot(link, across, 0)
    place = pl.ds(pl.multiple_of(lax.axis_index("col") * slab, slab), slab)
    out[...] = whole[:, place, :]


def partner_kernel(n_row, struct1, struct2, other1, other2, inv1, inv2, after1, after2, rows):
    for p, (struct, other, inverse) in enumerate(((struct1, other1, inv1), (struct2, other2, inv2))):
        keep = listed(struct, other.shape[0], n_row)
        rows[p] = factor_rows(other, inverse, keep).astype(jnp.bfloat16)


def sum_kernel(rows, others, mine1, theirs1, mine2, theirs2, linked, after, out):
    blocks, slab, width = mine1.shape
    flat = (blocks * slab, width)

    def both(a, b):
        return jnp.concatenate([a.reshape(flat), b.reshape(flat)], axis=0)

    def factor(p):
        return both(rows[p].astype(jnp.float32), others[p].astype(jnp.float32)).astype(jnp.bfloat16)

    link = linked[...]
    sum1 = both(mine1[...], theirs1[...])
    u2 = factor(1)
    first = split_dot(factor(0), sum1, 0)
    cross = split_dot(u2, sum1, 0)
    top = cross.T - split_dot(first, link)
    second = split_dot(u2, both(mine2[...], theirs2[...]), 0) - split_dot(cross, link) - split_dot(link, top, 0)
    half = width // 2
    for i, part in enumerate((first, top, second)):
        part = part.reshape(width // slab, slab, width)
        for h in range(2):
            out[h, :, i] = part[:, :, h * half : (h + 1) * half]


def column_kernel(n_row, struct1, struct2, kept1, came1, kept2, came2, linked, column1, column2):
    blocks, slab, width = column1.shape
    sum1 = kept1[...] + came1[...].astype(jnp.float32)
    sum2 = kept2[...] + came2[...].astype(jnp.float32)
    col1 = jnp.where(listed(struct1, blocks, n_row), -sum1, 0.0)
    column1[...] = col1
    carried = split_dot(col1.reshape(blocks * slab, width), linked[...]).reshape(sum2.shape)
    column2[...] = jnp.where(listed(struct2, blocks, n_row), -(sum2 + carried), 0.0)


def swapped(value, axis, size, mask):
    return lax.ppermute(value, axis, [(i, i ^ mask) for i in range(size)])


def halves(value, axis, ways):
    kept, sent = (lax.dynamic_index_in_dim(value, way, axis, keepdims=False) for way in ways)
    return kept, sent


def body(stored_inverse, panel_first, panel_second, panel_link, inv_first, inv_second, struct_first, struct_second):
    n_row, n_col = lax.axis_size("row"), lax.axis_size("col")
    here_col = lax.axis_index("col")
    row_blocks, _, col_blocks, _, width, _ = stored_inverse.shape
    slab = width // n_col
    cycle = n_col // n_row
    n_bits = n_col.bit_length() - 1
    f32, bf16 = jnp.float32, jnp.bfloat16
    shape = jax.ShapeDtypeStruct
    big = pltpu.CompilerParams(vmem_limit_bytes=12 * 1024 * 1024)
    stored = stored_inverse.reshape(row_blocks, col_blocks, width, width)
    panel = (row_blocks, slab, width)

    panels = [panel_first.reshape(panel), panel_second.reshape(panel)]
    _, turn = place_of(here_col, n_row)
    picks = [((s - turn + cycle) % cycle).astype(jnp.uint32) for s in range(cycle)]
    ways = [(here_col >> bit) & 1 for bit in range(n_bits)]
    ways = [(way.astype(jnp.uint32), (1 - way).astype(jnp.uint32)) for way in ways]
    core = lax.axis_index("row") & 1
    cores = (core.astype(jnp.uint32), (1 - core).astype(jnp.uint32))
    panels, picks, ways, cores = lax.optimization_barrier((panels, picks, ways, cores))

    turns = jnp.stack(panels).reshape(2, col_blocks, cycle, slab, width)
    got = []
    for s in range(cycle):
        moves = []
        for r in range(n_row):
            for c in range(n_col):
                row, t = place_of(c, n_row)
                moves.append((r * n_col + c, row * n_col + r + (s - t) % cycle * n_row))
        part = lax.dynamic_index_in_dim(turns, picks[s], 2, keepdims=False)
        got.append(lax.ppermute(part, ("row", "col"), moves))
    pieces = jnp.stack(got)[None]

    order = [0]
    bit = n_row // 2
    while bit:
        pieces = jnp.concatenate([pieces, swapped(pieces, "row", n_row, bit)])
        order += [o ^ bit for o in order]
        bit //= 2
    pieces = jnp.stack([pieces[order.index(m)] for m in range(n_row)])

    orders = (list(range(n_bits)), [1, 0] + list(range(2, n_bits)))
    half = (n_col // 2,) + panel
    split = pl.pallas_call(
        functools.partial(product_kernel, n_row, n_col, (orders[0][0], orders[1][0])),
        out_shape=[shape(half, f32)] * 2 + [shape(half, bf16)] * 2,
        in_specs=[SMEM, SMEM] + [VMEM] * 4,
        out_specs=[VMEM] * 4,
        scratch_shapes=[
            pltpu.VMEM((2, col_blocks, n_col, slab, width), bf16 if slab % 16 == 0 else f32),
            pltpu.VMEM((col_blocks * width, 2 * width), bf16),
        ],
        compiler_params=big,
        name="products",
    )(struct_first, struct_second, inv_first, inv_second, stored, pieces)

    rows, linked, consts = pl.pallas_call(
        functools.partial(prepare_kernel, n_row),
        out_shape=[shape((2,) + panel, bf16), shape((width, width), f32), shape((3, slab, width), f32)],
        in_specs=[SMEM, SMEM] + [VMEM] * 5 + [ANY],
        out_specs=[VMEM] * 3,
        scratch_shapes=[pltpu.VMEM((3, width, width), f32)],
        compiler_params=big,
        name="prepare",
        cost_estimate=pl.CostEstimate(flops=6 * 10 * width**3, bytes_accessed=8 * width**2, transcendentals=0),
    )(struct_first, struct_second, *panels, panel_link, inv_first, inv_second, split[0])

    panels, consts = lax.optimization_barrier((panels, consts))
    others = [swapped(p, "col", n_col, n_col // 2) for p in panels]

    last, after = [], []
    for p in range(2):
        keep, came = split[p], swapped(split[2 + p], "col", n_col, 1 << orders[p][0])
        after.append(came)
        left = sorted(set(range(n_bits)) - {orders[p][0]})
        for bit in orders[p][1:]:
            low = 1 << left.index(bit)
            left.remove(bit)
            total = (keep + came.astype(f32)).reshape((-1, 2, low) + panel)
            keep, theirs = halves(total, 1, ways[bit])
            keep, theirs = keep.reshape((-1,) + panel), theirs.reshape((-1,) + panel)
            if left:
                came = swapped(theirs.astype(bf16), "col", n_col, 1 << bit)
        last.append((keep[0], theirs[0]))

    other_rows = pl.pallas_call(
        functools.partial(partner_kernel, n_row),
        out_shape=shape((2,) + panel, bf16),
        in_specs=[SMEM, SMEM] + [VMEM] * 4 + [ANY] * 2,
        out_specs=VMEM,
        compiler_params=big,
        name="partner",
        cost_estimate=pl.CostEstimate(flops=8 * width**3, bytes_accessed=4 * width**2, transcendentals=0),
    )(struct_first, struct_second, *others, inv_first, inv_second, *after)
    sums = pl.pallas_call(
        sum_kernel,
        out_shape=shape((2, n_col, 3, slab, width // 2), f32),
        in_specs=[VMEM] * 7 + [ANY],
        out_specs=VMEM,
        compiler_params=big,
        name="sums",
    )(rows, other_rows, last[0][0], last[0][1], last[1][0], last[1][1], linked, consts)
    done = [swapped(theirs.astype(bf16), "col", n_col, n_col // 2) for _, theirs in last]

    keep, send = halves(sums, 0, cores)
    sums = keep + swapped(send, "row", n_row, 1)
    for bit in range(n_bits):
        if bit == 1:
            sums, done[0] = lax.optimization_barrier((sums, done[0]))
            for row_bit in range(1, n_row.bit_length() - 1):
                sums = sums.astype(bf16)
                sums = sums.astype(f32) + swapped(sums, "row", n_row, 1 << row_bit).astype(f32)
            sums, done[1] = lax.optimization_barrier((sums, done[1]))
        keep, send = halves(sums.reshape(-1, 2, 3, slab, width // 2), 1, ways[bit])
        sums = keep + swapped(send.astype(bf16), "col", n_col, 1 << bit).astype(f32)
    mine = sums.reshape(3, slab, width // 2)
    beside = swapped(mine, "row", n_row, 1)

    column_first, column_second = pl.pallas_call(
        functools.partial(column_kernel, n_row),
        out_shape=[shape(panel, f32)] * 2,
        in_specs=[SMEM, SMEM] + [VMEM] * 5,
        out_specs=[VMEM] * 2,
        compiler_params=big,
        name="columns",
    )(struct_first, struct_second, last[0][0], done[0], last[1][0], done[1], linked)

    pair = jnp.stack([mine, beside])
    total = jnp.concatenate([lax.dynamic_index_in_dim(pair, way, 0, keepdims=False) for way in cores], axis=-1)
    diag_first, link_block, diag_second = consts + total
    out = (row_blocks, 1, slab, width)
    return column_first.reshape(out), column_second.reshape(out), diag_first, link_block, diag_second


def solution(mesh):
    placed = (
        P(None, "row", None, "col", None, None),
        P(None, "row", "col", None),
        P(None, "row", "col", None),
        P(),
        P(),
        P(),
        P(),
        P(),
    )
    return jax.shard_map(
        body,
        mesh=mesh,
        in_specs=placed,
        out_specs=(
            P(None, "row", "col", None),
            P(None, "row", "col", None),
            P("col", None),
            P("col", None),
            P("col", None),
        ),
        check_vma=False,
    )
```

```python
import functools

import jax
import jax.numpy as jnp
from jax import lax
from jax.experimental import pallas as pl
from jax.experimental.pallas import tpu as pltpu
from jax.sharding import PartitionSpec as P

precise = lax.Precision.HIGHEST
SMEM = pl.BlockSpec(memory_space=pltpu.SMEM)
VMEM = pl.BlockSpec(memory_space=pltpu.VMEM)
HBM = pl.BlockSpec(memory_space=pltpu.HBM)
ANY = pl.BlockSpec(memory_space=pl.ANY)


def exact_dot(left, right, left_dim=1):
    dims = (((left_dim,), (0,)), ((), ()))
    return lax.dot_general(left, right, dims, precision=precise, preferred_element_type=jnp.float32)


def split_dot(left, right, left_dim=1):
    def halves(value):
        if value.dtype == jnp.bfloat16:
            return [value]
        high = value.astype(jnp.bfloat16)
        return [high, (value - high.astype(jnp.float32)).astype(jnp.bfloat16)]

    dims = (((left_dim,), (0,)), ((), ()))
    total = None
    for i, a in enumerate(halves(left)):
        for j, b in enumerate(halves(right)):
            if i + j < 2:
                term = lax.dot_general(a, b, dims, preferred_element_type=jnp.float32)
                total = term if total is None else total + term
    return total


def listed(struct_ref, blocks, n_row):
    ids = lax.broadcasted_iota(jnp.int32, (blocks, 1, 1), 0) * n_row + lax.axis_index("row")

    def look(place, found):
        return jnp.where(ids == struct_ref[place], 1, found)

    found = lax.fori_loop(0, struct_ref.shape[0], look, jnp.zeros((blocks, 1, 1), jnp.int32))
    return found == 1


def slice_of(row, turn, n_row):
    return turn * n_row + row


def place_of(piece, n_row):
    return piece % n_row, piece // n_row


def product_kernel(n_row, n_col, first_bits, struct1, struct2, inv1, inv2, stored, pieces, *rest):
    cycle = n_col // n_row
    keeps, sends = rest[:2], rest[2:4]
    loose, factor = rest[4:]
    row_blocks = stored.shape[0]
    _, col_blocks, _, slab, width = loose.shape
    here_row, here_col = lax.axis_index("row"), lax.axis_index("col")

    group = here_col // n_row
    for m in range(n_row):
        row = here_row ^ m
        for s in range(cycle):
            slot = slice_of(row, lax.rem(s - group + cycle, cycle), n_row)
            for p in range(2):
                for b in range(col_blocks):
                    loose[p, b, slot] = pieces[m, s, p, b].astype(loose.dtype)
    for p, (struct, inverse) in enumerate(((struct1, inv1), (struct2, inv2))):

        def look(place, found):
            return tuple(f | (struct[place] == b * n_col + here_col).astype(jnp.int32) for b, f in enumerate(found))

        found = lax.fori_loop(0, struct.shape[0], look, (jnp.int32(0),) * col_blocks)
        blocks = loose[p].reshape(col_blocks * width, width).astype(jnp.bfloat16)
        product = split_dot(blocks, inverse[...])
        for b in range(col_blocks):
            place = slice(b * width, (b + 1) * width)
            factor[place, p * width : (p + 1) * width] = jnp.where(found[b] == 1, product[place], 0.0).astype(jnp.bfloat16)

    step = 2 if row_blocks % 2 == 0 else 1
    for a in range(0, row_blocks, step):
        wide = [jnp.concatenate([stored[a + i, b] for b in range(col_blocks)], axis=1) for i in range(step)]
        totals = jnp.dot(jnp.concatenate(wide, axis=0), factor[...], preferred_element_type=jnp.float32)
        for i in range(step):
            total = totals[i * width : (i + 1) * width]
            group, place = divmod(a + i, row_blocks // 2)
            bit = first_bits[group]
            upper = ((here_col >> bit) & 1) == 1
            for p in range(2):
                for j in range(n_col // 2):
                    low = ((j >> bit) << (bit + 1)) | (j & ((1 << bit) - 1))
                    high = low | (1 << bit)
                    x = total[low * slab : (low + 1) * slab, p * width : (p + 1) * width]
                    y = total[high * slab : (high + 1) * slab, p * width : (p + 1) * width]
                    keeps[group][j, p, place] = jnp.where(upper, y, x)
                    sends[group][j, p, place] = jnp.where(upper, x, y).astype(jnp.bfloat16)


def prepare_kernel(n_row, struct1, struct2, low, high, link, inv1, inv2, after, rows, linked, out, whole):
    slices, _, half, slab, width = low.shape
    for p, (struct, inverse) in enumerate(((struct1, inv1), (struct2, inv2))):
        keep = listed(struct, 2 * half, n_row)
        for group, part in enumerate((low, high)):
            flat = part[:, p].astype(jnp.float32).reshape(slices * half * slab, width).astype(jnp.bfloat16)
            product = split_dot(flat, inverse[...]).reshape(slices, half, slab, width)
            mine = keep[group * half : (group + 1) * half][None]
            rows[group, p] = jnp.where(mine, product, 0.0).astype(jnp.bfloat16)
    linked[...] = exact_dot(link[...].astype(jnp.float32), inv2[...])
    link = linked[...]
    gram1 = exact_dot(inv1[...], inv1[...], 0)
    across = exact_dot(gram1, link)
    whole[0] = gram1
    whole[1] = -across
    whole[2] = exact_dot(inv2[...], inv2[...], 0) + exact_dot(link, across, 0)
    place = pl.ds(pl.multiple_of(lax.axis_index("col") * slab, slab), slab)
    out[...] = whole[:, place, :]


def sum_kernel(first_bits, masks, rows, total_low, total_high, linked, after, out):
    _, _, half, slab, width = total_low.shape
    here_col = lax.axis_index("col")

    def gathered(p):
        parts = []
        for bit, own, total in zip(first_bits, masks, (total_low, total_high)):
            for mask in own:
                piece = here_col ^ mask
                place = ((piece >> (bit + 1)) << bit) | (piece & ((1 << bit) - 1))
                parts.append(total[place, p].reshape(half * slab, width))
        return jnp.concatenate(parts, axis=0)

    def factor(p):
        parts = [rows[g, p].astype(jnp.float32).reshape(-1, width) for g in range(2)]
        return jnp.concatenate(parts, axis=0).astype(jnp.bfloat16)

    link = linked[...]
    sum1 = gathered(0)
    u2 = factor(1)
    first = split_dot(factor(0), sum1, 0)
    cross = split_dot(u2, sum1, 0)
    top = cross.T - split_dot(first, link)
    second = split_dot(u2, gathered(1), 0) - split_dot(cross, link) - split_dot(link, top, 0)
    for i, part in enumerate((first, top, second)):
        out[i] = part.reshape(width // slab, slab, width)


def column_kernel(n_row, struct1, struct2, kept_low, came_low, kept_high, came_high, linked, column1, column2):
    blocks, slab, width = column1.shape
    sums = []
    for p in range(2):
        parts = [k[p] + c[p].astype(jnp.float32) for k, c in ((kept_low, came_low), (kept_high, came_high))]
        sums.append(jnp.concatenate(parts, axis=0))
    col1 = jnp.where(listed(struct1, blocks, n_row), -sums[0], 0.0)
    column1[...] = col1
    carried = split_dot(col1.reshape(blocks * slab, width), linked[...]).reshape(col1.shape)
    column2[...] = jnp.where(listed(struct2, blocks, n_row), -(sums[1] + carried), 0.0)


def swapped(value, axis, size, mask):
    return lax.ppermute(value, axis, [(i, i ^ mask) for i in range(size)])


def halves(value, axis, ways):
    kept, sent = (lax.dynamic_index_in_dim(value, way, axis, keepdims=False) for way in ways)
    return kept, sent


def body(stored_inverse, panel_first, panel_second, panel_link, inv_first, inv_second, struct_first, struct_second):
    n_row, n_col = lax.axis_size("row"), lax.axis_size("col")
    here_col = lax.axis_index("col")
    row_blocks, _, col_blocks, _, width, _ = stored_inverse.shape
    slab = width // n_col
    cycle = n_col // n_row
    n_bits = n_col.bit_length() - 1
    f32, bf16 = jnp.float32, jnp.bfloat16
    shape = jax.ShapeDtypeStruct
    big = pltpu.CompilerParams(vmem_limit_bytes=12 * 1024 * 1024)
    stored = stored_inverse.reshape(row_blocks, col_blocks, width, width)
    panel = (row_blocks, slab, width)

    panels = [panel_first.reshape(panel), panel_second.reshape(panel)]
    _, turn = place_of(here_col, n_row)
    picks = [((s - turn + cycle) % cycle).astype(jnp.uint32) for s in range(cycle)]
    ways = [(here_col >> bit) & 1 for bit in range(n_bits)]
    ways = [(way.astype(jnp.uint32), (1 - way).astype(jnp.uint32)) for way in ways]
    panels, picks, ways = lax.optimization_barrier((panels, picks, ways))

    raw = jnp.stack(panels)
    turns = raw.reshape(2, col_blocks, cycle, slab, width)
    got = []
    for s in range(cycle):
        moves = []
        for r in range(n_row):
            for c in range(n_col):
                row, t = place_of(c, n_row)
                moves.append((r * n_col + c, row * n_col + r + (s - t) % cycle * n_row))
        part = lax.dynamic_index_in_dim(turns, picks[s], 2, keepdims=False)
        got.append(lax.ppermute(part, ("row", "col"), moves))
    base, base_masks = raw[None], [0]
    for bit in range(n_bits - 1, 1, -1):
        base = jnp.concatenate([base, swapped(base, "col", n_col, 1 << bit)])
        base_masks += [m ^ (1 << bit) for m in base_masks]
    got, base = lax.optimization_barrier((got, base))
    half = row_blocks // 2
    low, high = base[:, :, :half], base[:, :, half:]
    low = jnp.concatenate([low, swapped(low, "col", n_col, 2)])
    high = jnp.concatenate([high, swapped(high, "col", n_col, 1)])
    masks = (base_masks + [m ^ 2 for m in base_masks], base_masks + [m ^ 1 for m in base_masks])

    pieces = jnp.stack(got)[None]
    order = [0]
    bit = n_row // 2
    while bit:
        if bit == 1:
            pieces, low, high = lax.optimization_barrier((pieces, low, high))
        pieces = jnp.concatenate([pieces, swapped(pieces, "row", n_row, bit)])
        order += [o ^ bit for o in order]
        bit //= 2
    pieces = jnp.stack([pieces[order.index(m)] for m in range(n_row)])

    orders = (list(range(n_bits)), [1, 0] + list(range(2, n_bits)))
    block = (2, half, slab, width)
    kept = (n_col // 2,) + block
    split = pl.pallas_call(
        functools.partial(product_kernel, n_row, n_col, (orders[0][0], orders[1][0])),
        out_shape=[shape(kept, f32)] * 2 + [shape(kept, bf16)] * 2,
        in_specs=[SMEM, SMEM] + [VMEM] * 4,
        out_specs=[VMEM] * 4,
        scratch_shapes=[
            pltpu.VMEM((2, col_blocks, n_col, slab, width), bf16 if slab % 16 == 0 else f32),
            pltpu.VMEM((col_blocks * width, 2 * width), bf16),
        ],
        compiler_params=big,
        name="products",
    )(struct_first, struct_second, inv_first, inv_second, stored, pieces)

    rows, linked, consts = pl.pallas_call(
        functools.partial(prepare_kernel, n_row),
        out_shape=[shape((2, 2, n_col // 2) + block[1:], bf16), shape((width, width), f32), shape((3, slab, width), f32)],
        in_specs=[SMEM, SMEM] + [VMEM] * 5 + [ANY],
        out_specs=[VMEM] * 3,
        scratch_shapes=[pltpu.VMEM((3, width, width), f32)],
        compiler_params=big,
        name="prepare",
        cost_estimate=pl.CostEstimate(flops=6 * 10 * width**3, bytes_accessed=8 * width**2, transcendentals=0),
    )(struct_first, struct_second, low, high, panel_link, inv_first, inv_second, split[0])

    def step(bit, keep, send):
        return keep, swapped(send.astype(bf16), "col", n_col, 1 << bit)

    state = [step(orders[g][0], split[g], split[2 + g]) for g in range(2)]
    left = [sorted(set(range(n_bits)) - {order[0]}) for order in orders]
    totals = []
    for i in range(1, n_bits):
        for g in range(2):
            keep, came = state[g]
            bit = orders[g][i]
            low_size = 1 << left[g].index(bit)
            left[g].remove(bit)
            total = keep + came.astype(f32)
            if i == 1:
                totals.append(total)
            keep, send = halves(total.reshape((-1, 2, low_size) + block), 1, ways[bit])
            state[g] = step(bit, keep.reshape((-1,) + block), send.reshape((-1,) + block))

    sums = pl.pallas_call(
        functools.partial(sum_kernel, [order[0] for order in orders], masks),
        out_shape=shape((3, n_col, slab, width), f32),
        in_specs=[VMEM] * 4 + [ANY],
        out_specs=VMEM,
        compiler_params=big,
        name="sums",
    )(rows, *totals, linked, consts)
    for bit in range(n_bits):
        keep, send = halves(sums.reshape(3, -1, 2, slab, width), 2, ways[bit])
        sums = keep + swapped(send.astype(bf16), "col", n_col, 1 << bit).astype(f32)

    column_first, column_second = pl.pallas_call(
        functools.partial(column_kernel, n_row),
        out_shape=[shape(panel, f32)] * 2,
        in_specs=[SMEM, SMEM] + [VMEM] * 5,
        out_specs=[VMEM] * 2,
        compiler_params=big,
        name="columns",
    )(struct_first, struct_second, state[0][0][0], state[0][1][0], state[1][0][0], state[1][1][0], linked)

    total = sums.reshape(3, slab, width)
    for bit in range(n_row.bit_length() - 1):
        total = total + swapped(total, "row", n_row, 1 << bit)
    diag_first, link_block, diag_second = consts + total
    out = (row_blocks, 1, slab, width)
    return column_first.reshape(out), column_second.reshape(out), diag_first, link_block, diag_second


def solution(mesh):
    placed = (
        P(None, "row", None, "col", None, None),
        P(None, "row", "col", None),
        P(None, "row", "col", None),
        P(),
        P(),
        P(),
        P(),
        P(),
    )
    return jax.shard_map(
        body,
        mesh=mesh,
        in_specs=placed,
        out_specs=(
            P(None, "row", "col", None),
            P(None, "row", "col", None),
            P("col", None),
            P("col", None),
            P("col", None),
        ),
        check_vma=False,
    )
```

```python
import functools

import jax
import jax.numpy as jnp
from jax import lax
from jax.experimental import pallas as pl
from jax.experimental.pallas import tpu as pltpu
from jax.sharding import PartitionSpec as P

precise = lax.Precision.HIGHEST
SMEM = pl.BlockSpec(memory_space=pltpu.SMEM)
VMEM = pl.BlockSpec(memory_space=pltpu.VMEM)
HBM = pl.BlockSpec(memory_space=pltpu.HBM)
ANY = pl.BlockSpec(memory_space=pl.ANY)


def exact_dot(left, right, left_dim=1):
    dims = (((left_dim,), (0,)), ((), ()))
    return lax.dot_general(left, right, dims, precision=precise, preferred_element_type=jnp.float32)


def split_dot(left, right, left_dim=1):
    def halves(value):
        if value.dtype == jnp.bfloat16:
            return [value]
        high = value.astype(jnp.bfloat16)
        return [high, (value - high.astype(jnp.float32)).astype(jnp.bfloat16)]

    dims = (((left_dim,), (0,)), ((), ()))
    total = None
    for i, a in enumerate(halves(left)):
        for j, b in enumerate(halves(right)):
            if i + j < 2:
                term = lax.dot_general(a, b, dims, preferred_element_type=jnp.float32)
                total = term if total is None else total + term
    return total


def listed(struct_ref, blocks, n_row):
    ids = lax.broadcasted_iota(jnp.int32, (blocks, 1, 1), 0) * n_row + lax.axis_index("row")

    def look(place, found):
        return jnp.where(ids == struct_ref[place], 1, found)

    found = lax.fori_loop(0, struct_ref.shape[0], look, jnp.zeros((blocks, 1, 1), jnp.int32))
    return found == 1


def slice_of(row, turn, n_row):
    return turn * n_row + row


def place_of(piece, n_row):
    return piece % n_row, piece // n_row


def product_kernel(n_row, n_col, first_bits, struct1, struct2, inv1, inv2, stored, pieces, *rest):
    cycle = n_col // n_row
    keeps, sends = rest[:2], rest[2:4]
    loose, factor = rest[4:]
    row_blocks = stored.shape[0]
    _, col_blocks, _, slab, width = loose.shape
    here_row, here_col = lax.axis_index("row"), lax.axis_index("col")

    group = here_col // n_row
    for m in range(n_row):
        row = here_row ^ m
        for s in range(cycle):
            slot = slice_of(row, lax.rem(s - group + cycle, cycle), n_row)
            for p in range(2):
                for b in range(col_blocks):
                    loose[p, b, slot] = pieces[m, s, p, b].astype(loose.dtype)
    for p, (struct, inverse) in enumerate(((struct1, inv1), (struct2, inv2))):

        def look(place, found):
            return tuple(f | (struct[place] == b * n_col + here_col).astype(jnp.int32) for b, f in enumerate(found))

        found = lax.fori_loop(0, struct.shape[0], look, (jnp.int32(0),) * col_blocks)
        blocks = loose[p].reshape(col_blocks * width, width).astype(jnp.bfloat16)
        product = split_dot(blocks, inverse[...])
        for b in range(col_blocks):
            place = slice(b * width, (b + 1) * width)
            factor[place, p * width : (p + 1) * width] = jnp.where(found[b] == 1, product[place], 0.0).astype(jnp.bfloat16)

    step = 2 if row_blocks % 2 == 0 else 1
    for a in range(0, row_blocks, step):
        wide = [jnp.concatenate([stored[a + i, b] for b in range(col_blocks)], axis=1) for i in range(step)]
        totals = jnp.dot(jnp.concatenate(wide, axis=0), factor[...], preferred_element_type=jnp.float32)
        for i in range(step):
            total = totals[i * width : (i + 1) * width]
            for p in range(2):
                bit = first_bits[p]
                upper = ((here_col >> bit) & 1) == 1
                for j in range(n_col // 2):
                    low = ((j >> bit) << (bit + 1)) | (j & ((1 << bit) - 1))
                    high = low | (1 << bit)
                    x = total[low * slab : (low + 1) * slab, p * width : (p + 1) * width]
                    y = total[high * slab : (high + 1) * slab, p * width : (p + 1) * width]
                    keeps[p][j, a + i] = jnp.where(upper, y, x)
                    sends[p][j, a + i] = jnp.where(upper, x, y).astype(jnp.bfloat16)


def factor_rows(panel, inverse, keep):
    blocks, slab, width = panel.shape
    flat = panel[...].astype(jnp.float32).reshape(blocks * slab, width).astype(jnp.bfloat16)
    product = split_dot(flat, inverse[...]).reshape(blocks, slab, width)
    return jnp.where(keep, product, 0.0)


def prepare_kernel(n_row, struct1, struct2, mine1, mine2, link, inv1, inv2, after, rows, linked, out, whole):
    blocks, slab, width = mine1.shape
    for p, (struct, mine, inverse) in enumerate(((struct1, mine1, inv1), (struct2, mine2, inv2))):
        rows[p] = factor_rows(mine, inverse, listed(struct, blocks, n_row)).astype(jnp.bfloat16)
    linked[...] = exact_dot(link[...].astype(jnp.float32), inv2[...])
    link = linked[...]
    gram1 = exact_dot(inv1[...], inv1[...], 0)
    across = exact_dot(gram1, link)
    whole[0] = gram1
    whole[1] = -across
    whole[2] = exact_dot(inv2[...], inv2[...], 0) + exact_dot(link, across, 0)
    place = pl.ds(pl.multiple_of(lax.axis_index("col") * slab, slab), slab)
    out[...] = whole[:, place, :]


def partner_kernel(n_row, struct1, struct2, other1, other2, inv1, inv2, after1, after2, rows):
    for p, (struct, other, inverse) in enumerate(((struct1, other1, inv1), (struct2, other2, inv2))):
        keep = listed(struct, other.shape[0], n_row)
        rows[p] = factor_rows(other, inverse, keep).astype(jnp.bfloat16)


def sum_kernel(rows, others, mine1, theirs1, mine2, theirs2, linked, after, out):
    blocks, slab, width = mine1.shape
    flat = (blocks * slab, width)

    def both(a, b):
        return jnp.concatenate([a.reshape(flat), b.reshape(flat)], axis=0)

    def factor(p):
        return both(rows[p].astype(jnp.float32), others[p].astype(jnp.float32)).astype(jnp.bfloat16)

    link = linked[...]
    sum1 = both(mine1[...], theirs1[...])
    u2 = factor(1)
    first = split_dot(factor(0), sum1, 0)
    cross = split_dot(u2, sum1, 0)
    top = cross.T - split_dot(first, link)
    second = split_dot(u2, both(mine2[...], theirs2[...]), 0) - split_dot(cross, link) - split_dot(link, top, 0)
    for i, part in enumerate((first, top, second)):
        out[:, i] = part.reshape(width // slab, slab, width)


def column_kernel(n_row, struct1, struct2, kept1, came1, kept2, came2, linked, column1, column2):
    blocks, slab, width = column1.shape
    sum1 = kept1[...] + came1[...].astype(jnp.float32)
    sum2 = kept2[...] + came2[...].astype(jnp.float32)
    col1 = jnp.where(listed(struct1, blocks, n_row), -sum1, 0.0)
    column1[...] = col1
    carried = split_dot(col1.reshape(blocks * slab, width), linked[...]).reshape(sum2.shape)
    column2[...] = jnp.where(listed(struct2, blocks, n_row), -(sum2 + carried), 0.0)


def swapped(value, axis, size, mask):
    return lax.ppermute(value, axis, [(i, i ^ mask) for i in range(size)])


def halves(value, axis, ways):
    kept, sent = (lax.dynamic_index_in_dim(value, way, axis, keepdims=False) for way in ways)
    return kept, sent


def body(stored_inverse, panel_first, panel_second, panel_link, inv_first, inv_second, struct_first, struct_second):
    n_row, n_col = lax.axis_size("row"), lax.axis_size("col")
    here_col = lax.axis_index("col")
    row_blocks, _, col_blocks, _, width, _ = stored_inverse.shape
    slab = width // n_col
    cycle = n_col // n_row
    n_bits = n_col.bit_length() - 1
    f32, bf16 = jnp.float32, jnp.bfloat16
    shape = jax.ShapeDtypeStruct
    big = pltpu.CompilerParams(vmem_limit_bytes=12 * 1024 * 1024)
    stored = stored_inverse.reshape(row_blocks, col_blocks, width, width)
    panel = (row_blocks, slab, width)

    panels = [panel_first.reshape(panel), panel_second.reshape(panel)]
    _, turn = place_of(here_col, n_row)
    picks = [((s - turn + cycle) % cycle).astype(jnp.uint32) for s in range(cycle)]
    ways = [(here_col >> bit) & 1 for bit in range(n_bits)]
    ways = [(way.astype(jnp.uint32), (1 - way).astype(jnp.uint32)) for way in ways]
    panels, picks, ways = lax.optimization_barrier((panels, picks, ways))

    turns = jnp.stack(panels).reshape(2, col_blocks, cycle, slab, width)
    got = []
    for s in range(cycle):
        moves = []
        for r in range(n_row):
            for c in range(n_col):
                row, t = place_of(c, n_row)
                moves.append((r * n_col + c, row * n_col + r + (s - t) % cycle * n_row))
        part = lax.dynamic_index_in_dim(turns, picks[s], 2, keepdims=False)
        got.append(lax.ppermute(part, ("row", "col"), moves))
    pieces = jnp.stack(got)[None]

    order = [0]
    bit = n_row // 2
    while bit:
        pieces = jnp.concatenate([pieces, swapped(pieces, "row", n_row, bit)])
        order += [o ^ bit for o in order]
        bit //= 2
    pieces = jnp.stack([pieces[order.index(m)] for m in range(n_row)])

    orders = (list(range(n_bits)), [1, 0] + list(range(2, n_bits)))
    half = (n_col // 2,) + panel
    split = pl.pallas_call(
        functools.partial(product_kernel, n_row, n_col, (orders[0][0], orders[1][0])),
        out_shape=[shape(half, f32)] * 2 + [shape(half, bf16)] * 2,
        in_specs=[SMEM, SMEM] + [VMEM] * 4,
        out_specs=[VMEM] * 4,
        scratch_shapes=[
            pltpu.VMEM((2, col_blocks, n_col, slab, width), bf16 if slab % 16 == 0 else f32),
            pltpu.VMEM((col_blocks * width, 2 * width), bf16),
        ],
        compiler_params=big,
        name="products",
    )(struct_first, struct_second, inv_first, inv_second, stored, pieces)

    rows, linked, consts = pl.pallas_call(
        functools.partial(prepare_kernel, n_row),
        out_shape=[shape((2,) + panel, bf16), shape((width, width), f32), shape((3, slab, width), f32)],
        in_specs=[SMEM, SMEM] + [VMEM] * 5 + [ANY],
        out_specs=[VMEM] * 3,
        scratch_shapes=[pltpu.VMEM((3, width, width), f32)],
        compiler_params=big,
        name="prepare",
        cost_estimate=pl.CostEstimate(flops=6 * 10 * width**3, bytes_accessed=8 * width**2, transcendentals=0),
    )(struct_first, struct_second, *panels, panel_link, inv_first, inv_second, split[0])

    panels, consts = lax.optimization_barrier((panels, consts))
    others = [swapped(p, "col", n_col, n_col // 2) for p in panels]

    last, after = [], []
    for p in range(2):
        keep, came = split[p], swapped(split[2 + p], "col", n_col, 1 << orders[p][0])
        after.append(came)
        left = sorted(set(range(n_bits)) - {orders[p][0]})
        for bit in orders[p][1:]:
            low = 1 << left.index(bit)
            left.remove(bit)
            total = (keep + came.astype(f32)).reshape((-1, 2, low) + panel)
            keep, theirs = halves(total, 1, ways[bit])
            keep, theirs = keep.reshape((-1,) + panel), theirs.reshape((-1,) + panel)
            if left:
                came = swapped(theirs.astype(bf16), "col", n_col, 1 << bit)
        last.append((keep[0], theirs[0]))

    other_rows = pl.pallas_call(
        functools.partial(partner_kernel, n_row),
        out_shape=shape((2,) + panel, bf16),
        in_specs=[SMEM, SMEM] + [VMEM] * 4 + [ANY] * 2,
        out_specs=VMEM,
        compiler_params=big,
        name="partner",
        cost_estimate=pl.CostEstimate(flops=8 * width**3, bytes_accessed=4 * width**2, transcendentals=0),
    )(struct_first, struct_second, *others, inv_first, inv_second, *after)
    sums = pl.pallas_call(
        sum_kernel,
        out_shape=shape((n_col, 3, slab, width), f32),
        in_specs=[VMEM] * 7 + [ANY],
        out_specs=VMEM,
        compiler_params=big,
        name="sums",
    )(rows, other_rows, last[0][0], last[0][1], last[1][0], last[1][1], linked, consts)
    done = [swapped(theirs.astype(bf16), "col", n_col, n_col // 2) for _, theirs in last]

    for bit in range(n_bits):
        if bit == 1:
            sums, done[0] = lax.optimization_barrier((sums, done[0]))
            sums = sums + swapped(sums, "row", n_row, 1)
            for row_bit in range(1, n_row.bit_length() - 1):
                sums = sums.astype(bf16)
                sums = sums.astype(f32) + swapped(sums, "row", n_row, 1 << row_bit).astype(f32)
            sums, done[1] = lax.optimization_barrier((sums, done[1]))
        keep, send = halves(sums.reshape(-1, 2, 3, slab, width), 1, ways[bit])
        sums = keep + swapped(send.astype(bf16), "col", n_col, 1 << bit).astype(f32)

    column_first, column_second = pl.pallas_call(
        functools.partial(column_kernel, n_row),
        out_shape=[shape(panel, f32)] * 2,
        in_specs=[SMEM, SMEM] + [VMEM] * 5,
        out_specs=[VMEM] * 2,
        compiler_params=big,
        name="columns",
    )(struct_first, struct_second, last[0][0], done[0], last[1][0], done[1], linked)

    diag_first, link_block, diag_second = consts + sums.reshape(3, slab, width)
    out = (row_blocks, 1, slab, width)
    return column_first.reshape(out), column_second.reshape(out), diag_first, link_block, diag_second


def solution(mesh):
    placed = (
        P(None, "row", None, "col", None, None),
        P(None, "row", "col", None),
        P(None, "row", "col", None),
        P(),
        P(),
        P(),
        P(),
        P(),
    )
    return jax.shard_map(
        body,
        mesh=mesh,
        in_specs=placed,
        out_specs=(
            P(None, "row", "col", None),
            P(None, "row", "col", None),
            P("col", None),
            P("col", None),
            P("col", None),
        ),
        check_vma=False,
    )
```

```python
import functools

import jax
import jax.numpy as jnp
from jax import lax
from jax.experimental import pallas as pl
from jax.experimental.pallas import tpu as pltpu
from jax.sharding import PartitionSpec as P

precise = lax.Precision.HIGHEST
SMEM = pl.BlockSpec(memory_space=pltpu.SMEM)
VMEM = pl.BlockSpec(memory_space=pltpu.VMEM)
HBM = pl.BlockSpec(memory_space=pltpu.HBM)
ANY = pl.BlockSpec(memory_space=pl.ANY)


def exact_dot(left, right, left_dim=1):
    dims = (((left_dim,), (0,)), ((), ()))
    return lax.dot_general(left, right, dims, precision=precise, preferred_element_type=jnp.float32)


def split_dot(left, right, left_dim=1):
    def halves(value):
        if value.dtype == jnp.bfloat16:
            return [value]
        high = value.astype(jnp.bfloat16)
        return [high, (value - high.astype(jnp.float32)).astype(jnp.bfloat16)]

    dims = (((left_dim,), (0,)), ((), ()))
    total = None
    for i, a in enumerate(halves(left)):
        for j, b in enumerate(halves(right)):
            if i + j < 2:
                term = lax.dot_general(a, b, dims, preferred_element_type=jnp.float32)
                total = term if total is None else total + term
    return total


def listed(struct_ref, blocks, n_row):
    ids = lax.broadcasted_iota(jnp.int32, (blocks, 1, 1), 0) * n_row + lax.axis_index("row")

    def look(place, found):
        return jnp.where(ids == struct_ref[place], 1, found)

    found = lax.fori_loop(0, struct_ref.shape[0], look, jnp.zeros((blocks, 1, 1), jnp.int32))
    return found == 1


def slice_of(row, turn, n_row):
    return turn * n_row + row


def place_of(piece, n_row):
    return piece % n_row, piece // n_row


def product_kernel(n_row, n_col, first_bits, struct1, struct2, inv1, inv2, stored, pieces, base, *rest):
    cycle = n_col // n_row
    keeps, sends = rest[:2], rest[2:4]
    loose, factor = rest[4:]
    row_blocks = stored.shape[0]
    _, col_blocks, _, slab, width = loose.shape
    here_row, here_col = lax.axis_index("row"), lax.axis_index("col")

    group = here_col // n_row
    for m in range(n_row):
        row = here_row ^ m
        for s in range(cycle):
            slot = slice_of(row, lax.rem(s - group + cycle, cycle), n_row)
            for p in range(2):
                for b in range(col_blocks):
                    loose[p, b, slot] = pieces[m, s, p, b].astype(loose.dtype)
    for p, (struct, inverse) in enumerate(((struct1, inv1), (struct2, inv2))):

        def look(place, found):
            return tuple(f | (struct[place] == b * n_col + here_col).astype(jnp.int32) for b, f in enumerate(found))

        found = lax.fori_loop(0, struct.shape[0], look, (jnp.int32(0),) * col_blocks)
        blocks = loose[p].reshape(col_blocks * width, width).astype(jnp.bfloat16)
        product = split_dot(blocks, inverse[...])
        for b in range(col_blocks):
            place = slice(b * width, (b + 1) * width)
            factor[place, p * width : (p + 1) * width] = jnp.where(found[b] == 1, product[place], 0.0).astype(jnp.bfloat16)

    half = row_blocks // 2
    for e in range(n_col // 4):
        for p in range(2):
            for i in range(half):
                sends[0][n_col // 2 + e, p, i] = base[e, p, half + i]
                sends[1][n_col // 2 + e, p, i] = base[e, p, i]

    step = 2 if row_blocks % 2 == 0 else 1
    for a in range(0, row_blocks, step):
        wide = [jnp.concatenate([stored[a + i, b] for b in range(col_blocks)], axis=1) for i in range(step)]
        totals = jnp.dot(jnp.concatenate(wide, axis=0), factor[...], preferred_element_type=jnp.float32)
        for i in range(step):
            total = totals[i * width : (i + 1) * width]
            group, place = divmod(a + i, half)
            bit = first_bits[group]
            upper = ((here_col >> bit) & 1) == 1
            for p in range(2):
                for j in range(n_col // 2):
                    low = ((j >> bit) << (bit + 1)) | (j & ((1 << bit) - 1))
                    high = low | (1 << bit)
                    x = total[low * slab : (low + 1) * slab, p * width : (p + 1) * width]
                    y = total[high * slab : (high + 1) * slab, p * width : (p + 1) * width]
                    keeps[group][j, p, place] = jnp.where(upper, y, x)
                    sends[group][j, p, place] = jnp.where(upper, x, y).astype(jnp.bfloat16)


def prepare_kernel(link, inv1, inv2, after, linked, out, whole):
    slab = out.shape[1]
    linked[...] = exact_dot(link[...].astype(jnp.float32), inv2[...])
    link = linked[...]
    gram1 = exact_dot(inv1[...], inv1[...], 0)
    across = exact_dot(gram1, link)
    whole[0] = gram1
    whole[1] = -across
    whole[2] = exact_dot(inv2[...], inv2[...], 0) + exact_dot(link, across, 0)
    place = pl.ds(pl.multiple_of(lax.axis_index("col") * slab, slab), slab)
    out[...] = whole[:, place, :]


def sum_kernel(n_row, first_bits, masks, struct1, struct2, inv1, inv2, base, kept_low, came_low, kept_high, came_high, linked, after, out):
    here_col = lax.axis_index("col")
    places, _, half, slab, width = kept_low.shape
    count = base.shape[0]
    groups = ((kept_low, came_low, came_high), (kept_high, came_high, came_low))

    def gathered(p):
        parts = []
        for bit, own, (kept, came, _) in zip(first_bits, masks, groups):
            for mask in own:
                piece = here_col ^ mask
                place = ((piece >> (bit + 1)) << bit) | (piece & ((1 << bit) - 1))
                parts.append((kept[place, p] + came[place, p].astype(jnp.float32)).reshape(half * slab, width))
        return jnp.concatenate(parts, axis=0)

    def factor(p, struct, inverse):
        keep = listed(struct, 2 * half, n_row)
        parts, kept_rows = [], []
        for g, (_, _, tail) in enumerate(groups):
            rows = slice(g * half, (g + 1) * half)
            parts += [base[:, p, rows].astype(jnp.float32), tail[places:, p].astype(jnp.float32)]
            mine = jnp.broadcast_to(keep[rows].astype(jnp.float32)[None], (2 * count, half, slab, 1))
            kept_rows.append(mine.reshape(2 * count * half * slab, 1))
        flat = jnp.concatenate([part.reshape(-1, width) for part in parts], axis=0).astype(jnp.bfloat16)
        product = split_dot(flat, inverse[...])
        return jnp.where(jnp.concatenate(kept_rows, axis=0) > 0.5, product, 0.0).astype(jnp.bfloat16)

    link = linked[...]
    sum1 = gathered(0)
    u2 = factor(1, struct2, inv2)
    first = split_dot(factor(0, struct1, inv1), sum1, 0)
    cross = split_dot(u2, sum1, 0)
    top = cross.T - split_dot(first, link)
    second = split_dot(u2, gathered(1), 0) - split_dot(cross, link) - split_dot(link, top, 0)
    across = width // 2
    for i, part in enumerate((first, top, second)):
        part = part.reshape(width // slab, slab, width)
        for h in range(2):
            out[h, :, i] = part[:, :, h * across : (h + 1) * across]


def column_kernel(n_row, struct1, struct2, kept_low, came_low, kept_high, came_high, linked, column1, column2):
    blocks, slab, width = column1.shape
    sums = []
    for p in range(2):
        parts = [k[p] + c[p].astype(jnp.float32) for k, c in ((kept_low, came_low), (kept_high, came_high))]
        sums.append(jnp.concatenate(parts, axis=0))
    col1 = jnp.where(listed(struct1, blocks, n_row), -sums[0], 0.0)
    column1[...] = col1
    carried = split_dot(col1.reshape(blocks * slab, width), linked[...]).reshape(col1.shape)
    column2[...] = jnp.where(listed(struct2, blocks, n_row), -(sums[1] + carried), 0.0)


def swapped(value, axis, size, mask):
    return lax.ppermute(value, axis, [(i, i ^ mask) for i in range(size)])


def halves(value, axis, ways):
    kept, sent = (lax.dynamic_index_in_dim(value, way, axis, keepdims=False) for way in ways)
    return kept, sent


def body(stored_inverse, panel_first, panel_second, panel_link, inv_first, inv_second, struct_first, struct_second):
    n_row, n_col = lax.axis_size("row"), lax.axis_size("col")
    here_col = lax.axis_index("col")
    row_blocks, _, col_blocks, _, width, _ = stored_inverse.shape
    slab = width // n_col
    cycle = n_col // n_row
    n_bits = n_col.bit_length() - 1
    f32, bf16 = jnp.float32, jnp.bfloat16
    shape = jax.ShapeDtypeStruct
    big = pltpu.CompilerParams(vmem_limit_bytes=12 * 1024 * 1024)
    stored = stored_inverse.reshape(row_blocks, col_blocks, width, width)
    panel = (row_blocks, slab, width)

    panels = [panel_first.reshape(panel), panel_second.reshape(panel)]
    _, turn = place_of(here_col, n_row)
    picks = [((s - turn + cycle) % cycle).astype(jnp.uint32) for s in range(cycle)]
    ways = [(here_col >> bit) & 1 for bit in range(n_bits)]
    ways = [(way.astype(jnp.uint32), (1 - way).astype(jnp.uint32)) for way in ways]
    core = lax.axis_index("row") & 1
    cores = (core.astype(jnp.uint32), (1 - core).astype(jnp.uint32))
    panels, picks, ways, cores = lax.optimization_barrier((panels, picks, ways, cores))

    raw = lax.optimization_barrier(jnp.stack(panels))
    turns = raw.reshape(2, col_blocks, cycle, slab, width)
    got = []
    for s in range(cycle):
        moves = []
        for r in range(n_row):
            for c in range(n_col):
                row, t = place_of(c, n_row)
                moves.append((r * n_col + c, row * n_col + r + (s - t) % cycle * n_row))
        part = lax.dynamic_index_in_dim(turns, picks[s], 2, keepdims=False)
        got.append(lax.ppermute(part, ("row", "col"), moves))
    base, base_masks = raw[None], [0]
    for bit in range(n_bits - 1, 1, -1):
        base = jnp.concatenate([base, swapped(base, "col", n_col, 1 << bit)])
        base_masks += [m ^ (1 << bit) for m in base_masks]
    masks = (base_masks + [m ^ 2 for m in base_masks], base_masks + [m ^ 1 for m in base_masks])

    pieces = {0: got}
    bit = n_row // 2
    while bit > 1:
        for m, parts in list(pieces.items()):
            pieces[m ^ bit] = [swapped(part, "row", n_row, bit) for part in parts]
        bit //= 2
    pieces = jnp.stack([jnp.stack(pieces[m]) for m in sorted(pieces)])
    pieces, base = lax.optimization_barrier((pieces, base))
    beside = swapped(pieces, "row", n_row, 1)
    pieces = jnp.stack([pieces, beside], axis=1).reshape((n_row,) + pieces.shape[1:])

    orders = ([0] + list(range(2, n_bits)) + [1], [1, 0] + list(range(2, n_bits)))
    half = row_blocks // 2
    block = (2, half, slab, width)
    kept = (n_col // 2,) + block
    split = pl.pallas_call(
        functools.partial(product_kernel, n_row, n_col, (orders[0][0], orders[1][0])),
        out_shape=[shape(kept, f32)] * 2 + [shape((3 * n_col // 4,) + block, bf16)] * 2,
        in_specs=[SMEM, SMEM] + [VMEM] * 5,
        out_specs=[VMEM] * 4,
        scratch_shapes=[
            pltpu.VMEM((2, col_blocks, n_col, slab, width), bf16 if slab % 16 == 0 else f32),
            pltpu.VMEM((col_blocks * width, 2 * width), bf16),
        ],
        compiler_params=big,
        name="products",
    )(struct_first, struct_second, inv_first, inv_second, stored, pieces, base)

    linked, consts = pl.pallas_call(
        prepare_kernel,
        out_shape=[shape((width, width), f32), shape((3, slab, width), f32)],
        in_specs=[VMEM] * 3 + [ANY],
        out_specs=[VMEM] * 2,
        scratch_shapes=[pltpu.VMEM((3, width, width), f32)],
        compiler_params=big,
        name="prepare",
        cost_estimate=pl.CostEstimate(flops=6 * 10 * width**3, bytes_accessed=8 * width**2, transcendentals=0),
    )(panel_link, inv_first, inv_second, split[0])

    places = n_col // 2
    messages = [swapped(split[2 + g], "col", n_col, 1 << orders[g][0]) for g in range(2)]
    state = [(split[g], messages[g][:places]) for g in range(2)]
    left = [sorted(set(range(n_bits)) - {order[0]}) for order in orders]
    def advance(i, state):
        kept, sent = [], []
        for g in range(2):
            keep, came = state[g]
            bit = orders[g][i]
            inner = 1 << left[g].index(bit)
            left[g].remove(bit)
            total = (keep + came.astype(f32)).reshape((-1, 2, inner) + block)
            keep, send = halves(total, 1, ways[bit])
            kept.append(keep.reshape((-1,) + block))
            sent.append(send.astype(bf16).reshape((-1,) + block))
        return [(kept[g], swapped(send, "col", n_col, 1 << orders[g][i])) for g, send in enumerate(sent)]

    state = advance(1, state)
    sums = pl.pallas_call(
        functools.partial(sum_kernel, n_row, [order[0] for order in orders], masks),
        out_shape=shape((2, n_col, 3, slab, width // 2), f32),
        in_specs=[SMEM, SMEM] + [VMEM] * 8 + [ANY],
        out_specs=VMEM,
        compiler_params=big,
        name="sums",
    )(struct_first, struct_second, inv_first, inv_second, base, split[0], messages[0], split[1], messages[1], linked, consts)
    keep, send = halves(sums, 0, cores)
    sums = keep + swapped(send, "row", n_row, 1)
    for bit in range(n_bits):
        if bit == 1:
            state, _ = lax.optimization_barrier((state, sums))
            for i in range(2, n_bits):
                state = advance(i, state)
        keep, send = halves(sums.reshape(-1, 2, 3, slab, width // 2), 1, ways[bit])
        sums = keep + swapped(send.astype(bf16), "col", n_col, 1 << bit).astype(f32)
    mine = sums.reshape(3, slab, width // 2)
    for bit in range(1, n_row.bit_length() - 1):
        mine = mine + swapped(mine, "row", n_row, 1 << bit)

    mine, state = lax.optimization_barrier((mine, state))
    column_first, column_second = pl.pallas_call(
        functools.partial(column_kernel, n_row),
        out_shape=[shape(panel, f32)] * 2,
        in_specs=[SMEM, SMEM] + [VMEM] * 5,
        out_specs=[VMEM] * 2,
        compiler_params=big,
        name="columns",
    )(struct_first, struct_second, *[part[0] for pair in state for part in pair], linked)

    pair = jnp.stack([mine, swapped(mine, "row", n_row, 1)])
    total = jnp.concatenate([lax.dynamic_index_in_dim(pair, way, 0, keepdims=False) for way in cores], axis=-1)
    diag_first, link_block, diag_second = consts + total
    out = (row_blocks, 1, slab, width)
    return column_first.reshape(out), column_second.reshape(out), diag_first, link_block, diag_second


def solution(mesh):
    placed = (
        P(None, "row", None, "col", None, None),
        P(None, "row", "col", None),
        P(None, "row", "col", None),
        P(),
        P(),
        P(),
        P(),
        P(),
    )
    return jax.shard_map(
        body,
        mesh=mesh,
        in_specs=placed,
        out_specs=(
            P(None, "row", "col", None),
            P(None, "row", "col", None),
            P("col", None),
            P("col", None),
            P("col", None),
        ),
        check_vma=False,
    )
```

```python
import functools

import jax
import jax.numpy as jnp
from jax import lax
from jax.experimental import pallas as pl
from jax.experimental.pallas import tpu as pltpu
from jax.sharding import PartitionSpec as P

precise = lax.Precision.HIGHEST
SMEM = pl.BlockSpec(memory_space=pltpu.SMEM)
VMEM = pl.BlockSpec(memory_space=pltpu.VMEM)
HBM = pl.BlockSpec(memory_space=pltpu.HBM)
ANY = pl.BlockSpec(memory_space=pl.ANY)


def exact_dot(left, right, left_dim=1):
    dims = (((left_dim,), (0,)), ((), ()))
    return lax.dot_general(left, right, dims, precision=precise, preferred_element_type=jnp.float32)


def split_dot(left, right, left_dim=1):
    def halves(value):
        if value.dtype == jnp.bfloat16:
            return [value]
        high = value.astype(jnp.bfloat16)
        return [high, (value - high.astype(jnp.float32)).astype(jnp.bfloat16)]

    dims = (((left_dim,), (0,)), ((), ()))
    total = None
    for i, a in enumerate(halves(left)):
        for j, b in enumerate(halves(right)):
            if i + j < 2:
                term = lax.dot_general(a, b, dims, preferred_element_type=jnp.float32)
                total = term if total is None else total + term
    return total


def listed(struct_ref, blocks, n_row):
    ids = lax.broadcasted_iota(jnp.int32, (blocks, 1, 1), 0) * n_row + lax.axis_index("row")

    def look(place, found):
        return jnp.where(ids == struct_ref[place], 1, found)

    found = lax.fori_loop(0, struct_ref.shape[0], look, jnp.zeros((blocks, 1, 1), jnp.int32))
    return found == 1


def slice_of(row, turn, n_row):
    return turn * n_row + row


def place_of(piece, n_row):
    return piece % n_row, piece // n_row


def product_kernel(n_row, n_col, first_bits, struct1, struct2, inv1, inv2, stored, pieces, *rest):
    cycle = n_col // n_row
    keeps, sends = rest[:2], rest[2:4]
    loose, factor = rest[4:]
    row_blocks = stored.shape[0]
    _, col_blocks, _, slab, width = loose.shape
    here_row, here_col = lax.axis_index("row"), lax.axis_index("col")

    group = here_col // n_row
    for m in range(n_row):
        row = here_row ^ m
        for s in range(cycle):
            slot = slice_of(row, lax.rem(s - group + cycle, cycle), n_row)
            for p in range(2):
                for b in range(col_blocks):
                    loose[p, b, slot] = pieces[m, s, p, b].astype(loose.dtype)
    for p, (struct, inverse) in enumerate(((struct1, inv1), (struct2, inv2))):

        def look(place, found):
            return tuple(f | (struct[place] == b * n_col + here_col).astype(jnp.int32) for b, f in enumerate(found))

        found = lax.fori_loop(0, struct.shape[0], look, (jnp.int32(0),) * col_blocks)
        blocks = loose[p].reshape(col_blocks * width, width).astype(jnp.bfloat16)
        product = split_dot(blocks, inverse[...])
        for b in range(col_blocks):
            place = slice(b * width, (b + 1) * width)
            factor[place, p * width : (p + 1) * width] = jnp.where(found[b] == 1, product[place], 0.0).astype(jnp.bfloat16)

    half = row_blocks // 2
    step = 2 if row_blocks % 2 == 0 else 1
    for a in range(0, row_blocks, step):
        wide = [jnp.concatenate([stored[a + i, b] for b in range(col_blocks)], axis=1) for i in range(step)]
        totals = jnp.dot(jnp.concatenate(wide, axis=0), factor[...], preferred_element_type=jnp.float32)
        for i in range(step):
            total = totals[i * width : (i + 1) * width]
            group, place = divmod(a + i, half)
            bit = first_bits[group]
            upper = ((here_col >> bit) & 1) == 1
            for p in range(2):
                for j in range(n_col // 2):
                    low = ((j >> bit) << (bit + 1)) | (j & ((1 << bit) - 1))
                    high = low | (1 << bit)
                    x = total[low * slab : (low + 1) * slab, p * width : (p + 1) * width]
                    y = total[high * slab : (high + 1) * slab, p * width : (p + 1) * width]
                    keeps[group][j, p, place] = jnp.where(upper, y, x)
                    sends[group][j, p, place] = jnp.where(upper, x, y).astype(jnp.bfloat16)


def prepare_kernel(link, inv1, inv2, after, linked, out, whole):
    slab = out.shape[1]
    linked[...] = exact_dot(link[...].astype(jnp.float32), inv2[...])
    link = linked[...]
    gram1 = exact_dot(inv1[...], inv1[...], 0)
    across = exact_dot(gram1, link)
    whole[0] = gram1
    whole[1] = -across
    whole[2] = exact_dot(inv2[...], inv2[...], 0) + exact_dot(link, across, 0)
    place = pl.ds(pl.multiple_of(lax.axis_index("col") * slab, slab), slab)
    out[...] = whole[:, place, :]


def form_kernel(n_row, struct1, struct2, inv1, inv2, base, rows):
    slices, _, blocks, slab, width = base.shape
    for p, (struct, inverse) in enumerate(((struct1, inv1), (struct2, inv2))):
        keep = listed(struct, blocks, n_row)
        flat = base[:, p].astype(jnp.float32).reshape(slices * blocks * slab, width).astype(jnp.bfloat16)
        product = split_dot(flat, inverse[...]).reshape(slices, blocks, slab, width)
        rows[:, p] = jnp.where(keep[None], product, 0.0).astype(jnp.bfloat16)


def sum_kernel(last_bit, rows, total_low, total_high, linked, after, out):
    _, _, half, slab, width = total_low.shape
    mine = (lax.axis_index("col") >> last_bit) & 1

    def gathered(p):
        parts = [total[place, p].reshape(half * slab, width) for place in (mine, 1 - mine) for total in (total_low, total_high)]
        return jnp.concatenate(parts, axis=0)

    def factor(p):
        return rows[:, p].astype(jnp.float32).reshape(-1, width).astype(jnp.bfloat16)

    link = linked[...]
    sum1 = gathered(0)
    u2 = factor(1)
    first = split_dot(factor(0), sum1, 0)
    cross = split_dot(u2, sum1, 0)
    top = cross.T - split_dot(first, link)
    second = split_dot(u2, gathered(1), 0) - split_dot(cross, link) - split_dot(link, top, 0)
    across = width // 2
    for i, part in enumerate((first, top, second)):
        part = part.reshape(width // slab, slab, width)
        for h in range(2):
            out[h, :, i] = part[:, :, h * across : (h + 1) * across]


def column_kernel(n_row, struct1, struct2, kept_low, came_low, kept_high, came_high, linked, column1, column2):
    blocks, slab, width = column1.shape
    sums = []
    for p in range(2):
        parts = [k[p] + c[p].astype(jnp.float32) for k, c in ((kept_low, came_low), (kept_high, came_high))]
        sums.append(jnp.concatenate(parts, axis=0))
    col1 = jnp.where(listed(struct1, blocks, n_row), -sums[0], 0.0)
    column1[...] = col1
    carried = split_dot(col1.reshape(blocks * slab, width), linked[...]).reshape(col1.shape)
    column2[...] = jnp.where(listed(struct2, blocks, n_row), -(sums[1] + carried), 0.0)


def swapped(value, axis, size, mask):
    return lax.ppermute(value, axis, [(i, i ^ mask) for i in range(size)])


def halves(value, axis, ways):
    kept, sent = (lax.dynamic_index_in_dim(value, way, axis, keepdims=False) for way in ways)
    return kept, sent


def body(stored_inverse, panel_first, panel_second, panel_link, inv_first, inv_second, struct_first, struct_second):
    n_row, n_col = lax.axis_size("row"), lax.axis_size("col")
    here_col = lax.axis_index("col")
    row_blocks, _, col_blocks, _, width, _ = stored_inverse.shape
    slab = width // n_col
    cycle = n_col // n_row
    n_bits = n_col.bit_length() - 1
    f32, bf16 = jnp.float32, jnp.bfloat16
    shape = jax.ShapeDtypeStruct
    big = pltpu.CompilerParams(vmem_limit_bytes=12 * 1024 * 1024)
    stored = stored_inverse.reshape(row_blocks, col_blocks, width, width)
    panel = (row_blocks, slab, width)

    panels = [panel_first.reshape(panel), panel_second.reshape(panel)]
    _, turn = place_of(here_col, n_row)
    picks = [((s - turn + cycle) % cycle).astype(jnp.uint32) for s in range(cycle)]
    ways = [(here_col >> bit) & 1 for bit in range(n_bits)]
    ways = [(way.astype(jnp.uint32), (1 - way).astype(jnp.uint32)) for way in ways]
    core = lax.axis_index("row") & 1
    cores = (core.astype(jnp.uint32), (1 - core).astype(jnp.uint32))
    panels, picks, ways, cores = lax.optimization_barrier((panels, picks, ways, cores))

    raw = lax.optimization_barrier(jnp.stack(panels))
    turns = raw.reshape(2, col_blocks, cycle, slab, width)
    got = []
    for s in range(cycle):
        moves = []
        for r in range(n_row):
            for c in range(n_col):
                row, t = place_of(c, n_row)
                moves.append((r * n_col + c, row * n_col + r + (s - t) % cycle * n_row))
        part = lax.dynamic_index_in_dim(turns, picks[s], 2, keepdims=False)
        got.append(lax.ppermute(part, ("row", "col"), moves))
    base = jnp.stack([raw, swapped(raw, "col", n_col, n_col // 2)])

    pieces = {0: got}
    bit = n_row // 2
    while bit > 1:
        for m, parts in list(pieces.items()):
            pieces[m ^ bit] = [swapped(part, "row", n_row, bit) for part in parts]
        bit //= 2
    pieces = jnp.stack([jnp.stack(pieces[m]) for m in sorted(pieces)])
    pieces, base = lax.optimization_barrier((pieces, base))
    rows = pl.pallas_call(
        functools.partial(form_kernel, n_row),
        out_shape=shape(base.shape, bf16),
        in_specs=[SMEM, SMEM] + [VMEM] * 3,
        out_specs=VMEM,
        compiler_params=big,
        name="form",
        cost_estimate=pl.CostEstimate(flops=8 * width**3, bytes_accessed=4 * width**2, transcendentals=0),
    )(struct_first, struct_second, inv_first, inv_second, base)
    beside, rows = lax.optimization_barrier((swapped(pieces, "row", n_row, 1), rows))
    pieces = jnp.stack([pieces, beside], axis=1).reshape((n_row,) + pieces.shape[1:])

    orders = (list(range(n_bits)), [1, 0] + list(range(2, n_bits)))
    half = row_blocks // 2
    block = (2, half, slab, width)
    kept = (n_col // 2,) + block
    split = pl.pallas_call(
        functools.partial(product_kernel, n_row, n_col, (orders[0][0], orders[1][0])),
        out_shape=[shape(kept, f32)] * 2 + [shape(kept, bf16)] * 2,
        in_specs=[SMEM, SMEM] + [VMEM] * 4,
        out_specs=[VMEM] * 4,
        scratch_shapes=[
            pltpu.VMEM((2, col_blocks, n_col, slab, width), bf16 if slab % 16 == 0 else f32),
            pltpu.VMEM((col_blocks * width, 2 * width), bf16),
        ],
        compiler_params=big,
        name="products",
    )(struct_first, struct_second, inv_first, inv_second, stored, pieces)

    linked, consts = pl.pallas_call(
        prepare_kernel,
        out_shape=[shape((width, width), f32), shape((3, slab, width), f32)],
        in_specs=[VMEM] * 3 + [ANY],
        out_specs=[VMEM] * 2,
        scratch_shapes=[pltpu.VMEM((3, width, width), f32)],
        compiler_params=big,
        name="prepare",
        cost_estimate=pl.CostEstimate(flops=6 * 10 * width**3, bytes_accessed=8 * width**2, transcendentals=0),
    )(panel_link, inv_first, inv_second, split[0])

    state = [(split[g], swapped(split[2 + g], "col", n_col, 1 << orders[g][0])) for g in range(2)]
    left = [sorted(set(range(n_bits)) - {order[0]}) for order in orders]
    for i in range(1, n_bits):
        totals, last = [], []
        for g in range(2):
            keep, came = state[g]
            bit = orders[g][i]
            inner = 1 << left[g].index(bit)
            left[g].remove(bit)
            totals.append(keep + came.astype(f32))
            keep, send = halves(totals[g].reshape((-1, 2, inner) + block), 1, ways[bit])
            keep, send = keep.reshape((-1,) + block), send.astype(bf16).reshape((-1,) + block)
            last.append((keep, swapped(send, "col", n_col, 1 << bit)))
        state = last

    sums = pl.pallas_call(
        functools.partial(sum_kernel, n_bits - 1),
        out_shape=shape((2, n_col, 3, slab, width // 2), f32),
        in_specs=[VMEM] * 4 + [ANY],
        out_specs=VMEM,
        compiler_params=big,
        name="sums",
    )(rows, *totals, linked, consts)
    keep, send = halves(sums, 0, cores)
    sums = keep + swapped(send, "row", n_row, 1)
    for bit in range(n_bits):
        keep, send = halves(sums.reshape(-1, 2, 3, slab, width // 2), 1, ways[bit])
        sums = keep + swapped(send.astype(bf16), "col", n_col, 1 << bit).astype(f32)
    mine = sums.reshape(3, slab, width // 2)
    for bit in range(1, n_row.bit_length() - 1):
        mine = mine + swapped(mine, "row", n_row, 1 << bit)

    mine, state = lax.optimization_barrier((mine, state))
    column_first, column_second = pl.pallas_call(
        functools.partial(column_kernel, n_row),
        out_shape=[shape(panel, f32)] * 2,
        in_specs=[SMEM, SMEM] + [VMEM] * 5,
        out_specs=[VMEM] * 2,
        compiler_params=big,
        name="columns",
    )(struct_first, struct_second, *[part[0] for pair in state for part in pair], linked)

    pair = jnp.stack([mine, swapped(mine, "row", n_row, 1)])
    total = jnp.concatenate([lax.dynamic_index_in_dim(pair, way, 0, keepdims=False) for way in cores], axis=-1)
    diag_first, link_block, diag_second = consts + total
    out = (row_blocks, 1, slab, width)
    return column_first.reshape(out), column_second.reshape(out), diag_first, link_block, diag_second


def solution(mesh):
    placed = (
        P(None, "row", None, "col", None, None),
        P(None, "row", "col", None),
        P(None, "row", "col", None),
        P(),
        P(),
        P(),
        P(),
        P(),
    )
    return jax.shard_map(
        body,
        mesh=mesh,
        in_specs=placed,
        out_specs=(
            P(None, "row", "col", None),
            P(None, "row", "col", None),
            P("col", None),
            P("col", None),
            P("col", None),
        ),
        check_vma=False,
    )
```

```python
import functools

import jax
import jax.numpy as jnp
from jax import lax
from jax.experimental import pallas as pl
from jax.experimental.pallas import tpu as pltpu
from jax.sharding import PartitionSpec as P

precise = lax.Precision.HIGHEST
SMEM = pl.BlockSpec(memory_space=pltpu.SMEM)
VMEM = pl.BlockSpec(memory_space=pltpu.VMEM)
HBM = pl.BlockSpec(memory_space=pltpu.HBM)
ANY = pl.BlockSpec(memory_space=pl.ANY)


def exact_dot(left, right, left_dim=1):
    dims = (((left_dim,), (0,)), ((), ()))
    return lax.dot_general(left, right, dims, precision=precise, preferred_element_type=jnp.float32)


def split_dot(left, right, left_dim=1):
    def halves(value):
        if value.dtype == jnp.bfloat16:
            return [value]
        high = value.astype(jnp.bfloat16)
        return [high, (value - high.astype(jnp.float32)).astype(jnp.bfloat16)]

    dims = (((left_dim,), (0,)), ((), ()))
    total = None
    for i, a in enumerate(halves(left)):
        for j, b in enumerate(halves(right)):
            if i + j < 2:
                term = lax.dot_general(a, b, dims, preferred_element_type=jnp.float32)
                total = term if total is None else total + term
    return total


def listed(struct_ref, blocks, n_row):
    ids = lax.broadcasted_iota(jnp.int32, (blocks, 1, 1), 0) * n_row + lax.axis_index("row")

    def look(place, found):
        return jnp.where(ids == struct_ref[place], 1, found)

    found = lax.fori_loop(0, struct_ref.shape[0], look, jnp.zeros((blocks, 1, 1), jnp.int32))
    return found == 1


def slice_of(row, turn, n_row):
    return turn * n_row + row


def place_of(piece, n_row):
    return piece % n_row, piece // n_row


def product_kernel(n_row, n_col, first_bits, struct1, struct2, inv1, inv2, stored, pieces, *rest):
    cycle = n_col // n_row
    keeps, sends = rest[:2], rest[2:4]
    loose, factor = rest[4:]
    row_blocks = stored.shape[0]
    _, col_blocks, _, slab, width = loose.shape
    here_row, here_col = lax.axis_index("row"), lax.axis_index("col")

    group = here_col // n_row
    for m in range(n_row):
        row = here_row ^ m
        for s in range(cycle):
            slot = slice_of(row, lax.rem(s - group + cycle, cycle), n_row)
            for p in range(2):
                for b in range(col_blocks):
                    loose[p, b, slot] = pieces[m, s, p, b].astype(loose.dtype)
    for p, (struct, inverse) in enumerate(((struct1, inv1), (struct2, inv2))):

        def look(place, found):
            return tuple(f | (struct[place] == b * n_col + here_col).astype(jnp.int32) for b, f in enumerate(found))

        found = lax.fori_loop(0, struct.shape[0], look, (jnp.int32(0),) * col_blocks)
        blocks = loose[p].reshape(col_blocks * width, width).astype(jnp.bfloat16)
        product = split_dot(blocks, inverse[...])
        for b in range(col_blocks):
            place = slice(b * width, (b + 1) * width)
            factor[place, p * width : (p + 1) * width] = jnp.where(found[b] == 1, product[place], 0.0).astype(jnp.bfloat16)

    half = row_blocks // 2
    step = 2 if row_blocks % 2 == 0 else 1
    for a in range(0, row_blocks, step):
        wide = [jnp.concatenate([stored[a + i, b] for b in range(col_blocks)], axis=1) for i in range(step)]
        totals = jnp.dot(jnp.concatenate(wide, axis=0), factor[...], preferred_element_type=jnp.float32)
        for i in range(step):
            total = totals[i * width : (i + 1) * width]
            group, place = divmod(a + i, half)
            bit = first_bits[group]
            upper = ((here_col >> bit) & 1) == 1
            for p in range(2):
                for j in range(n_col // 2):
                    low = ((j >> bit) << (bit + 1)) | (j & ((1 << bit) - 1))
                    high = low | (1 << bit)
                    x = total[low * slab : (low + 1) * slab, p * width : (p + 1) * width]
                    y = total[high * slab : (high + 1) * slab, p * width : (p + 1) * width]
                    keeps[group][j, p, place] = jnp.where(upper, y, x)
                    sends[group][j, p, place] = jnp.where(upper, x, y).astype(jnp.bfloat16)


def prepare_kernel(link, inv1, inv2, after, linked, out, whole):
    slab = out.shape[1]
    linked[...] = exact_dot(link[...].astype(jnp.float32), inv2[...])
    link = linked[...]
    gram1 = exact_dot(inv1[...], inv1[...], 0)
    across = exact_dot(gram1, link)
    whole[0] = gram1
    whole[1] = -across
    whole[2] = exact_dot(inv2[...], inv2[...], 0) + exact_dot(link, across, 0)
    place = pl.ds(pl.multiple_of(lax.axis_index("col") * slab, slab), slab)
    out[...] = whole[:, place, :]


def form_kernel(n_row, struct1, struct2, inv1, inv2, base, rows):
    slices, _, blocks, slab, width = base.shape
    for p, (struct, inverse) in enumerate(((struct1, inv1), (struct2, inv2))):
        keep = listed(struct, blocks, n_row)
        flat = base[:, p].astype(jnp.float32).reshape(slices * blocks * slab, width).astype(jnp.bfloat16)
        product = split_dot(flat, inverse[...]).reshape(slices, blocks, slab, width)
        rows[:, p] = jnp.where(keep[None], product, 0.0).astype(jnp.bfloat16)


def sum_kernel(last_bit, rows, total_low, total_high, linked, after, out):
    _, _, half, slab, width = total_low.shape
    mine = (lax.axis_index("col") >> last_bit) & 1

    def gathered(p):
        parts = [total[place, p].reshape(half * slab, width) for place in (mine, 1 - mine) for total in (total_low, total_high)]
        return jnp.concatenate(parts, axis=0)

    def factor(p):
        return rows[:, p].astype(jnp.float32).reshape(-1, width).astype(jnp.bfloat16)

    link = linked[...]
    sum1 = gathered(0)
    u2 = factor(1)
    first = split_dot(factor(0), sum1, 0)
    cross = split_dot(u2, sum1, 0)
    top = cross.T - split_dot(first, link)
    second = split_dot(u2, gathered(1), 0) - split_dot(cross, link) - split_dot(link, top, 0)
    across = width // 2
    for i, part in enumerate((first, top, second)):
        part = part.reshape(width // slab, slab, width)
        for h in range(2):
            out[h, :, i] = part[:, :, h * across : (h + 1) * across]


def column_kernel(n_row, struct1, struct2, kept_low, came_low, kept_high, came_high, linked, column1, column2):
    blocks, slab, width = column1.shape
    sums = []
    for p in range(2):
        parts = [k[p] + c[p].astype(jnp.float32) for k, c in ((kept_low, came_low), (kept_high, came_high))]
        sums.append(jnp.concatenate(parts, axis=0))
    col1 = jnp.where(listed(struct1, blocks, n_row), -sums[0], 0.0)
    column1[...] = col1
    carried = split_dot(col1.reshape(blocks * slab, width), linked[...]).reshape(col1.shape)
    column2[...] = jnp.where(listed(struct2, blocks, n_row), -(sums[1] + carried), 0.0)


def swapped(value, axis, size, mask):
    return lax.ppermute(value, axis, [(i, i ^ mask) for i in range(size)])


def halves(value, axis, ways):
    kept, sent = (lax.dynamic_index_in_dim(value, way, axis, keepdims=False) for way in ways)
    return kept, sent


def body(stored_inverse, panel_first, panel_second, panel_link, inv_first, inv_second, struct_first, struct_second):
    n_row, n_col = lax.axis_size("row"), lax.axis_size("col")
    here_col = lax.axis_index("col")
    row_blocks, _, col_blocks, _, width, _ = stored_inverse.shape
    slab = width // n_col
    cycle = n_col // n_row
    n_bits = n_col.bit_length() - 1
    f32, bf16 = jnp.float32, jnp.bfloat16
    shape = jax.ShapeDtypeStruct
    big = pltpu.CompilerParams(vmem_limit_bytes=12 * 1024 * 1024)
    stored = stored_inverse.reshape(row_blocks, col_blocks, width, width)
    panel = (row_blocks, slab, width)

    panels = [panel_first.reshape(panel), panel_second.reshape(panel)]
    _, turn = place_of(here_col, n_row)
    picks = [((s - turn + cycle) % cycle).astype(jnp.uint32) for s in range(cycle)]
    ways = [(here_col >> bit) & 1 for bit in range(n_bits)]
    ways = [(way.astype(jnp.uint32), (1 - way).astype(jnp.uint32)) for way in ways]
    core = lax.axis_index("row") & 1
    cores = (core.astype(jnp.uint32), (1 - core).astype(jnp.uint32))
    panels, picks, ways, cores = lax.optimization_barrier((panels, picks, ways, cores))

    raw = lax.optimization_barrier(jnp.stack(panels))
    turns = raw.reshape(2, col_blocks, cycle, slab, width)
    got = []
    for s in range(cycle):
        moves = []
        for r in range(n_row):
            for c in range(n_col):
                row, t = place_of(c, n_row)
                moves.append((r * n_col + c, row * n_col + r + (s - t) % cycle * n_row))
        part = lax.dynamic_index_in_dim(turns, picks[s], 2, keepdims=False)
        got.append(lax.ppermute(part, ("row", "col"), moves))
    base = jnp.stack([raw, swapped(raw, "col", n_col, n_col // 2)])

    pieces = {0: got}
    bit = n_row // 2
    while bit > 1:
        for m, parts in list(pieces.items()):
            pieces[m ^ bit] = [swapped(part, "row", n_row, bit) for part in parts]
        bit //= 2
    pieces = jnp.stack([jnp.stack(pieces[m]) for m in sorted(pieces)])
    pieces, base = lax.optimization_barrier((pieces, base))
    rows = pl.pallas_call(
        functools.partial(form_kernel, n_row),
        out_shape=shape(base.shape, bf16),
        in_specs=[SMEM, SMEM] + [VMEM] * 3,
        out_specs=VMEM,
        compiler_params=big,
        name="form",
        cost_estimate=pl.CostEstimate(flops=8 * width**3, bytes_accessed=4 * width**2, transcendentals=0),
    )(struct_first, struct_second, inv_first, inv_second, base)
    beside, rows = lax.optimization_barrier((swapped(pieces, "row", n_row, 1), rows))
    pieces = jnp.stack([pieces, beside], axis=1).reshape((n_row,) + pieces.shape[1:])

    orders = (list(range(n_bits)), [1, 0] + list(range(2, n_bits)))
    half = row_blocks // 2
    block = (2, half, slab, width)
    kept = (n_col // 2,) + block
    split = pl.pallas_call(
        functools.partial(product_kernel, n_row, n_col, (orders[0][0], orders[1][0])),
        out_shape=[shape(kept, f32)] * 2 + [shape(kept, bf16)] * 2,
        in_specs=[SMEM, SMEM] + [VMEM] * 4,
        out_specs=[VMEM] * 4,
        scratch_shapes=[
            pltpu.VMEM((2, col_blocks, n_col, slab, width), bf16 if slab % 16 == 0 else f32),
            pltpu.VMEM((col_blocks * width, 2 * width), bf16),
        ],
        compiler_params=big,
        name="products",
    )(struct_first, struct_second, inv_first, inv_second, stored, pieces)

    linked, consts = pl.pallas_call(
        prepare_kernel,
        out_shape=[shape((width, width), f32), shape((3, slab, width), f32)],
        in_specs=[VMEM] * 3 + [ANY],
        out_specs=[VMEM] * 2,
        scratch_shapes=[pltpu.VMEM((3, width, width), f32)],
        compiler_params=big,
        name="prepare",
        cost_estimate=pl.CostEstimate(flops=6 * 10 * width**3, bytes_accessed=8 * width**2, transcendentals=0),
    )(panel_link, inv_first, inv_second, split[0])

    state = [(split[g], swapped(split[2 + g], "col", n_col, 1 << orders[g][0])) for g in range(2)]
    left = [sorted(set(range(n_bits)) - {order[0]}) for order in orders]
    for i in range(1, n_bits):
        totals, last = [], []
        for g in range(2):
            keep, came = state[g]
            bit = orders[g][i]
            inner = 1 << left[g].index(bit)
            left[g].remove(bit)
            totals.append(keep + came.astype(f32))
            keep, send = halves(totals[g].reshape((-1, 2, inner) + block), 1, ways[bit])
            keep, send = keep.reshape((-1,) + block), send.astype(bf16).reshape((-1,) + block)
            last.append((keep, send))
        if i < n_bits - 1 and orders[0][i] != orders[1][i]:
            state = [(keep, swapped(send, "col", n_col, 1 << order[i])) for (keep, send), order in zip(last, orders)]
        else:
            came = swapped(jnp.stack([send for _, send in last]), "col", n_col, 1 << orders[0][i])
            state = [(keep, came[g]) for g, (keep, _) in enumerate(last)]

    sums = pl.pallas_call(
        functools.partial(sum_kernel, n_bits - 1),
        out_shape=shape((2, n_col, 3, slab, width // 2), f32),
        in_specs=[VMEM] * 4 + [ANY],
        out_specs=VMEM,
        compiler_params=big,
        name="sums",
    )(rows, *totals, linked, consts)
    keep, send = halves(sums, 0, cores)
    sums = keep + swapped(send, "row", n_row, 1)
    view = sums.reshape(-1, 2, 2, 3, slab, width // 2)

    def part(high, low):
        return halves(halves(view, 1, ways[1])[high], 1, ways[0])[low]

    sums = part(0, 0)
    for mask in (1, 2, 3):
        sums = sums + swapped(part(mask >> 1, mask & 1).astype(bf16), "col", n_col, mask).astype(f32)
    for bit in range(2, n_bits - 1):
        keep, send = halves(sums.reshape(-1, 2, 3, slab, width // 2), 1, ways[bit])
        sums = keep + swapped(send.astype(bf16), "col", n_col, 1 << bit).astype(f32)
    keep, send = (part.astype(bf16) for part in halves(sums.reshape(2, 3, slab, width // 2), 0, ways[n_bits - 1]))
    across = [(r * n_col + c, (r ^ 2) * n_col + (c ^ (n_col // 2))) for r in range(n_row) for c in range(n_col)]
    near = keep.astype(f32) + swapped(send, "col", n_col, n_col // 2).astype(f32)
    far = swapped(keep, "row", n_row, 2).astype(f32) + lax.ppermute(send, ("row", "col"), across).astype(f32)
    mine = near + far
    for bit in range(2, n_row.bit_length() - 1):
        mine = mine + swapped(mine, "row", n_row, 1 << bit)

    mine, state = lax.optimization_barrier((mine, state))
    column_first, column_second = pl.pallas_call(
        functools.partial(column_kernel, n_row),
        out_shape=[shape(panel, f32)] * 2,
        in_specs=[SMEM, SMEM] + [VMEM] * 5,
        out_specs=[VMEM] * 2,
        compiler_params=big,
        name="columns",
    )(struct_first, struct_second, *[part[0] for pair in state for part in pair], linked)

    pair = jnp.stack([mine, swapped(mine, "row", n_row, 1)])
    total = jnp.concatenate([lax.dynamic_index_in_dim(pair, way, 0, keepdims=False) for way in cores], axis=-1)
    diag_first, link_block, diag_second = consts + total
    out = (row_blocks, 1, slab, width)
    return column_first.reshape(out), column_second.reshape(out), diag_first, link_block, diag_second


def solution(mesh):
    placed = (
        P(None, "row", None, "col", None, None),
        P(None, "row", "col", None),
        P(None, "row", "col", None),
        P(),
        P(),
        P(),
        P(),
        P(),
    )
    return jax.shard_map(
        body,
        mesh=mesh,
        in_specs=placed,
        out_specs=(
            P(None, "row", "col", None),
            P(None, "row", "col", None),
            P("col", None),
            P("col", None),
            P("col", None),
        ),
        check_vma=False,
    )
```

```python
import functools

import jax
import jax.numpy as jnp
from jax import lax
from jax.experimental import pallas as pl
from jax.experimental.pallas import tpu as pltpu
from jax.sharding import PartitionSpec as P

precise = lax.Precision.HIGHEST
SMEM = pl.BlockSpec(memory_space=pltpu.SMEM)
VMEM = pl.BlockSpec(memory_space=pltpu.VMEM)
HBM = pl.BlockSpec(memory_space=pltpu.HBM)
ANY = pl.BlockSpec(memory_space=pl.ANY)


def exact_dot(left, right, left_dim=1):
    dims = (((left_dim,), (0,)), ((), ()))
    return lax.dot_general(left, right, dims, precision=precise, preferred_element_type=jnp.float32)


def split_dot(left, right, left_dim=1):
    def halves(value):
        if value.dtype == jnp.bfloat16:
            return [value]
        high = value.astype(jnp.bfloat16)
        return [high, (value - high.astype(jnp.float32)).astype(jnp.bfloat16)]

    dims = (((left_dim,), (0,)), ((), ()))
    total = None
    for i, a in enumerate(halves(left)):
        for j, b in enumerate(halves(right)):
            if i + j < 2:
                term = lax.dot_general(a, b, dims, preferred_element_type=jnp.float32)
                total = term if total is None else total + term
    return total


def listed(struct_ref, blocks, n_row):
    ids = lax.broadcasted_iota(jnp.int32, (blocks, 1, 1), 0) * n_row + lax.axis_index("row")

    def look(place, found):
        return jnp.where(ids == struct_ref[place], 1, found)

    found = lax.fori_loop(0, struct_ref.shape[0], look, jnp.zeros((blocks, 1, 1), jnp.int32))
    return found == 1


def slice_of(row, turn, n_row):
    return turn * n_row + row


def place_of(piece, n_row):
    return piece % n_row, piece // n_row


def product_kernel(n_row, n_col, first_bits, struct1, struct2, inv1, inv2, stored, pieces, *rest):
    cycle = n_col // n_row
    keeps, sends = rest[:2], rest[2:4]
    loose, factor = rest[4:]
    row_blocks = stored.shape[0]
    _, col_blocks, _, slab, width = loose.shape
    here_row, here_col = lax.axis_index("row"), lax.axis_index("col")

    group = here_col // n_row
    for m in range(n_row):
        row = here_row ^ m
        for s in range(cycle):
            slot = slice_of(row, lax.rem(s - group + cycle, cycle), n_row)
            for p in range(2):
                for b in range(col_blocks):
                    loose[p, b, slot] = pieces[m, s, p, b].astype(loose.dtype)
    for p, (struct, inverse) in enumerate(((struct1, inv1), (struct2, inv2))):

        def look(place, found):
            return tuple(f | (struct[place] == b * n_col + here_col).astype(jnp.int32) for b, f in enumerate(found))

        found = lax.fori_loop(0, struct.shape[0], look, (jnp.int32(0),) * col_blocks)
        blocks = loose[p].reshape(col_blocks * width, width).astype(jnp.bfloat16)
        product = split_dot(blocks, inverse[...])
        for b in range(col_blocks):
            place = slice(b * width, (b + 1) * width)
            factor[place, p * width : (p + 1) * width] = jnp.where(found[b] == 1, product[place], 0.0).astype(jnp.bfloat16)

    half = row_blocks // 2
    step = 2 if row_blocks % 2 == 0 else 1
    for a in range(0, row_blocks, step):
        wide = [jnp.concatenate([stored[a + i, b] for b in range(col_blocks)], axis=1) for i in range(step)]
        totals = jnp.dot(jnp.concatenate(wide, axis=0), factor[...], preferred_element_type=jnp.float32)
        for i in range(step):
            total = totals[i * width : (i + 1) * width]
            group, place = divmod(a + i, half)
            bit = first_bits[group]
            upper = ((here_col >> bit) & 1) == 1
            for p in range(2):
                for j in range(n_col // 2):
                    low = ((j >> bit) << (bit + 1)) | (j & ((1 << bit) - 1))
                    high = low | (1 << bit)
                    x = total[low * slab : (low + 1) * slab, p * width : (p + 1) * width]
                    y = total[high * slab : (high + 1) * slab, p * width : (p + 1) * width]
                    keeps[group][j, p, place] = jnp.where(upper, y, x)
                    sends[group][j, p, place] = jnp.where(upper, x, y).astype(jnp.bfloat16)


def prepare_kernel(link, inv1, inv2, after, linked, out, whole):
    slab = out.shape[1]
    linked[...] = exact_dot(link[...].astype(jnp.float32), inv2[...])
    link = linked[...]
    gram1 = exact_dot(inv1[...], inv1[...], 0)
    across = exact_dot(gram1, link)
    whole[0] = gram1
    whole[1] = -across
    whole[2] = exact_dot(inv2[...], inv2[...], 0) + exact_dot(link, across, 0)
    place = pl.ds(pl.multiple_of(lax.axis_index("col") * slab, slab), slab)
    out[...] = whole[:, place, :]


def form_kernel(n_row, struct1, struct2, inv1, inv2, base, rows):
    slices, _, blocks, slab, width = base.shape
    for p, (struct, inverse) in enumerate(((struct1, inv1), (struct2, inv2))):
        keep = listed(struct, blocks, n_row)
        flat = base[:, p].astype(jnp.float32).reshape(slices * blocks * slab, width).astype(jnp.bfloat16)
        product = split_dot(flat, inverse[...]).reshape(slices, blocks, slab, width)
        rows[:, p] = jnp.where(keep[None], product, 0.0).astype(jnp.bfloat16)


def sum_kernel(last_bit, rows, total_low, total_high, linked, after, out):
    _, _, half, slab, width = total_low.shape
    mine = (lax.axis_index("col") >> last_bit) & 1

    def gathered(p):
        parts = [total[place, p].reshape(half * slab, width) for place in (mine, 1 - mine) for total in (total_low, total_high)]
        return jnp.concatenate(parts, axis=0)

    def factor(p):
        return rows[:, p].astype(jnp.float32).reshape(-1, width).astype(jnp.bfloat16)

    link = linked[...]
    sum1 = gathered(0)
    u2 = factor(1)
    first = split_dot(factor(0), sum1, 0)
    cross = split_dot(u2, sum1, 0)
    top = cross.T - split_dot(first, link)
    second = split_dot(u2, gathered(1), 0) - split_dot(cross, link) - split_dot(link, top, 0)
    across = width // 2
    for i, part in enumerate((first, top, second)):
        part = part.reshape(width // slab, slab, width)
        for h in range(2):
            out[h, :, i] = part[:, :, h * across : (h + 1) * across]


def column_kernel(n_row, struct1, struct2, kept_low, came_low, kept_high, came_high, linked, column1, column2):
    blocks, slab, width = column1.shape
    sums = []
    for p in range(2):
        parts = [k[p] + c[p].astype(jnp.float32) for k, c in ((kept_low, came_low), (kept_high, came_high))]
        sums.append(jnp.concatenate(parts, axis=0))
    col1 = jnp.where(listed(struct1, blocks, n_row), -sums[0], 0.0)
    column1[...] = col1
    carried = split_dot(col1.reshape(blocks * slab, width), linked[...]).reshape(col1.shape)
    column2[...] = jnp.where(listed(struct2, blocks, n_row), -(sums[1] + carried), 0.0)


def swapped(value, axis, size, mask):
    return lax.ppermute(value, axis, [(i, i ^ mask) for i in range(size)])


def halves(value, axis, ways):
    kept, sent = (lax.dynamic_index_in_dim(value, way, axis, keepdims=False) for way in ways)
    return kept, sent


def body(stored_inverse, panel_first, panel_second, panel_link, inv_first, inv_second, struct_first, struct_second):
    n_row, n_col = lax.axis_size("row"), lax.axis_size("col")
    here_col = lax.axis_index("col")
    row_blocks, _, col_blocks, _, width, _ = stored_inverse.shape
    slab = width // n_col
    cycle = n_col // n_row
    n_bits = n_col.bit_length() - 1
    f32, bf16 = jnp.float32, jnp.bfloat16
    shape = jax.ShapeDtypeStruct
    big = pltpu.CompilerParams(vmem_limit_bytes=12 * 1024 * 1024)
    stored = stored_inverse.reshape(row_blocks, col_blocks, width, width)
    panel = (row_blocks, slab, width)

    panels = [panel_first.reshape(panel), panel_second.reshape(panel)]
    _, turn = place_of(here_col, n_row)
    picks = [((s - turn + cycle) % cycle).astype(jnp.uint32) for s in range(cycle)]
    ways = [(here_col >> bit) & 1 for bit in range(n_bits)]
    ways = [(way.astype(jnp.uint32), (1 - way).astype(jnp.uint32)) for way in ways]
    core = lax.axis_index("row") & 1
    cores = (core.astype(jnp.uint32), (1 - core).astype(jnp.uint32))
    quads = [(((here_col >> (n_bits - 1)) << 1) | ((here_col >> 1) & 1)) ^ m for m in range(4)]
    quads = [quad.astype(jnp.uint32) for quad in quads]
    panels, picks, ways, cores, quads = lax.optimization_barrier((panels, picks, ways, cores, quads))

    raw = lax.optimization_barrier(jnp.stack(panels))
    turns = raw.reshape(2, col_blocks, cycle, slab, width)
    got = []
    for s in range(cycle):
        moves = []
        for r in range(n_row):
            for c in range(n_col):
                row, t = place_of(c, n_row)
                moves.append((r * n_col + c, row * n_col + r + (s - t) % cycle * n_row))
        part = lax.dynamic_index_in_dim(turns, picks[s], 2, keepdims=False)
        got.append(lax.ppermute(part, ("row", "col"), moves))
    base = jnp.stack([raw, swapped(raw, "col", n_col, n_col // 2)])

    pieces = {0: got}
    bit = n_row // 2
    while bit > 1:
        for m, parts in list(pieces.items()):
            pieces[m ^ bit] = [swapped(part, "row", n_row, bit) for part in parts]
        bit //= 2
    pieces = jnp.stack([jnp.stack(pieces[m]) for m in sorted(pieces)])
    pieces, base = lax.optimization_barrier((pieces, base))
    rows = pl.pallas_call(
        functools.partial(form_kernel, n_row),
        out_shape=shape(base.shape, bf16),
        in_specs=[SMEM, SMEM] + [VMEM] * 3,
        out_specs=VMEM,
        compiler_params=big,
        name="form",
        cost_estimate=pl.CostEstimate(flops=8 * width**3, bytes_accessed=4 * width**2, transcendentals=0),
    )(struct_first, struct_second, inv_first, inv_second, base)
    beside, rows = lax.optimization_barrier((swapped(pieces, "row", n_row, 1), rows))
    pieces = jnp.stack([pieces, beside], axis=1).reshape((n_row,) + pieces.shape[1:])

    orders = (list(range(n_bits)), [1, 0] + list(range(2, n_bits)))
    half = row_blocks // 2
    block = (2, half, slab, width)
    kept = (n_col // 2,) + block
    split = pl.pallas_call(
        functools.partial(product_kernel, n_row, n_col, (orders[0][0], orders[1][0])),
        out_shape=[shape(kept, f32)] * 2 + [shape(kept, bf16)] * 2,
        in_specs=[SMEM, SMEM] + [VMEM] * 4,
        out_specs=[VMEM] * 4,
        scratch_shapes=[
            pltpu.VMEM((2, col_blocks, n_col, slab, width), bf16 if slab % 16 == 0 else f32),
            pltpu.VMEM((col_blocks * width, 2 * width), bf16),
        ],
        compiler_params=big,
        name="products",
    )(struct_first, struct_second, inv_first, inv_second, stored, pieces)

    linked, consts = pl.pallas_call(
        prepare_kernel,
        out_shape=[shape((width, width), f32), shape((3, slab, width), f32)],
        in_specs=[VMEM] * 3 + [ANY],
        out_specs=[VMEM] * 2,
        scratch_shapes=[pltpu.VMEM((3, width, width), f32)],
        compiler_params=big,
        name="prepare",
        cost_estimate=pl.CostEstimate(flops=6 * 10 * width**3, bytes_accessed=8 * width**2, transcendentals=0),
    )(panel_link, inv_first, inv_second, split[0])

    state = [(split[g], swapped(split[2 + g], "col", n_col, 1 << orders[g][0])) for g in range(2)]
    left = [sorted(set(range(n_bits)) - {order[0]}) for order in orders]
    for i in range(1, n_bits):
        totals, last = [], []
        for g in range(2):
            keep, came = state[g]
            bit = orders[g][i]
            inner = 1 << left[g].index(bit)
            left[g].remove(bit)
            totals.append(keep + came.astype(f32))
            keep, send = halves(totals[g].reshape((-1, 2, inner) + block), 1, ways[bit])
            keep, send = keep.reshape((-1,) + block), send.astype(bf16).reshape((-1,) + block)
            last.append((keep, send))
        if i < n_bits - 1 and orders[0][i] != orders[1][i]:
            state = [(keep, swapped(send, "col", n_col, 1 << order[i])) for (keep, send), order in zip(last, orders)]
        else:
            came = swapped(jnp.stack([send for _, send in last]), "col", n_col, 1 << orders[0][i])
            state = [(keep, came[g]) for g, (keep, _) in enumerate(last)]

    sums = pl.pallas_call(
        functools.partial(sum_kernel, n_bits - 1),
        out_shape=shape((2, n_col, 3, slab, width // 2), f32),
        in_specs=[VMEM] * 4 + [ANY],
        out_specs=VMEM,
        compiler_params=big,
        name="sums",
    )(rows, *totals, linked, consts)
    keep, send = halves(sums, 0, cores)
    sums = keep + swapped(send, "row", n_row, 1)
    tail = (3, slab, width // 2)
    keep, send = (part.astype(bf16) for part in halves(sums.reshape((-1, 2) + tail), 1, ways[0]))
    across = [(r * n_col + c, (r ^ 2) * n_col + (c ^ 1)) for r in range(n_row) for c in range(n_col)]
    near = keep.astype(f32) + swapped(send, "col", n_col, 1).astype(f32)
    far = swapped(keep, "row", n_row, 2).astype(f32) + lax.ppermute(send, ("row", "col"), across).astype(f32)
    sums = near + far
    for bit in range(2, n_bits - 1):
        keep, send = halves(sums.reshape((-1, 2, 2) + tail), 1, ways[bit])
        sums = keep + swapped(send.astype(bf16), "col", n_col, 1 << bit).astype(f32)
    parts = [lax.dynamic_index_in_dim(sums.reshape((4,) + tail), quad, 0, keepdims=False) for quad in quads]
    mine = parts[0]
    for m in range(1, 4):
        mask = ((m >> 1) << (n_bits - 1)) | ((m & 1) << 1)
        mine = mine + swapped(parts[m].astype(bf16), "col", n_col, mask).astype(f32)
    for bit in range(2, n_row.bit_length() - 1):
        mine = mine + swapped(mine, "row", n_row, 1 << bit)

    mine, state = lax.optimization_barrier((mine, state))
    column_first, column_second = pl.pallas_call(
        functools.partial(column_kernel, n_row),
        out_shape=[shape(panel, f32)] * 2,
        in_specs=[SMEM, SMEM] + [VMEM] * 5,
        out_specs=[VMEM] * 2,
        compiler_params=big,
        name="columns",
    )(struct_first, struct_second, *[part[0] for pair in state for part in pair], linked)

    pair = jnp.stack([mine, swapped(mine, "row", n_row, 1)])
    total = jnp.concatenate([lax.dynamic_index_in_dim(pair, way, 0, keepdims=False) for way in cores], axis=-1)
    diag_first, link_block, diag_second = consts + total
    out = (row_blocks, 1, slab, width)
    return column_first.reshape(out), column_second.reshape(out), diag_first, link_block, diag_second


def solution(mesh):
    placed = (
        P(None, "row", None, "col", None, None),
        P(None, "row", "col", None),
        P(None, "row", "col", None),
        P(),
        P(),
        P(),
        P(),
        P(),
    )
    return jax.shard_map(
        body,
        mesh=mesh,
        in_specs=placed,
        out_specs=(
            P(None, "row", "col", None),
            P(None, "row", "col", None),
            P("col", None),
            P("col", None),
            P("col", None),
        ),
        check_vma=False,
    )
```

```python
import functools

import jax
import jax.numpy as jnp
from jax import lax
from jax.experimental import pallas as pl
from jax.experimental.pallas import tpu as pltpu
from jax.sharding import PartitionSpec as P

precise = lax.Precision.HIGHEST
SMEM = pl.BlockSpec(memory_space=pltpu.SMEM)
VMEM = pl.BlockSpec(memory_space=pltpu.VMEM)
HBM = pl.BlockSpec(memory_space=pltpu.HBM)
ANY = pl.BlockSpec(memory_space=pl.ANY)


def exact_dot(left, right, left_dim=1):
    dims = (((left_dim,), (0,)), ((), ()))
    return lax.dot_general(left, right, dims, precision=precise, preferred_element_type=jnp.float32)


def split_dot(left, right, left_dim=1):
    def halves(value):
        if value.dtype == jnp.bfloat16:
            return [value]
        high = value.astype(jnp.bfloat16)
        return [high, (value - high.astype(jnp.float32)).astype(jnp.bfloat16)]

    dims = (((left_dim,), (0,)), ((), ()))
    total = None
    for i, a in enumerate(halves(left)):
        for j, b in enumerate(halves(right)):
            if i + j < 2:
                term = lax.dot_general(a, b, dims, preferred_element_type=jnp.float32)
                total = term if total is None else total + term
    return total


def listed(struct_ref, blocks, n_row):
    ids = lax.broadcasted_iota(jnp.int32, (blocks, 1, 1), 0) * n_row + lax.axis_index("row")

    def look(place, found):
        return jnp.where(ids == struct_ref[place], 1, found)

    found = lax.fori_loop(0, struct_ref.shape[0], look, jnp.zeros((blocks, 1, 1), jnp.int32))
    return found == 1


def place_of(piece, n_row):
    return piece % n_row, piece // n_row


def product_kernel(n_row, n_col, first_bits, struct1, struct2, inv1, inv2, stored, pieces, *rest):
    cycle = n_col // n_row
    keeps, sends = rest[:2], rest[2:4]
    (factor,) = rest[4:]
    row_blocks = stored.shape[0]
    _, _, _, col_blocks, slab, width = pieces.shape
    packed = jnp.bfloat16 if slab % 16 == 0 else jnp.float32
    here_row, here_col = lax.axis_index("row"), lax.axis_index("col")

    group = here_col // n_row
    places = [(row ^ here_row, lax.rem(turn + group, cycle)) for turn in range(cycle) for row in range(n_row)]
    for p, (struct, inverse) in enumerate(((struct1, inv1), (struct2, inv2))):

        def look(place, found):
            return tuple(f | (struct[place] == b * n_col + here_col).astype(jnp.int32) for b, f in enumerate(found))

        found = lax.fori_loop(0, struct.shape[0], look, (jnp.int32(0),) * col_blocks)
        slices = [pieces[m, s, p, b].astype(packed) for b in range(col_blocks) for m, s in places]
        blocks = jnp.concatenate(slices, axis=0).astype(jnp.bfloat16)
        product = split_dot(blocks, inverse[...])
        for b in range(col_blocks):
            place = slice(b * width, (b + 1) * width)
            factor[place, p * width : (p + 1) * width] = jnp.where(found[b] == 1, product[place], 0.0).astype(jnp.bfloat16)

    half = row_blocks // 2
    step = 2 if row_blocks % 2 == 0 else 1
    for a in range(0, row_blocks, step):
        wide = [jnp.concatenate([stored[a + i, b] for b in range(col_blocks)], axis=1) for i in range(step)]
        totals = jnp.dot(jnp.concatenate(wide, axis=0), factor[...], preferred_element_type=jnp.float32)
        for i in range(step):
            total = totals[i * width : (i + 1) * width]
            group, place = divmod(a + i, half)
            bit = first_bits[group]
            upper = ((here_col >> bit) & 1) == 1
            for p in range(2):
                for j in range(n_col // 2):
                    low = ((j >> bit) << (bit + 1)) | (j & ((1 << bit) - 1))
                    high = low | (1 << bit)
                    x = total[low * slab : (low + 1) * slab, p * width : (p + 1) * width]
                    y = total[high * slab : (high + 1) * slab, p * width : (p + 1) * width]
                    keeps[group][j, p, place] = jnp.where(upper, y, x)
                    sends[group][j, p, place] = jnp.where(upper, x, y).astype(jnp.bfloat16)


def prepare_kernel(link, inv1, inv2, after, linked, out, whole):
    slab = out.shape[1]
    linked[...] = exact_dot(link[...].astype(jnp.float32), inv2[...])
    link = linked[...]
    gram1 = exact_dot(inv1[...], inv1[...], 0)
    across = exact_dot(gram1, link)
    whole[0] = gram1
    whole[1] = -across
    whole[2] = exact_dot(inv2[...], inv2[...], 0) + exact_dot(link, across, 0)
    place = pl.ds(pl.multiple_of(lax.axis_index("col") * slab, slab), slab)
    out[...] = whole[:, place, :]


def form_kernel(n_row, struct1, struct2, inv1, inv2, base, rows):
    slices, _, blocks, slab, width = base.shape
    for p, (struct, inverse) in enumerate(((struct1, inv1), (struct2, inv2))):
        keep = listed(struct, blocks, n_row)
        flat = base[:, p].astype(jnp.float32).reshape(slices * blocks * slab, width).astype(jnp.bfloat16)
        product = split_dot(flat, inverse[...]).reshape(slices, blocks, slab, width)
        rows[:, p] = jnp.where(keep[None], product, 0.0).astype(jnp.bfloat16)


def sum_kernel(last_bit, rows, total_low, total_high, linked, after, out):
    _, _, half, slab, width = total_low.shape
    mine = (lax.axis_index("col") >> last_bit) & 1

    def gathered(p):
        parts = [total[place, p].reshape(half * slab, width) for place in (mine, 1 - mine) for total in (total_low, total_high)]
        return jnp.concatenate(parts, axis=0)

    def factor(p):
        return rows[:, p].astype(jnp.float32).reshape(-1, width).astype(jnp.bfloat16)

    link = linked[...]
    sum1 = gathered(0)
    u2 = factor(1)
    first = split_dot(factor(0), sum1, 0)
    cross = split_dot(u2, sum1, 0)
    top = cross.T - split_dot(first, link)
    second = split_dot(u2, gathered(1), 0) - split_dot(cross, link) - split_dot(link, top, 0)
    across = width // 2
    for i, part in enumerate((first, top, second)):
        part = part.reshape(width // slab, slab, width)
        for h in range(2):
            out[h, :, i] = part[:, :, h * across : (h + 1) * across]


def column_kernel(n_row, struct1, struct2, kept_low, came_low, kept_high, came_high, linked, column1, column2):
    blocks, slab, width = column1.shape
    sums = []
    for p in range(2):
        parts = [k[p] + c[p].astype(jnp.float32) for k, c in ((kept_low, came_low), (kept_high, came_high))]
        sums.append(jnp.concatenate(parts, axis=0))
    col1 = jnp.where(listed(struct1, blocks, n_row), -sums[0], 0.0)
    column1[...] = col1
    carried = split_dot(col1.reshape(blocks * slab, width), linked[...]).reshape(col1.shape)
    column2[...] = jnp.where(listed(struct2, blocks, n_row), -(sums[1] + carried), 0.0)


def swapped(value, axis, size, mask):
    return lax.ppermute(value, axis, [(i, i ^ mask) for i in range(size)])


def halves(value, axis, ways):
    kept, sent = (lax.dynamic_index_in_dim(value, way, axis, keepdims=False) for way in ways)
    return kept, sent


def body(stored_inverse, panel_first, panel_second, panel_link, inv_first, inv_second, struct_first, struct_second):
    n_row, n_col = lax.axis_size("row"), lax.axis_size("col")
    here_col = lax.axis_index("col")
    row_blocks, _, col_blocks, _, width, _ = stored_inverse.shape
    slab = width // n_col
    cycle = n_col // n_row
    n_bits = n_col.bit_length() - 1
    f32, bf16 = jnp.float32, jnp.bfloat16
    shape = jax.ShapeDtypeStruct
    big = pltpu.CompilerParams(vmem_limit_bytes=12 * 1024 * 1024)
    stored = stored_inverse.reshape(row_blocks, col_blocks, width, width)
    panel = (row_blocks, slab, width)

    panels = [panel_first.reshape(panel), panel_second.reshape(panel)]
    _, turn = place_of(here_col, n_row)
    picks = [((s - turn + cycle) % cycle).astype(jnp.uint32) for s in range(cycle)]
    ways = [(here_col >> bit) & 1 for bit in range(n_bits)]
    ways = [(way.astype(jnp.uint32), (1 - way).astype(jnp.uint32)) for way in ways]
    core = lax.axis_index("row") & 1
    cores = (core.astype(jnp.uint32), (1 - core).astype(jnp.uint32))
    quads = [(here_col & 3) ^ m for m in range(4)]
    quads = [quad.astype(jnp.uint32) for quad in quads]
    panels, picks, ways, cores, quads = lax.optimization_barrier((panels, picks, ways, cores, quads))

    raw = lax.optimization_barrier(jnp.stack(panels))
    turns = raw.reshape(2, col_blocks, cycle, slab, width)
    got = []
    for s in range(cycle):
        moves = []
        for r in range(n_row):
            for c in range(n_col):
                row, t = place_of(c, n_row)
                moves.append((r * n_col + c, row * n_col + r + (s - t) % cycle * n_row))
        part = lax.dynamic_index_in_dim(turns, picks[s], 2, keepdims=False)
        got.append(lax.ppermute(part, ("row", "col"), moves))
    base = jnp.stack([raw, swapped(raw, "col", n_col, n_col // 2)])

    pieces = {0: got}
    bit = n_row // 2
    while bit > 1:
        for m, parts in list(pieces.items()):
            pieces[m ^ bit] = [swapped(part, "row", n_row, bit) for part in parts]
        bit //= 2
    pieces = jnp.stack([jnp.stack(pieces[m]) for m in sorted(pieces)])
    pieces, base = lax.optimization_barrier((pieces, base))
    rows = pl.pallas_call(
        functools.partial(form_kernel, n_row),
        out_shape=shape(base.shape, bf16),
        in_specs=[SMEM, SMEM] + [VMEM] * 3,
        out_specs=VMEM,
        compiler_params=big,
        name="form",
        cost_estimate=pl.CostEstimate(flops=8 * width**3, bytes_accessed=4 * width**2, transcendentals=0),
    )(struct_first, struct_second, inv_first, inv_second, base)
    beside, rows = lax.optimization_barrier((swapped(pieces, "row", n_row, 1), rows))
    pieces = jnp.stack([pieces, beside], axis=1).reshape((n_row,) + pieces.shape[1:])

    orders = (list(range(n_bits)), [1, 0] + list(range(2, n_bits)))
    half = row_blocks // 2
    block = (2, half, slab, width)
    kept = (n_col // 2,) + block
    split = pl.pallas_call(
        functools.partial(product_kernel, n_row, n_col, (orders[0][0], orders[1][0])),
        out_shape=[shape(kept, f32)] * 2 + [shape(kept, bf16)] * 2,
        in_specs=[SMEM, SMEM] + [VMEM] * 4,
        out_specs=[VMEM] * 4,
        scratch_shapes=[
            pltpu.VMEM((col_blocks * width, 2 * width), bf16),
        ],
        compiler_params=big,
        name="products",
    )(struct_first, struct_second, inv_first, inv_second, stored, pieces)

    linked, consts = pl.pallas_call(
        prepare_kernel,
        out_shape=[shape((width, width), f32), shape((3, slab, width), f32)],
        in_specs=[VMEM] * 3 + [ANY],
        out_specs=[VMEM] * 2,
        scratch_shapes=[pltpu.VMEM((3, width, width), f32)],
        compiler_params=big,
        name="prepare",
        cost_estimate=pl.CostEstimate(flops=6 * 10 * width**3, bytes_accessed=8 * width**2, transcendentals=0),
    )(panel_link, inv_first, inv_second, split[0])

    state = [(split[g], swapped(split[2 + g], "col", n_col, 1 << orders[g][0])) for g in range(2)]
    left = [sorted(set(range(n_bits)) - {order[0]}) for order in orders]
    for i in range(1, n_bits):
        totals, last = [], []
        for g in range(2):
            keep, came = state[g]
            bit = orders[g][i]
            inner = 1 << left[g].index(bit)
            left[g].remove(bit)
            totals.append(keep + came.astype(f32))
            keep, send = halves(totals[g].reshape((-1, 2, inner) + block), 1, ways[bit])
            keep, send = keep.reshape((-1,) + block), send.astype(bf16).reshape((-1,) + block)
            last.append((keep, send))
        if i < n_bits - 1 and orders[0][i] != orders[1][i]:
            state = [(keep, swapped(send, "col", n_col, 1 << order[i])) for (keep, send), order in zip(last, orders)]
        else:
            came = swapped(jnp.stack([send for _, send in last]), "col", n_col, 1 << orders[0][i])
            state = [(keep, came[g]) for g, (keep, _) in enumerate(last)]

    sums = pl.pallas_call(
        functools.partial(sum_kernel, n_bits - 1),
        out_shape=shape((2, n_col, 3, slab, width // 2), f32),
        in_specs=[VMEM] * 4 + [ANY],
        out_specs=VMEM,
        compiler_params=big,
        name="sums",
    )(rows, *totals, linked, consts)
    keep, send = halves(sums, 0, cores)
    sums = keep + swapped(send, "row", n_row, 1)
    tail = (3, slab, width // 2)
    parts = [lax.dynamic_index_in_dim(sums.reshape((-1, 4) + tail), quad, 1, keepdims=False) for quad in quads]
    sums = parts[0]
    for m in range(1, 4):
        sums = sums + swapped(parts[m].astype(bf16), "col", n_col, m).astype(f32)
    for bit in range(2, n_bits - 1):
        keep, send = halves(sums.reshape((-1, 2) + tail), 1, ways[bit])
        sums = keep + swapped(send.astype(bf16), "col", n_col, 1 << bit).astype(f32)
    keep, send = (part.astype(bf16) for part in halves(sums.reshape((2,) + tail), 0, ways[n_bits - 1]))
    across = [(r * n_col + c, (r ^ 2) * n_col + (c ^ (n_col // 2))) for r in range(n_row) for c in range(n_col)]
    near = keep.astype(f32) + swapped(send, "col", n_col, n_col // 2).astype(f32)
    far = swapped(keep, "row", n_row, 2).astype(f32) + lax.ppermute(send, ("row", "col"), across).astype(f32)
    mine = near + far
    for bit in range(2, n_row.bit_length() - 1):
        mine = mine + swapped(mine, "row", n_row, 1 << bit)

    mine, state = lax.optimization_barrier((mine, state))
    column_first, column_second = pl.pallas_call(
        functools.partial(column_kernel, n_row),
        out_shape=[shape(panel, f32)] * 2,
        in_specs=[SMEM, SMEM] + [VMEM] * 5,
        out_specs=[VMEM] * 2,
        compiler_params=big,
        name="columns",
    )(struct_first, struct_second, *[part[0] for pair in state for part in pair], linked)

    pair = jnp.stack([mine, swapped(mine, "row", n_row, 1)])
    total = jnp.concatenate([lax.dynamic_index_in_dim(pair, way, 0, keepdims=False) for way in cores], axis=-1)
    diag_first, link_block, diag_second = consts + total
    out = (row_blocks, 1, slab, width)
    return column_first.reshape(out), column_second.reshape(out), diag_first, link_block, diag_second


def solution(mesh):
    placed = (
        P(None, "row", None, "col", None, None),
        P(None, "row", "col", None),
        P(None, "row", "col", None),
        P(),
        P(),
        P(),
        P(),
        P(),
    )
    return jax.shard_map(
        body,
        mesh=mesh,
        in_specs=placed,
        out_specs=(
            P(None, "row", "col", None),
            P(None, "row", "col", None),
            P("col", None),
            P("col", None),
            P("col", None),
        ),
        check_vma=False,
    )
```

```python
import functools

import jax
import jax.numpy as jnp
from jax import lax
from jax.experimental import pallas as pl
from jax.experimental.pallas import tpu as pltpu
from jax.sharding import PartitionSpec as P

precise = lax.Precision.HIGHEST
SMEM = pl.BlockSpec(memory_space=pltpu.SMEM)
VMEM = pl.BlockSpec(memory_space=pltpu.VMEM)
HBM = pl.BlockSpec(memory_space=pltpu.HBM)
ANY = pl.BlockSpec(memory_space=pl.ANY)


def exact_dot(left, right, left_dim=1):
    dims = (((left_dim,), (0,)), ((), ()))
    return lax.dot_general(left, right, dims, precision=precise, preferred_element_type=jnp.float32)


def split_dot(left, right, left_dim=1):
    def halves(value):
        if value.dtype == jnp.bfloat16:
            return [value]
        high = value.astype(jnp.bfloat16)
        return [high, (value - high.astype(jnp.float32)).astype(jnp.bfloat16)]

    dims = (((left_dim,), (0,)), ((), ()))
    total = None
    for i, a in enumerate(halves(left)):
        for j, b in enumerate(halves(right)):
            if i + j < 2:
                term = lax.dot_general(a, b, dims, preferred_element_type=jnp.float32)
                total = term if total is None else total + term
    return total


def listed(struct_ref, blocks, n_row):
    ids = lax.broadcasted_iota(jnp.int32, (blocks, 1, 1), 0) * n_row + lax.axis_index("row")

    def look(place, found):
        return jnp.where(ids == struct_ref[place], 1, found)

    found = lax.fori_loop(0, struct_ref.shape[0], look, jnp.zeros((blocks, 1, 1), jnp.int32))
    return found == 1


def place_of(piece, n_row):
    return piece % n_row, piece // n_row


def product_kernel(n_row, n_col, first_bits, struct1, struct2, inv1, inv2, stored, pieces, *rest):
    cycle = n_col // n_row
    keeps, sends = rest[:2], rest[2:4]
    (factor,) = rest[4:]
    row_blocks = stored.shape[0]
    _, _, _, col_blocks, slab, width = pieces.shape
    packed = jnp.bfloat16 if slab % 16 == 0 else jnp.float32
    here_row, here_col = lax.axis_index("row"), lax.axis_index("col")

    group = here_col // n_row
    places = [(row ^ here_row, lax.rem(turn + group, cycle)) for turn in range(cycle) for row in range(n_row)]
    for p, (struct, inverse) in enumerate(((struct1, inv1), (struct2, inv2))):

        def look(place, found):
            return tuple(f | (struct[place] == b * n_col + here_col).astype(jnp.int32) for b, f in enumerate(found))

        found = lax.fori_loop(0, struct.shape[0], look, (jnp.int32(0),) * col_blocks)
        slices = [pieces[m, s, p, b].astype(packed) for b in range(col_blocks) for m, s in places]
        blocks = jnp.concatenate(slices, axis=0).astype(jnp.bfloat16)
        product = split_dot(blocks, inverse[...])
        for b in range(col_blocks):
            place = slice(b * width, (b + 1) * width)
            factor[place, p * width : (p + 1) * width] = jnp.where(found[b] == 1, product[place], 0.0).astype(jnp.bfloat16)

    half = row_blocks // 2
    step = 2 if row_blocks % 2 == 0 else 1
    for a in range(0, row_blocks, step):
        wide = [jnp.concatenate([stored[a + i, b] for b in range(col_blocks)], axis=1) for i in range(step)]
        totals = jnp.dot(jnp.concatenate(wide, axis=0), factor[...], preferred_element_type=jnp.float32)
        for i in range(step):
            total = totals[i * width : (i + 1) * width]
            group, place = divmod(a + i, half)
            bit = first_bits[group]
            upper = ((here_col >> bit) & 1) == 1
            for p in range(2):
                for j in range(n_col // 2):
                    low = ((j >> bit) << (bit + 1)) | (j & ((1 << bit) - 1))
                    high = low | (1 << bit)
                    x = total[low * slab : (low + 1) * slab, p * width : (p + 1) * width]
                    y = total[high * slab : (high + 1) * slab, p * width : (p + 1) * width]
                    keeps[group][j, p, place] = jnp.where(upper, y, x)
                    sends[group][j, p, place] = jnp.where(upper, x, y).astype(jnp.bfloat16)


def prepare_kernel(link, inv1, inv2, after, linked, out, whole):
    slab = out.shape[1]
    linked[...] = exact_dot(link[...].astype(jnp.float32), inv2[...])
    link = linked[...]
    gram1 = exact_dot(inv1[...], inv1[...], 0)
    across = exact_dot(gram1, link)
    whole[0] = gram1
    whole[1] = -across
    whole[2] = exact_dot(inv2[...], inv2[...], 0) + exact_dot(link, across, 0)
    place = pl.ds(pl.multiple_of(lax.axis_index("col") * slab, slab), slab)
    out[...] = whole[:, place, :]


def form_kernel(n_row, struct1, struct2, inv1, inv2, base, after, rows):
    slices, _, blocks, slab, width = base.shape
    for p, (struct, inverse) in enumerate(((struct1, inv1), (struct2, inv2))):
        keep = listed(struct, blocks, n_row)
        flat = base[:, p].astype(jnp.float32).reshape(slices * blocks * slab, width).astype(jnp.bfloat16)
        product = split_dot(flat, inverse[...]).reshape(slices, blocks, slab, width)
        rows[:, p] = jnp.where(keep[None], product, 0.0).astype(jnp.bfloat16)


def sum_kernel(last_bit, rows, total_low, total_high, linked, after, out):
    _, _, half, slab, width = total_low.shape
    mine = (lax.axis_index("col") >> last_bit) & 1

    def gathered(p):
        parts = [total[place, p].reshape(half * slab, width) for place in (mine, 1 - mine) for total in (total_low, total_high)]
        return jnp.concatenate(parts, axis=0)

    def factor(p):
        return rows[:, p].astype(jnp.float32).reshape(-1, width).astype(jnp.bfloat16)

    link = linked[...]
    sum1 = gathered(0)
    u2 = factor(1)
    first = split_dot(factor(0), sum1, 0)
    cross = split_dot(u2, sum1, 0)
    top = cross.T - split_dot(first, link)
    second = split_dot(u2, gathered(1), 0) - split_dot(cross, link) - split_dot(link, top, 0)
    across = width // 2
    for i, part in enumerate((first, top, second)):
        part = part.reshape(width // slab, slab, width)
        for h in range(2):
            out[h, :, i] = part[:, :, h * across : (h + 1) * across]


def column_kernel(n_row, struct1, struct2, kept_low, came_low, kept_high, came_high, linked, column1, column2):
    blocks, slab, width = column1.shape
    sums = []
    for p in range(2):
        parts = [k[p] + c[p].astype(jnp.float32) for k, c in ((kept_low, came_low), (kept_high, came_high))]
        sums.append(jnp.concatenate(parts, axis=0))
    col1 = jnp.where(listed(struct1, blocks, n_row), -sums[0], 0.0)
    column1[...] = col1
    carried = split_dot(col1.reshape(blocks * slab, width), linked[...]).reshape(col1.shape)
    column2[...] = jnp.where(listed(struct2, blocks, n_row), -(sums[1] + carried), 0.0)


def swapped(value, axis, size, mask):
    return lax.ppermute(value, axis, [(i, i ^ mask) for i in range(size)])


def halves(value, axis, ways):
    kept, sent = (lax.dynamic_index_in_dim(value, way, axis, keepdims=False) for way in ways)
    return kept, sent


def body(stored_inverse, panel_first, panel_second, panel_link, inv_first, inv_second, struct_first, struct_second):
    n_row, n_col = lax.axis_size("row"), lax.axis_size("col")
    here_col = lax.axis_index("col")
    row_blocks, _, col_blocks, _, width, _ = stored_inverse.shape
    slab = width // n_col
    cycle = n_col // n_row
    n_bits = n_col.bit_length() - 1
    f32, bf16 = jnp.float32, jnp.bfloat16
    shape = jax.ShapeDtypeStruct
    big = pltpu.CompilerParams(vmem_limit_bytes=12 * 1024 * 1024)
    stored = stored_inverse.reshape(row_blocks, col_blocks, width, width)
    panel = (row_blocks, slab, width)

    panels = [panel_first.reshape(panel), panel_second.reshape(panel)]
    _, turn = place_of(here_col, n_row)
    picks = [((s - turn + cycle) % cycle).astype(jnp.uint32) for s in range(cycle)]
    ways = [(here_col >> bit) & 1 for bit in range(n_bits)]
    ways = [(way.astype(jnp.uint32), (1 - way).astype(jnp.uint32)) for way in ways]
    core = lax.axis_index("row") & 1
    cores = (core.astype(jnp.uint32), (1 - core).astype(jnp.uint32))
    quads = [(here_col & 3) ^ m for m in range(4)]
    quads = [quad.astype(jnp.uint32) for quad in quads]
    panels, picks, ways, cores, quads = lax.optimization_barrier((panels, picks, ways, cores, quads))

    raw = lax.optimization_barrier(jnp.stack(panels))
    turns = raw.reshape(2, col_blocks, cycle, slab, width)
    got = []
    for s in range(cycle):
        moves = []
        for r in range(n_row):
            for c in range(n_col):
                row, t = place_of(c, n_row)
                moves.append((r * n_col + c, row * n_col + r + (s - t) % cycle * n_row))
        part = lax.dynamic_index_in_dim(turns, picks[s], 2, keepdims=False)
        got.append(lax.ppermute(part, ("row", "col"), moves))
    base = jnp.stack([raw, swapped(raw, "col", n_col, n_col // 2)])

    pieces = {0: got}
    bit = n_row // 2
    while bit > 1:
        for m, parts in list(pieces.items()):
            pieces[m ^ bit] = [swapped(part, "row", n_row, bit) for part in parts]
        bit //= 2
    pieces = jnp.stack([jnp.stack(pieces[m]) for m in sorted(pieces)])
    beside = swapped(pieces, "row", n_row, 1)
    pieces = jnp.stack([pieces, beside], axis=1).reshape((n_row,) + pieces.shape[1:])

    orders = (list(range(n_bits)), [1, 0] + list(range(2, n_bits)))
    half = row_blocks // 2
    block = (2, half, slab, width)
    kept = (n_col // 2,) + block
    split = pl.pallas_call(
        functools.partial(product_kernel, n_row, n_col, (orders[0][0], orders[1][0])),
        out_shape=[shape(kept, f32)] * 2 + [shape(kept, bf16)] * 2,
        in_specs=[SMEM, SMEM] + [VMEM] * 4,
        out_specs=[VMEM] * 4,
        scratch_shapes=[
            pltpu.VMEM((col_blocks * width, 2 * width), bf16),
        ],
        compiler_params=big,
        name="products",
    )(struct_first, struct_second, inv_first, inv_second, stored, pieces)

    rows = pl.pallas_call(
        functools.partial(form_kernel, n_row),
        out_shape=shape(base.shape, bf16),
        in_specs=[SMEM, SMEM] + [VMEM] * 3 + [ANY],
        out_specs=VMEM,
        compiler_params=big,
        name="form",
        cost_estimate=pl.CostEstimate(flops=100 * width**3, bytes_accessed=4 * width**2, transcendentals=0),
    )(struct_first, struct_second, inv_first, inv_second, base, split[0])
    linked, consts = pl.pallas_call(
        prepare_kernel,
        out_shape=[shape((width, width), f32), shape((3, slab, width), f32)],
        in_specs=[VMEM] * 3 + [ANY],
        out_specs=[VMEM] * 2,
        scratch_shapes=[pltpu.VMEM((3, width, width), f32)],
        compiler_params=big,
        name="prepare",
        cost_estimate=pl.CostEstimate(flops=60 * width**3, bytes_accessed=8 * width**2, transcendentals=0),
    )(panel_link, inv_first, inv_second, rows)

    state = [(split[g], swapped(split[2 + g], "col", n_col, 1 << orders[g][0])) for g in range(2)]
    state = lax.optimization_barrier(state)
    left = [sorted(set(range(n_bits)) - {order[0]}) for order in orders]
    for i in range(1, n_bits):
        totals, last = [], []
        for g in range(2):
            keep, came = state[g]
            bit = orders[g][i]
            inner = 1 << left[g].index(bit)
            left[g].remove(bit)
            totals.append(keep + came.astype(f32))
            keep, send = halves(totals[g].reshape((-1, 2, inner) + block), 1, ways[bit])
            keep, send = keep.reshape((-1,) + block), send.astype(bf16).reshape((-1,) + block)
            last.append((keep, send))
        if i < n_bits - 1 and orders[0][i] != orders[1][i]:
            state = [(keep, swapped(send, "col", n_col, 1 << order[i])) for (keep, send), order in zip(last, orders)]
        else:
            came = swapped(jnp.stack([send for _, send in last]), "col", n_col, 1 << orders[0][i])
            state = [(keep, came[g]) for g, (keep, _) in enumerate(last)]

    sums = pl.pallas_call(
        functools.partial(sum_kernel, n_bits - 1),
        out_shape=shape((2, n_col, 3, slab, width // 2), f32),
        in_specs=[VMEM] * 4 + [ANY],
        out_specs=VMEM,
        compiler_params=big,
        name="sums",
    )(rows, *totals, linked, consts)
    keep, send = halves(sums, 0, cores)
    sums = keep + swapped(send, "row", n_row, 1)
    tail = (3, slab, width // 2)
    parts = [lax.dynamic_index_in_dim(sums.reshape((-1, 4) + tail), quad, 1, keepdims=False) for quad in quads]
    sums = parts[0]
    for m in range(1, 4):
        sums = sums + swapped(parts[m].astype(bf16), "col", n_col, m).astype(f32)
    for bit in range(2, n_bits - 1):
        keep, send = halves(sums.reshape((-1, 2) + tail), 1, ways[bit])
        sums = keep + swapped(send.astype(bf16), "col", n_col, 1 << bit).astype(f32)
    keep, send = (part.astype(bf16) for part in halves(sums.reshape((2,) + tail), 0, ways[n_bits - 1]))
    across = [(r * n_col + c, (r ^ 2) * n_col + (c ^ (n_col // 2))) for r in range(n_row) for c in range(n_col)]
    near = keep.astype(f32) + swapped(send, "col", n_col, n_col // 2).astype(f32)
    far = swapped(keep, "row", n_row, 2).astype(f32) + lax.ppermute(send, ("row", "col"), across).astype(f32)
    mine = near + far
    for bit in range(2, n_row.bit_length() - 1):
        mine = mine + swapped(mine, "row", n_row, 1 << bit)

    mine, state = lax.optimization_barrier((mine, state))
    column_first, column_second = pl.pallas_call(
        functools.partial(column_kernel, n_row),
        out_shape=[shape(panel, f32)] * 2,
        in_specs=[SMEM, SMEM] + [VMEM] * 5,
        out_specs=[VMEM] * 2,
        compiler_params=big,
        name="columns",
    )(struct_first, struct_second, *[part[0] for pair in state for part in pair], linked)

    pair = jnp.stack([mine, swapped(mine, "row", n_row, 1)])
    total = jnp.concatenate([lax.dynamic_index_in_dim(pair, way, 0, keepdims=False) for way in cores], axis=-1)
    diag_first, link_block, diag_second = consts + total
    out = (row_blocks, 1, slab, width)
    return column_first.reshape(out), column_second.reshape(out), diag_first, link_block, diag_second


def solution(mesh):
    placed = (
        P(None, "row", None, "col", None, None),
        P(None, "row", "col", None),
        P(None, "row", "col", None),
        P(),
        P(),
        P(),
        P(),
        P(),
    )
    return jax.shard_map(
        body,
        mesh=mesh,
        in_specs=placed,
        out_specs=(
            P(None, "row", "col", None),
            P(None, "row", "col", None),
            P("col", None),
            P("col", None),
            P("col", None),
        ),
        check_vma=False,
    )
```

```python
import functools

import jax
import jax.numpy as jnp
from jax import lax
from jax.experimental import pallas as pl
from jax.experimental.pallas import tpu as pltpu
from jax.sharding import PartitionSpec as P

precise = lax.Precision.HIGHEST
SMEM = pl.BlockSpec(memory_space=pltpu.SMEM)
VMEM = pl.BlockSpec(memory_space=pltpu.VMEM)
HBM = pl.BlockSpec(memory_space=pltpu.HBM)
ANY = pl.BlockSpec(memory_space=pl.ANY)


def exact_dot(left, right, left_dim=1):
    dims = (((left_dim,), (0,)), ((), ()))
    return lax.dot_general(left, right, dims, precision=precise, preferred_element_type=jnp.float32)


def split_dot(left, right, left_dim=1):
    def halves(value):
        if value.dtype == jnp.bfloat16:
            return [value]
        high = value.astype(jnp.bfloat16)
        return [high, (value - high.astype(jnp.float32)).astype(jnp.bfloat16)]

    dims = (((left_dim,), (0,)), ((), ()))
    total = None
    for i, a in enumerate(halves(left)):
        for j, b in enumerate(halves(right)):
            if i + j < 2:
                term = lax.dot_general(a, b, dims, preferred_element_type=jnp.float32)
                total = term if total is None else total + term
    return total


def listed(struct_ref, blocks, n_row):
    ids = lax.broadcasted_iota(jnp.int32, (blocks, 1, 1), 0) * n_row + lax.axis_index("row")

    def look(place, found):
        return jnp.where(ids == struct_ref[place], 1, found)

    found = lax.fori_loop(0, struct_ref.shape[0], look, jnp.zeros((blocks, 1, 1), jnp.int32))
    return found == 1


def place_of(piece, n_row):
    return piece % n_row, piece // n_row


def product_kernel(n_row, n_col, first_bits, struct1, struct2, inv1, inv2, stored, pieces, *rest):
    cycle = n_col // n_row
    keeps, sends = rest[:2], rest[2:4]
    (factor,) = rest[4:]
    row_blocks = stored.shape[0]
    _, _, _, col_blocks, slab, width = pieces.shape
    packed = jnp.bfloat16 if slab % 16 == 0 else jnp.float32
    here_row, here_col = lax.axis_index("row"), lax.axis_index("col")

    group = here_col // n_row
    places = [(row ^ here_row, lax.rem(turn + group, cycle)) for turn in range(cycle) for row in range(n_row)]
    for p, (struct, inverse) in enumerate(((struct1, inv1), (struct2, inv2))):

        def look(place, found):
            return tuple(f | (struct[place] == b * n_col + here_col).astype(jnp.int32) for b, f in enumerate(found))

        found = lax.fori_loop(0, struct.shape[0], look, (jnp.int32(0),) * col_blocks)
        slices = [pieces[m, s, p, b].astype(packed) for b in range(col_blocks) for m, s in places]
        blocks = jnp.concatenate(slices, axis=0).astype(jnp.bfloat16)
        product = split_dot(blocks, inverse[...])
        for b in range(col_blocks):
            place = slice(b * width, (b + 1) * width)
            factor[place, p * width : (p + 1) * width] = jnp.where(found[b] == 1, product[place], 0.0).astype(jnp.bfloat16)

    half = row_blocks // 2
    step = 2 if row_blocks % 2 == 0 else 1
    for a in range(0, row_blocks, step):
        wide = [jnp.concatenate([stored[a + i, b] for b in range(col_blocks)], axis=1) for i in range(step)]
        totals = jnp.dot(jnp.concatenate(wide, axis=0), factor[...], preferred_element_type=jnp.float32)
        for i in range(step):
            total = totals[i * width : (i + 1) * width]
            group, place = divmod(a + i, half)
            bit = first_bits[group]
            upper = ((here_col >> bit) & 1) == 1
            for p in range(2):
                for j in range(n_col // 2):
                    low = ((j >> bit) << (bit + 1)) | (j & ((1 << bit) - 1))
                    high = low | (1 << bit)
                    x = total[low * slab : (low + 1) * slab, p * width : (p + 1) * width]
                    y = total[high * slab : (high + 1) * slab, p * width : (p + 1) * width]
                    keeps[group][j, p, place] = jnp.where(upper, y, x)
                    sends[group][j, p, place] = jnp.where(upper, x, y).astype(jnp.bfloat16)


def prepare_kernel(link, inv1, inv2, after, linked, out, whole):
    slab = out.shape[1]
    linked[...] = exact_dot(link[...].astype(jnp.float32), inv2[...])
    link = linked[...]
    gram1 = exact_dot(inv1[...], inv1[...], 0)
    across = exact_dot(gram1, link)
    whole[0] = gram1
    whole[1] = -across
    whole[2] = exact_dot(inv2[...], inv2[...], 0) + exact_dot(link, across, 0)
    place = pl.ds(pl.multiple_of(lax.axis_index("col") * slab, slab), slab)
    out[...] = whole[:, place, :]


def form_kernel(n_row, struct1, struct2, inv1, inv2, base, rows):
    slices, _, blocks, slab, width = base.shape
    for p, (struct, inverse) in enumerate(((struct1, inv1), (struct2, inv2))):
        keep = listed(struct, blocks, n_row)
        flat = base[:, p].astype(jnp.float32).reshape(slices * blocks * slab, width).astype(jnp.bfloat16)
        product = split_dot(flat, inverse[...]).reshape(slices, blocks, slab, width)
        rows[:, p] = jnp.where(keep[None], product, 0.0).astype(jnp.bfloat16)


def sum_kernel(last_bit, rows, total_low, total_high, linked, after, out):
    _, _, half, slab, width = total_low.shape
    mine = (lax.axis_index("col") >> last_bit) & 1

    def gathered(p):
        parts = [total[place, p].reshape(half * slab, width) for place in (mine, 1 - mine) for total in (total_low, total_high)]
        return jnp.concatenate(parts, axis=0)

    def factor(p):
        return rows[:, p].astype(jnp.float32).reshape(-1, width).astype(jnp.bfloat16)

    link = linked[...]
    sum1 = gathered(0)
    u2 = factor(1)
    first = split_dot(factor(0), sum1, 0)
    cross = split_dot(u2, sum1, 0)
    top = cross.T - split_dot(first, link)
    second = split_dot(u2, gathered(1), 0) - split_dot(cross, link) - split_dot(link, top, 0)
    for i, part in enumerate((first, top, second)):
        out[:, i] = part.reshape(width // slab, slab, width)


def column_kernel(n_row, struct1, struct2, kept_low, came_low, kept_high, came_high, linked, column1, column2):
    blocks, slab, width = column1.shape
    sums = []
    for p in range(2):
        parts = [k[p] + c[p].astype(jnp.float32) for k, c in ((kept_low, came_low), (kept_high, came_high))]
        sums.append(jnp.concatenate(parts, axis=0))
    col1 = jnp.where(listed(struct1, blocks, n_row), -sums[0], 0.0)
    column1[...] = col1
    carried = split_dot(col1.reshape(blocks * slab, width), linked[...]).reshape(col1.shape)
    column2[...] = jnp.where(listed(struct2, blocks, n_row), -(sums[1] + carried), 0.0)


def swapped(value, axis, size, mask):
    return lax.ppermute(value, axis, [(i, i ^ mask) for i in range(size)])


def halves(value, axis, ways):
    kept, sent = (lax.dynamic_index_in_dim(value, way, axis, keepdims=False) for way in ways)
    return kept, sent


def body(stored_inverse, panel_first, panel_second, panel_link, inv_first, inv_second, struct_first, struct_second):
    n_row, n_col = lax.axis_size("row"), lax.axis_size("col")
    here_col = lax.axis_index("col")
    row_blocks, _, col_blocks, _, width, _ = stored_inverse.shape
    slab = width // n_col
    cycle = n_col // n_row
    n_bits = n_col.bit_length() - 1
    f32, bf16 = jnp.float32, jnp.bfloat16
    shape = jax.ShapeDtypeStruct
    big = pltpu.CompilerParams(vmem_limit_bytes=12 * 1024 * 1024)
    stored = stored_inverse.reshape(row_blocks, col_blocks, width, width)
    panel = (row_blocks, slab, width)

    panels = [panel_first.reshape(panel), panel_second.reshape(panel)]
    _, turn = place_of(here_col, n_row)
    picks = [((s - turn + cycle) % cycle).astype(jnp.uint32) for s in range(cycle)]
    ways = [(here_col >> bit) & 1 for bit in range(n_bits)]
    ways = [(way.astype(jnp.uint32), (1 - way).astype(jnp.uint32)) for way in ways]
    quads = [(here_col & 3) ^ m for m in range(4)]
    quads = [quad.astype(jnp.uint32) for quad in quads]
    panels, picks, ways, quads = lax.optimization_barrier((panels, picks, ways, quads))

    raw = lax.optimization_barrier(jnp.stack(panels))
    turns = raw.reshape(2, col_blocks, cycle, slab, width)
    got = []
    for s in range(cycle):
        moves = []
        for r in range(n_row):
            for c in range(n_col):
                row, t = place_of(c, n_row)
                moves.append((r * n_col + c, row * n_col + r + (s - t) % cycle * n_row))
        part = lax.dynamic_index_in_dim(turns, picks[s], 2, keepdims=False)
        got.append(lax.ppermute(part, ("row", "col"), moves))
    base = jnp.stack([raw, swapped(raw, "col", n_col, n_col // 2)])

    pieces = {0: got}
    bit = n_row // 2
    while bit > 1:
        for m, parts in list(pieces.items()):
            pieces[m ^ bit] = [swapped(part, "row", n_row, bit) for part in parts]
        bit //= 2
    pieces = jnp.stack([jnp.stack(pieces[m]) for m in sorted(pieces)])
    pieces, base = lax.optimization_barrier((pieces, base))
    rows = pl.pallas_call(
        functools.partial(form_kernel, n_row),
        out_shape=shape(base.shape, bf16),
        in_specs=[SMEM, SMEM] + [VMEM] * 3,
        out_specs=VMEM,
        compiler_params=big,
        name="form",
        cost_estimate=pl.CostEstimate(flops=8 * width**3, bytes_accessed=4 * width**2, transcendentals=0),
    )(struct_first, struct_second, inv_first, inv_second, base)
    beside, rows = lax.optimization_barrier((swapped(pieces, "row", n_row, 1), rows))
    pieces = jnp.stack([pieces, beside], axis=1).reshape((n_row,) + pieces.shape[1:])

    orders = (list(range(n_bits)), [1, 0] + list(range(2, n_bits)))
    half = row_blocks // 2
    block = (2, half, slab, width)
    kept = (n_col // 2,) + block
    split = pl.pallas_call(
        functools.partial(product_kernel, n_row, n_col, (orders[0][0], orders[1][0])),
        out_shape=[shape(kept, f32)] * 2 + [shape(kept, bf16)] * 2,
        in_specs=[SMEM, SMEM] + [VMEM] * 4,
        out_specs=[VMEM] * 4,
        scratch_shapes=[
            pltpu.VMEM((col_blocks * width, 2 * width), bf16),
        ],
        compiler_params=big,
        name="products",
    )(struct_first, struct_second, inv_first, inv_second, stored, pieces)

    linked, consts = pl.pallas_call(
        prepare_kernel,
        out_shape=[shape((width, width), f32), shape((3, slab, width), f32)],
        in_specs=[VMEM] * 3 + [ANY],
        out_specs=[VMEM] * 2,
        scratch_shapes=[pltpu.VMEM((3, width, width), f32)],
        compiler_params=big,
        name="prepare",
        cost_estimate=pl.CostEstimate(flops=6 * 10 * width**3, bytes_accessed=8 * width**2, transcendentals=0),
    )(panel_link, inv_first, inv_second, split[0])

    state = [(split[g], swapped(split[2 + g], "col", n_col, 1 << orders[g][0])) for g in range(2)]
    left = [sorted(set(range(n_bits)) - {order[0]}) for order in orders]
    for i in range(1, n_bits):
        totals, last = [], []
        for g in range(2):
            keep, came = state[g]
            bit = orders[g][i]
            inner = 1 << left[g].index(bit)
            left[g].remove(bit)
            totals.append(keep + came.astype(f32))
            keep, send = halves(totals[g].reshape((-1, 2, inner) + block), 1, ways[bit])
            keep, send = keep.reshape((-1,) + block), send.astype(bf16).reshape((-1,) + block)
            last.append((keep, send))
        if i < n_bits - 1 and orders[0][i] != orders[1][i]:
            state = [(keep, swapped(send, "col", n_col, 1 << order[i])) for (keep, send), order in zip(last, orders)]
        else:
            came = swapped(jnp.stack([send for _, send in last]), "col", n_col, 1 << orders[0][i])
            state = [(keep, came[g]) for g, (keep, _) in enumerate(last)]

    sums = pl.pallas_call(
        functools.partial(sum_kernel, n_bits - 1),
        out_shape=shape((n_col, 3, slab, width), f32),
        in_specs=[VMEM] * 4 + [ANY],
        out_specs=VMEM,
        compiler_params=big,
        name="sums",
    )(rows, *totals, linked, consts)
    tail = (3, slab, width)
    parts = [lax.dynamic_index_in_dim(sums.reshape((-1, 4) + tail), quad, 1, keepdims=False) for quad in quads]
    sums = parts[0]
    for m in range(1, 4):
        sums = sums + swapped(parts[m].astype(bf16), "col", n_col, m).astype(f32)
    for bit in range(2, n_bits - 1):
        keep, send = halves(sums.reshape((-1, 2) + tail), 1, ways[bit])
        sums = keep + swapped(send.astype(bf16), "col", n_col, 1 << bit).astype(f32)
    sums, state = lax.optimization_barrier((sums, state))
    keep, send = (part.astype(bf16) for part in halves(sums.reshape((2,) + tail), 0, ways[n_bits - 1]))
    across = [(r * n_col + c, (r ^ 2) * n_col + (c ^ (n_col // 2))) for r in range(n_row) for c in range(n_col)]
    near = keep.astype(f32) + swapped(send, "col", n_col, n_col // 2).astype(f32)
    far = swapped(keep, "row", n_row, 2).astype(f32) + lax.ppermute(send, ("row", "col"), across).astype(f32)
    mine = near + far
    for bit in range(2, n_row.bit_length() - 1):
        mine = mine + swapped(mine, "row", n_row, 1 << bit)

    column_first, column_second = pl.pallas_call(
        functools.partial(column_kernel, n_row),
        out_shape=[shape(panel, f32)] * 2,
        in_specs=[SMEM, SMEM] + [VMEM] * 5,
        out_specs=[VMEM] * 2,
        compiler_params=big,
        name="columns",
    )(struct_first, struct_second, *[part[0] for pair in state for part in pair], linked)

    total = mine + swapped(mine, "row", n_row, 1)
    diag_first, link_block, diag_second = consts + total
    out = (row_blocks, 1, slab, width)
    return column_first.reshape(out), column_second.reshape(out), diag_first, link_block, diag_second


def solution(mesh):
    placed = (
        P(None, "row", None, "col", None, None),
        P(None, "row", "col", None),
        P(None, "row", "col", None),
        P(),
        P(),
        P(),
        P(),
        P(),
    )
    return jax.shard_map(
        body,
        mesh=mesh,
        in_specs=placed,
        out_specs=(
            P(None, "row", "col", None),
            P(None, "row", "col", None),
            P("col", None),
            P("col", None),
            P("col", None),
        ),
        check_vma=False,
    )
```

```python
import functools

import jax
import jax.numpy as jnp
from jax import lax
from jax.experimental import pallas as pl
from jax.experimental.pallas import tpu as pltpu
from jax.sharding import PartitionSpec as P

precise = lax.Precision.HIGHEST
SMEM = pl.BlockSpec(memory_space=pltpu.SMEM)
VMEM = pl.BlockSpec(memory_space=pltpu.VMEM)
HBM = pl.BlockSpec(memory_space=pltpu.HBM)
ANY = pl.BlockSpec(memory_space=pl.ANY)


def exact_dot(left, right, left_dim=1):
    dims = (((left_dim,), (0,)), ((), ()))
    return lax.dot_general(left, right, dims, precision=precise, preferred_element_type=jnp.float32)


def split_dot(left, right, left_dim=1):
    def halves(value):
        if value.dtype == jnp.bfloat16:
            return [value]
        high = value.astype(jnp.bfloat16)
        return [high, (value - high.astype(jnp.float32)).astype(jnp.bfloat16)]

    dims = (((left_dim,), (0,)), ((), ()))
    total = None
    for i, a in enumerate(halves(left)):
        for j, b in enumerate(halves(right)):
            if i + j < 2:
                term = lax.dot_general(a, b, dims, preferred_element_type=jnp.float32)
                total = term if total is None else total + term
    return total


def listed(struct_ref, blocks, n_row):
    ids = lax.broadcasted_iota(jnp.int32, (blocks, 1, 1), 0) * n_row + lax.axis_index("row")

    def look(place, found):
        return jnp.where(ids == struct_ref[place], 1, found)

    found = lax.fori_loop(0, struct_ref.shape[0], look, jnp.zeros((blocks, 1, 1), jnp.int32))
    return found == 1


def place_of(piece, n_row):
    return piece % n_row, piece // n_row


def product_kernel(n_row, n_col, first_bits, struct1, struct2, inv1, inv2, stored, pieces, *rest):
    cycle = n_col // n_row
    keeps, sends = rest[:2], rest[2:4]
    (factor,) = rest[4:]
    row_blocks = stored.shape[0]
    _, _, _, col_blocks, slab, width = pieces.shape
    packed = jnp.bfloat16 if slab % 16 == 0 else jnp.float32
    here_row, here_col = lax.axis_index("row"), lax.axis_index("col")

    group = here_col // n_row
    places = [(row ^ here_row, lax.rem(turn + group, cycle)) for turn in range(cycle) for row in range(n_row)]
    for p, (struct, inverse) in enumerate(((struct1, inv1), (struct2, inv2))):

        def look(place, found):
            return tuple(f | (struct[place] == b * n_col + here_col).astype(jnp.int32) for b, f in enumerate(found))

        found = lax.fori_loop(0, struct.shape[0], look, (jnp.int32(0),) * col_blocks)
        slices = [pieces[m, s, p, b].astype(packed) for b in range(col_blocks) for m, s in places]
        blocks = jnp.concatenate(slices, axis=0).astype(jnp.bfloat16)
        product = split_dot(blocks, inverse[...])
        for b in range(col_blocks):
            place = slice(b * width, (b + 1) * width)
            factor[place, p * width : (p + 1) * width] = jnp.where(found[b] == 1, product[place], 0.0).astype(jnp.bfloat16)

    half = row_blocks // 2
    step = 2 if row_blocks % 2 == 0 else 1
    for a in range(0, row_blocks, step):
        wide = [jnp.concatenate([stored[a + i, b] for b in range(col_blocks)], axis=1) for i in range(step)]
        totals = jnp.dot(jnp.concatenate(wide, axis=0), factor[...], preferred_element_type=jnp.float32)
        for i in range(step):
            total = totals[i * width : (i + 1) * width]
            group, place = divmod(a + i, half)
            bit = first_bits[group]
            upper = ((here_col >> bit) & 1) == 1
            for p in range(2):
                for j in range(n_col // 2):
                    low = ((j >> bit) << (bit + 1)) | (j & ((1 << bit) - 1))
                    high = low | (1 << bit)
                    x = total[low * slab : (low + 1) * slab, p * width : (p + 1) * width]
                    y = total[high * slab : (high + 1) * slab, p * width : (p + 1) * width]
                    keeps[group][j, p, place] = jnp.where(upper, y, x)
                    sends[group][j, p, place] = jnp.where(upper, x, y).astype(jnp.bfloat16)


def prepare_kernel(link, inv1, inv2, after, linked, out, whole):
    slab = out.shape[1]
    linked[...] = exact_dot(link[...].astype(jnp.float32), inv2[...])
    link = linked[...]
    gram1 = exact_dot(inv1[...], inv1[...], 0)
    across = exact_dot(gram1, link)
    whole[0] = gram1
    whole[1] = -across
    whole[2] = exact_dot(inv2[...], inv2[...], 0) + exact_dot(link, across, 0)
    place = pl.ds(pl.multiple_of(lax.axis_index("col") * slab, slab), slab)
    out[...] = whole[:, place, :]


def form_kernel(n_row, struct1, struct2, inv1, inv2, raw, other1, other2, after1, after2, rows):
    _, blocks, slab, width = raw.shape
    for p, (struct, inverse, other) in enumerate(((struct1, inv1, other1), (struct2, inv2, other2))):
        keep = listed(struct, blocks, n_row)
        both = [part.astype(jnp.float32).reshape(blocks * slab, width) for part in (raw[p], other[...])]
        flat = jnp.concatenate(both, axis=0).astype(jnp.bfloat16)
        product = split_dot(flat, inverse[...]).reshape(2, blocks, slab, width)
        rows[:, p] = jnp.where(keep[None], product, 0.0).astype(jnp.bfloat16)


def sum_kernel(last_bit, rows, total_low, total_high, linked, after, out):
    _, _, half, slab, width = total_low.shape
    mine = (lax.axis_index("col") >> last_bit) & 1

    def gathered(p):
        parts = [total[place, p].reshape(half * slab, width) for place in (mine, 1 - mine) for total in (total_low, total_high)]
        return jnp.concatenate(parts, axis=0)

    def factor(p):
        return rows[:, p].astype(jnp.float32).reshape(-1, width).astype(jnp.bfloat16)

    link = linked[...]
    sum1 = gathered(0)
    u2 = factor(1)
    first = split_dot(factor(0), sum1, 0)
    cross = split_dot(u2, sum1, 0)
    top = cross.T - split_dot(first, link)
    second = split_dot(u2, gathered(1), 0) - split_dot(cross, link) - split_dot(link, top, 0)
    across = width // 2
    for i, part in enumerate((first, top, second)):
        part = part.reshape(width // slab, slab, width)
        for h in range(2):
            out[h, :, i] = part[:, :, h * across : (h + 1) * across]


def column_kernel(n_row, struct1, struct2, kept_low, came_low, kept_high, came_high, linked, column1, column2):
    blocks, slab, width = column1.shape
    sums = []
    for p in range(2):
        parts = [k[p] + c[p].astype(jnp.float32) for k, c in ((kept_low, came_low), (kept_high, came_high))]
        sums.append(jnp.concatenate(parts, axis=0))
    col1 = jnp.where(listed(struct1, blocks, n_row), -sums[0], 0.0)
    column1[...] = col1
    carried = split_dot(col1.reshape(blocks * slab, width), linked[...]).reshape(col1.shape)
    column2[...] = jnp.where(listed(struct2, blocks, n_row), -(sums[1] + carried), 0.0)


def swapped(value, axis, size, mask):
    return lax.ppermute(value, axis, [(i, i ^ mask) for i in range(size)])


def halves(value, axis, ways):
    kept, sent = (lax.dynamic_index_in_dim(value, way, axis, keepdims=False) for way in ways)
    return kept, sent


def body(stored_inverse, panel_first, panel_second, panel_link, inv_first, inv_second, struct_first, struct_second):
    n_row, n_col = lax.axis_size("row"), lax.axis_size("col")
    here_col = lax.axis_index("col")
    row_blocks, _, col_blocks, _, width, _ = stored_inverse.shape
    slab = width // n_col
    cycle = n_col // n_row
    n_bits = n_col.bit_length() - 1
    f32, bf16 = jnp.float32, jnp.bfloat16
    shape = jax.ShapeDtypeStruct
    big = pltpu.CompilerParams(vmem_limit_bytes=12 * 1024 * 1024)
    stored = stored_inverse.reshape(row_blocks, col_blocks, width, width)
    panel = (row_blocks, slab, width)

    panels = [panel_first.reshape(panel), panel_second.reshape(panel)]
    _, turn = place_of(here_col, n_row)
    picks = [((s - turn + cycle) % cycle).astype(jnp.uint32) for s in range(cycle)]
    ways = [(here_col >> bit) & 1 for bit in range(n_bits)]
    ways = [(way.astype(jnp.uint32), (1 - way).astype(jnp.uint32)) for way in ways]
    core = lax.axis_index("row") & 1
    cores = (core.astype(jnp.uint32), (1 - core).astype(jnp.uint32))
    quads = [(here_col & 3) ^ m for m in range(4)]
    quads = [quad.astype(jnp.uint32) for quad in quads]
    panels, picks, ways, cores, quads = lax.optimization_barrier((panels, picks, ways, cores, quads))

    raw = lax.optimization_barrier(jnp.stack(panels))
    turns = raw.reshape(2, col_blocks, cycle, slab, width)
    got = []
    for s in range(cycle):
        moves = []
        for r in range(n_row):
            for c in range(n_col):
                row, t = place_of(c, n_row)
                moves.append((r * n_col + c, row * n_col + r + (s - t) % cycle * n_row))
        part = lax.dynamic_index_in_dim(turns, picks[s], 2, keepdims=False)
        got.append(lax.ppermute(part, ("row", "col"), moves))
    pieces = {0: got}
    bit = n_row // 2
    while bit > 1:
        for m, parts in list(pieces.items()):
            pieces[m ^ bit] = [swapped(part, "row", n_row, bit) for part in parts]
        bit //= 2
    pieces = jnp.stack([jnp.stack(pieces[m]) for m in sorted(pieces)])
    beside = swapped(pieces, "row", n_row, 1)
    pieces = jnp.stack([pieces, beside], axis=1).reshape((n_row,) + pieces.shape[1:])

    orders = (list(range(n_bits)), [1, 0] + list(range(2, n_bits)))
    half = row_blocks // 2
    block = (2, half, slab, width)
    kept = (n_col // 2,) + block
    split = pl.pallas_call(
        functools.partial(product_kernel, n_row, n_col, (orders[0][0], orders[1][0])),
        out_shape=[shape(kept, f32)] * 2 + [shape(kept, bf16)] * 2,
        in_specs=[SMEM, SMEM] + [VMEM] * 4,
        out_specs=[VMEM] * 4,
        scratch_shapes=[
            pltpu.VMEM((col_blocks * width, 2 * width), bf16),
        ],
        compiler_params=big,
        name="products",
    )(struct_first, struct_second, inv_first, inv_second, stored, pieces)

    linked, consts = pl.pallas_call(
        prepare_kernel,
        out_shape=[shape((width, width), f32), shape((3, slab, width), f32)],
        in_specs=[VMEM] * 3 + [ANY],
        out_specs=[VMEM] * 2,
        scratch_shapes=[pltpu.VMEM((3, width, width), f32)],
        compiler_params=big,
        name="prepare",
        cost_estimate=pl.CostEstimate(flops=6 * 10 * width**3, bytes_accessed=8 * width**2, transcendentals=0),
    )(panel_link, inv_first, inv_second, split[0])

    state = [(split[g], swapped(split[2 + g], "col", n_col, 1 << orders[g][0])) for g in range(2)]
    raw, consts = lax.optimization_barrier((raw, consts))
    others = [swapped(panel_rows, "col", n_col, n_col // 2) for panel_rows in raw]
    rows = pl.pallas_call(
        functools.partial(form_kernel, n_row),
        out_shape=shape((2,) + raw.shape, bf16),
        in_specs=[SMEM, SMEM] + [VMEM] * 5 + [ANY] * 2,
        out_specs=VMEM,
        compiler_params=big,
        name="form",
        cost_estimate=pl.CostEstimate(flops=8 * width**3, bytes_accessed=4 * width**2, transcendentals=0),
    )(struct_first, struct_second, inv_first, inv_second, raw, *others, state[0][1], state[1][1])
    left = [sorted(set(range(n_bits)) - {order[0]}) for order in orders]
    for i in range(1, n_bits):
        totals, last = [], []
        for g in range(2):
            keep, came = state[g]
            bit = orders[g][i]
            inner = 1 << left[g].index(bit)
            left[g].remove(bit)
            totals.append(keep + came.astype(f32))
            keep, send = halves(totals[g].reshape((-1, 2, inner) + block), 1, ways[bit])
            keep, send = keep.reshape((-1,) + block), send.astype(bf16).reshape((-1,) + block)
            last.append((keep, send))
        if i < n_bits - 1 and orders[0][i] != orders[1][i]:
            state = [(keep, swapped(send, "col", n_col, 1 << order[i])) for (keep, send), order in zip(last, orders)]
        else:
            came = swapped(jnp.stack([send for _, send in last]), "col", n_col, 1 << orders[0][i])
            state = [(keep, came[g]) for g, (keep, _) in enumerate(last)]

    sums = pl.pallas_call(
        functools.partial(sum_kernel, n_bits - 1),
        out_shape=shape((2, n_col, 3, slab, width // 2), f32),
        in_specs=[VMEM] * 4 + [ANY],
        out_specs=VMEM,
        compiler_params=big,
        name="sums",
    )(rows, *totals, linked, consts)
    keep, send = halves(sums, 0, cores)
    sums = keep + swapped(send, "row", n_row, 1)
    tail = (3, slab, width // 2)
    parts = [lax.dynamic_index_in_dim(sums.reshape((-1, 4) + tail), quad, 1, keepdims=False) for quad in quads]
    sums = parts[0]
    for m in range(1, 4):
        sums = sums + swapped(parts[m].astype(bf16), "col", n_col, m).astype(f32)
    for bit in range(2, n_bits - 1):
        keep, send = halves(sums.reshape((-1, 2) + tail), 1, ways[bit])
        sums = keep + swapped(send.astype(bf16), "col", n_col, 1 << bit).astype(f32)
    keep, send = (part.astype(bf16) for part in halves(sums.reshape((2,) + tail), 0, ways[n_bits - 1]))
    across = [(r * n_col + c, (r ^ 2) * n_col + (c ^ (n_col // 2))) for r in range(n_row) for c in range(n_col)]
    near = keep.astype(f32) + swapped(send, "col", n_col, n_col // 2).astype(f32)
    far = swapped(keep, "row", n_row, 2).astype(f32) + lax.ppermute(send, ("row", "col"), across).astype(f32)
    mine = near + far
    for bit in range(2, n_row.bit_length() - 1):
        mine = mine + swapped(mine, "row", n_row, 1 << bit)

    mine, state = lax.optimization_barrier((mine, state))
    column_first, column_second = pl.pallas_call(
        functools.partial(column_kernel, n_row),
        out_shape=[shape(panel, f32)] * 2,
        in_specs=[SMEM, SMEM] + [VMEM] * 5,
        out_specs=[VMEM] * 2,
        compiler_params=big,
        name="columns",
    )(struct_first, struct_second, *[part[0] for pair in state for part in pair], linked)

    pair = jnp.stack([mine, swapped(mine, "row", n_row, 1)])
    total = jnp.concatenate([lax.dynamic_index_in_dim(pair, way, 0, keepdims=False) for way in cores], axis=-1)
    diag_first, link_block, diag_second = consts + total
    out = (row_blocks, 1, slab, width)
    return column_first.reshape(out), column_second.reshape(out), diag_first, link_block, diag_second


def solution(mesh):
    placed = (
        P(None, "row", None, "col", None, None),
        P(None, "row", "col", None),
        P(None, "row", "col", None),
        P(),
        P(),
        P(),
        P(),
        P(),
    )
    return jax.shard_map(
        body,
        mesh=mesh,
        in_specs=placed,
        out_specs=(
            P(None, "row", "col", None),
            P(None, "row", "col", None),
            P("col", None),
            P("col", None),
            P("col", None),
        ),
        check_vma=False,
    )
```

```python
import functools

import jax
import jax.numpy as jnp
from jax import lax
from jax.experimental import pallas as pl
from jax.experimental.pallas import tpu as pltpu
from jax.sharding import PartitionSpec as P

precise = lax.Precision.HIGHEST
SMEM = pl.BlockSpec(memory_space=pltpu.SMEM)
VMEM = pl.BlockSpec(memory_space=pltpu.VMEM)
HBM = pl.BlockSpec(memory_space=pltpu.HBM)
ANY = pl.BlockSpec(memory_space=pl.ANY)


def exact_dot(left, right, left_dim=1):
    dims = (((left_dim,), (0,)), ((), ()))
    return lax.dot_general(left, right, dims, precision=precise, preferred_element_type=jnp.float32)


def split_dot(left, right, left_dim=1):
    def halves(value):
        if value.dtype == jnp.bfloat16:
            return [value]
        high = value.astype(jnp.bfloat16)
        return [high, (value - high.astype(jnp.float32)).astype(jnp.bfloat16)]

    dims = (((left_dim,), (0,)), ((), ()))
    total = None
    for i, a in enumerate(halves(left)):
        for j, b in enumerate(halves(right)):
            if i + j < 2:
                term = lax.dot_general(a, b, dims, preferred_element_type=jnp.float32)
                total = term if total is None else total + term
    return total


def listed(struct_ref, blocks, n_row):
    ids = lax.broadcasted_iota(jnp.int32, (blocks, 1, 1), 0) * n_row + lax.axis_index("row")

    def look(place, found):
        return jnp.where(ids == struct_ref[place], 1, found)

    found = lax.fori_loop(0, struct_ref.shape[0], look, jnp.zeros((blocks, 1, 1), jnp.int32))
    return found == 1


def place_of(piece, n_row):
    return piece % n_row, piece // n_row


def product_kernel(n_row, n_col, first_bits, struct1, struct2, inv1, inv2, stored, pieces, *rest):
    cycle = n_col // n_row
    keeps, sends = rest[:2], rest[2:4]
    (factor,) = rest[4:]
    row_blocks = stored.shape[0]
    _, _, _, col_blocks, slab, width = pieces.shape
    packed = jnp.bfloat16 if slab % 16 == 0 else jnp.float32
    here_row, here_col = lax.axis_index("row"), lax.axis_index("col")

    group = here_col // n_row
    places = [(row ^ here_row, lax.rem(turn + group, cycle)) for turn in range(cycle) for row in range(n_row)]
    for p, (struct, inverse) in enumerate(((struct1, inv1), (struct2, inv2))):

        def look(place, found):
            return tuple(f | (struct[place] == b * n_col + here_col).astype(jnp.int32) for b, f in enumerate(found))

        found = lax.fori_loop(0, struct.shape[0], look, (jnp.int32(0),) * col_blocks)
        slices = [pieces[m, s, p, b].astype(packed) for b in range(col_blocks) for m, s in places]
        blocks = jnp.concatenate(slices, axis=0).astype(jnp.bfloat16)
        product = split_dot(blocks, inverse[...])
        for b in range(col_blocks):
            place = slice(b * width, (b + 1) * width)
            factor[place, p * width : (p + 1) * width] = jnp.where(found[b] == 1, product[place], 0.0).astype(jnp.bfloat16)

    half = row_blocks // 2
    for a in range(row_blocks):
        wide = jnp.concatenate([stored[a, b] for b in range(col_blocks)], axis=1)
        group, place = divmod(a, half)
        bit = first_bits[group]
        upper = ((here_col >> bit) & 1) == 1
        for p in range(2):
            total = jnp.dot(wide, factor[:, p * width : (p + 1) * width], preferred_element_type=jnp.float32)
            for j in range(n_col // 2):
                low = ((j >> bit) << (bit + 1)) | (j & ((1 << bit) - 1))
                high = low | (1 << bit)
                x = total[low * slab : (low + 1) * slab]
                y = total[high * slab : (high + 1) * slab]
                keeps[group][j, p, place] = jnp.where(upper, y, x)
                sends[group][j, p, place] = jnp.where(upper, x, y).astype(jnp.bfloat16)


def prepare_kernel(link, inv1, inv2, after, linked, out, whole):
    slab = out.shape[1]
    linked[...] = exact_dot(link[...].astype(jnp.float32), inv2[...])
    link = linked[...]
    gram1 = exact_dot(inv1[...], inv1[...], 0)
    across = exact_dot(gram1, link)
    whole[0] = gram1
    whole[1] = -across
    whole[2] = exact_dot(inv2[...], inv2[...], 0) + exact_dot(link, across, 0)
    place = pl.ds(pl.multiple_of(lax.axis_index("col") * slab, slab), slab)
    out[...] = whole[:, place, :]


def form_kernel(n_row, struct1, struct2, inv1, inv2, base, rows):
    slices, _, blocks, slab, width = base.shape
    for p, (struct, inverse) in enumerate(((struct1, inv1), (struct2, inv2))):
        keep = listed(struct, blocks, n_row)
        flat = base[:, p].astype(jnp.float32).reshape(slices * blocks * slab, width).astype(jnp.bfloat16)
        product = split_dot(flat, inverse[...]).reshape(slices, blocks, slab, width)
        rows[:, p] = jnp.where(keep[None], product, 0.0).astype(jnp.bfloat16)


def sum_kernel(last_bit, rows, total_low, total_high, linked, after, out):
    _, _, half, slab, width = total_low.shape
    mine = (lax.axis_index("col") >> last_bit) & 1

    def gathered(p):
        parts = [total[place, p].reshape(half * slab, width) for place in (mine, 1 - mine) for total in (total_low, total_high)]
        return jnp.concatenate(parts, axis=0)

    def factor(p):
        return rows[:, p].astype(jnp.float32).reshape(-1, width).astype(jnp.bfloat16)

    link = linked[...]
    sum1 = gathered(0)
    u2 = factor(1)
    first = split_dot(factor(0), sum1, 0)
    cross = split_dot(u2, sum1, 0)
    top = cross.T - split_dot(first, link)
    second = split_dot(u2, gathered(1), 0) - split_dot(cross, link) - split_dot(link, top, 0)
    across = width // 2
    for i, part in enumerate((first, top, second)):
        part = part.reshape(width // slab, slab, width)
        for h in range(2):
            out[h, :, i] = part[:, :, h * across : (h + 1) * across]


def column_kernel(n_row, struct1, struct2, kept_low, came_low, kept_high, came_high, linked, column1, column2):
    blocks, slab, width = column1.shape
    sums = []
    for p in range(2):
        parts = [k[p] + c[p].astype(jnp.float32) for k, c in ((kept_low, came_low), (kept_high, came_high))]
        sums.append(jnp.concatenate(parts, axis=0))
    col1 = jnp.where(listed(struct1, blocks, n_row), -sums[0], 0.0)
    column1[...] = col1
    carried = split_dot(col1.reshape(blocks * slab, width), linked[...]).reshape(col1.shape)
    column2[...] = jnp.where(listed(struct2, blocks, n_row), -(sums[1] + carried), 0.0)


def swapped(value, axis, size, mask):
    return lax.ppermute(value, axis, [(i, i ^ mask) for i in range(size)])


def halves(value, axis, ways):
    kept, sent = (lax.dynamic_index_in_dim(value, way, axis, keepdims=False) for way in ways)
    return kept, sent


def body(stored_inverse, panel_first, panel_second, panel_link, inv_first, inv_second, struct_first, struct_second):
    n_row, n_col = lax.axis_size("row"), lax.axis_size("col")
    here_col = lax.axis_index("col")
    row_blocks, _, col_blocks, _, width, _ = stored_inverse.shape
    slab = width // n_col
    cycle = n_col // n_row
    n_bits = n_col.bit_length() - 1
    f32, bf16 = jnp.float32, jnp.bfloat16
    shape = jax.ShapeDtypeStruct
    big = pltpu.CompilerParams(vmem_limit_bytes=12 * 1024 * 1024)
    stored = stored_inverse.reshape(row_blocks, col_blocks, width, width)
    panel = (row_blocks, slab, width)

    panels = [panel_first.reshape(panel), panel_second.reshape(panel)]
    _, turn = place_of(here_col, n_row)
    picks = [((s - turn + cycle) % cycle).astype(jnp.uint32) for s in range(cycle)]
    ways = [(here_col >> bit) & 1 for bit in range(n_bits)]
    ways = [(way.astype(jnp.uint32), (1 - way).astype(jnp.uint32)) for way in ways]
    core = lax.axis_index("row") & 1
    cores = (core.astype(jnp.uint32), (1 - core).astype(jnp.uint32))
    quads = [(here_col & 3) ^ m for m in range(4)]
    quads = [quad.astype(jnp.uint32) for quad in quads]
    panels, picks, ways, cores, quads = lax.optimization_barrier((panels, picks, ways, cores, quads))

    raw = lax.optimization_barrier(jnp.stack(panels))
    turns = raw.reshape(2, col_blocks, cycle, slab, width)
    got = []
    for s in range(cycle):
        moves = []
        for r in range(n_row):
            for c in range(n_col):
                row, t = place_of(c, n_row)
                moves.append((r * n_col + c, row * n_col + r + (s - t) % cycle * n_row))
        part = lax.dynamic_index_in_dim(turns, picks[s], 2, keepdims=False)
        got.append(lax.ppermute(part, ("row", "col"), moves))
    base = jnp.stack([raw, swapped(raw, "col", n_col, n_col // 2)])

    pieces = {0: got}
    bit = n_row // 2
    while bit > 1:
        for m, parts in list(pieces.items()):
            pieces[m ^ bit] = [swapped(part, "row", n_row, bit) for part in parts]
        bit //= 2
    pieces = jnp.stack([jnp.stack(pieces[m]) for m in sorted(pieces)])
    pieces, base = lax.optimization_barrier((pieces, base))
    rows = pl.pallas_call(
        functools.partial(form_kernel, n_row),
        out_shape=shape(base.shape, bf16),
        in_specs=[SMEM, SMEM] + [VMEM] * 3,
        out_specs=VMEM,
        compiler_params=big,
        name="form",
        cost_estimate=pl.CostEstimate(flops=8 * width**3, bytes_accessed=4 * width**2, transcendentals=0),
    )(struct_first, struct_second, inv_first, inv_second, base)
    beside, rows = lax.optimization_barrier((swapped(pieces, "row", n_row, 1), rows))
    pieces = jnp.stack([pieces, beside], axis=1).reshape((n_row,) + pieces.shape[1:])

    orders = (list(range(n_bits)), [1, 0] + list(range(2, n_bits)))
    half = row_blocks // 2
    block = (2, half, slab, width)
    kept = (n_col // 2,) + block
    split = pl.pallas_call(
        functools.partial(product_kernel, n_row, n_col, (orders[0][0], orders[1][0])),
        out_shape=[shape(kept, f32)] * 2 + [shape(kept, bf16)] * 2,
        in_specs=[SMEM, SMEM] + [VMEM] * 4,
        out_specs=[VMEM] * 4,
        scratch_shapes=[
            pltpu.VMEM((col_blocks * width, 2 * width), bf16),
        ],
        compiler_params=big,
        name="products",
    )(struct_first, struct_second, inv_first, inv_second, stored, pieces)

    linked, consts = pl.pallas_call(
        prepare_kernel,
        out_shape=[shape((width, width), f32), shape((3, slab, width), f32)],
        in_specs=[VMEM] * 3 + [ANY],
        out_specs=[VMEM] * 2,
        scratch_shapes=[pltpu.VMEM((3, width, width), f32)],
        compiler_params=big,
        name="prepare",
        cost_estimate=pl.CostEstimate(flops=6 * 10 * width**3, bytes_accessed=8 * width**2, transcendentals=0),
    )(panel_link, inv_first, inv_second, split[0])

    state = [(split[g], swapped(split[2 + g], "col", n_col, 1 << orders[g][0])) for g in range(2)]
    left = [sorted(set(range(n_bits)) - {order[0]}) for order in orders]
    for i in range(1, n_bits):
        totals, last = [], []
        for g in range(2):
            keep, came = state[g]
            bit = orders[g][i]
            inner = 1 << left[g].index(bit)
            left[g].remove(bit)
            totals.append(keep + came.astype(f32))
            keep, send = halves(totals[g].reshape((-1, 2, inner) + block), 1, ways[bit])
            keep, send = keep.reshape((-1,) + block), send.astype(bf16).reshape((-1,) + block)
            last.append((keep, send))
        if i < n_bits - 1 and orders[0][i] != orders[1][i]:
            state = [(keep, swapped(send, "col", n_col, 1 << order[i])) for (keep, send), order in zip(last, orders)]
        else:
            came = swapped(jnp.stack([send for _, send in last]), "col", n_col, 1 << orders[0][i])
            state = [(keep, came[g]) for g, (keep, _) in enumerate(last)]

    sums = pl.pallas_call(
        functools.partial(sum_kernel, n_bits - 1),
        out_shape=shape((2, n_col, 3, slab, width // 2), f32),
        in_specs=[VMEM] * 4 + [ANY],
        out_specs=VMEM,
        compiler_params=big,
        name="sums",
    )(rows, *totals, linked, consts)
    keep, send = halves(sums, 0, cores)
    sums = keep + swapped(send, "row", n_row, 1)
    tail = (3, slab, width // 2)
    parts = [lax.dynamic_index_in_dim(sums.reshape((-1, 4) + tail), quad, 1, keepdims=False) for quad in quads]
    sums = parts[0]
    for m in range(1, 4):
        sums = sums + swapped(parts[m].astype(bf16), "col", n_col, m).astype(f32)
    for bit in range(2, n_bits - 1):
        keep, send = halves(sums.reshape((-1, 2) + tail), 1, ways[bit])
        sums = keep + swapped(send.astype(bf16), "col", n_col, 1 << bit).astype(f32)
    keep, send = (part.astype(bf16) for part in halves(sums.reshape((2,) + tail), 0, ways[n_bits - 1]))
    across = [(r * n_col + c, (r ^ 2) * n_col + (c ^ (n_col // 2))) for r in range(n_row) for c in range(n_col)]
    near = keep.astype(f32) + swapped(send, "col", n_col, n_col // 2).astype(f32)
    far = swapped(keep, "row", n_row, 2).astype(f32) + lax.ppermute(send, ("row", "col"), across).astype(f32)
    mine = near + far
    for bit in range(2, n_row.bit_length() - 1):
        mine = mine + swapped(mine, "row", n_row, 1 << bit)

    mine, state = lax.optimization_barrier((mine, state))
    column_first, column_second = pl.pallas_call(
        functools.partial(column_kernel, n_row),
        out_shape=[shape(panel, f32)] * 2,
        in_specs=[SMEM, SMEM] + [VMEM] * 5,
        out_specs=[VMEM] * 2,
        compiler_params=big,
        name="columns",
    )(struct_first, struct_second, *[part[0] for pair in state for part in pair], linked)

    pair = jnp.stack([mine, swapped(mine, "row", n_row, 1)])
    total = jnp.concatenate([lax.dynamic_index_in_dim(pair, way, 0, keepdims=False) for way in cores], axis=-1)
    diag_first, link_block, diag_second = consts + total
    out = (row_blocks, 1, slab, width)
    return column_first.reshape(out), column_second.reshape(out), diag_first, link_block, diag_second


def solution(mesh):
    placed = (
        P(None, "row", None, "col", None, None),
        P(None, "row", "col", None),
        P(None, "row", "col", None),
        P(),
        P(),
        P(),
        P(),
        P(),
    )
    return jax.shard_map(
        body,
        mesh=mesh,
        in_specs=placed,
        out_specs=(
            P(None, "row", "col", None),
            P(None, "row", "col", None),
            P("col", None),
            P("col", None),
            P("col", None),
        ),
        check_vma=False,
    )
```

```python
import functools

import jax
import jax.numpy as jnp
from jax import lax
from jax.experimental import pallas as pl
from jax.experimental.pallas import tpu as pltpu
from jax.sharding import PartitionSpec as P

precise = lax.Precision.HIGHEST
SMEM = pl.BlockSpec(memory_space=pltpu.SMEM)
VMEM = pl.BlockSpec(memory_space=pltpu.VMEM)
HBM = pl.BlockSpec(memory_space=pltpu.HBM)
ANY = pl.BlockSpec(memory_space=pl.ANY)


def exact_dot(left, right, left_dim=1):
    dims = (((left_dim,), (0,)), ((), ()))
    return lax.dot_general(left, right, dims, precision=precise, preferred_element_type=jnp.float32)


def split_dot(left, right, left_dim=1):
    def halves(value):
        if value.dtype == jnp.bfloat16:
            return [value]
        high = value.astype(jnp.bfloat16)
        return [high, (value - high.astype(jnp.float32)).astype(jnp.bfloat16)]

    dims = (((left_dim,), (0,)), ((), ()))
    total = None
    for i, a in enumerate(halves(left)):
        for j, b in enumerate(halves(right)):
            if i + j < 2:
                term = lax.dot_general(a, b, dims, preferred_element_type=jnp.float32)
                total = term if total is None else total + term
    return total


def listed(struct_ref, blocks, n_row):
    ids = lax.broadcasted_iota(jnp.int32, (blocks, 1, 1), 0) * n_row + lax.axis_index("row")

    def look(place, found):
        return jnp.where(ids == struct_ref[place], 1, found)

    found = lax.fori_loop(0, struct_ref.shape[0], look, jnp.zeros((blocks, 1, 1), jnp.int32))
    return found == 1


def place_of(piece, n_row):
    return piece % n_row, piece // n_row


def product_kernel(n_row, n_col, first_bits, struct1, struct2, inv1, inv2, stored, pieces, *rest):
    cycle = n_col // n_row
    keeps, sends = rest[:2], rest[2:4]
    (factor,) = rest[4:]
    row_blocks = stored.shape[0]
    _, _, _, col_blocks, slab, width = pieces.shape
    packed = jnp.bfloat16 if slab % 16 == 0 else jnp.float32
    here_row, here_col = lax.axis_index("row"), lax.axis_index("col")

    group = here_col // n_row
    places = [(row ^ here_row, lax.rem(turn + group + cycle - 1, cycle)) for turn in range(cycle) for row in range(n_row)]
    for p, (struct, inverse) in enumerate(((struct1, inv1), (struct2, inv2))):

        def look(place, found):
            return tuple(f | (struct[place] == b * n_col + here_col).astype(jnp.int32) for b, f in enumerate(found))

        found = lax.fori_loop(0, struct.shape[0], look, (jnp.int32(0),) * col_blocks)
        slices = [pieces[m, s, p, b].astype(packed) for b in range(col_blocks) for m, s in places]
        blocks = jnp.concatenate(slices, axis=0).astype(jnp.bfloat16)
        product = split_dot(blocks, inverse[...])
        for b in range(col_blocks):
            place = slice(b * width, (b + 1) * width)
            factor[place, p * width : (p + 1) * width] = jnp.where(found[b] == 1, product[place], 0.0).astype(jnp.bfloat16)

    half = row_blocks // 2
    step = 2 if row_blocks % 2 == 0 else 1
    for a in range(0, row_blocks, step):
        wide = [jnp.concatenate([stored[a + i, b] for b in range(col_blocks)], axis=1) for i in range(step)]
        totals = jnp.dot(jnp.concatenate(wide, axis=0), factor[...], preferred_element_type=jnp.float32)
        for i in range(step):
            total = totals[i * width : (i + 1) * width]
            group, place = divmod(a + i, half)
            bit = first_bits[group]
            upper = ((here_col >> bit) & 1) == 1
            for p in range(2):
                for j in range(n_col // 2):
                    low = ((j >> bit) << (bit + 1)) | (j & ((1 << bit) - 1))
                    high = low | (1 << bit)
                    x = total[low * slab : (low + 1) * slab, p * width : (p + 1) * width]
                    y = total[high * slab : (high + 1) * slab, p * width : (p + 1) * width]
                    keeps[group][j, p, place] = jnp.where(upper, y, x)
                    sends[group][j, p, place] = jnp.where(upper, x, y).astype(jnp.bfloat16)


def prepare_kernel(link, inv1, inv2, after, linked, out, whole):
    slab = out.shape[1]
    linked[...] = exact_dot(link[...].astype(jnp.float32), inv2[...])
    link = linked[...]
    gram1 = exact_dot(inv1[...], inv1[...], 0)
    across = exact_dot(gram1, link)
    whole[0] = gram1
    whole[1] = -across
    whole[2] = exact_dot(inv2[...], inv2[...], 0) + exact_dot(link, across, 0)
    place = pl.ds(pl.multiple_of(lax.axis_index("col") * slab, slab), slab)
    out[...] = whole[:, place, :]


def form_kernel(n_row, struct1, struct2, inv1, inv2, base, rows):
    slices, _, blocks, slab, width = base.shape
    for p, (struct, inverse) in enumerate(((struct1, inv1), (struct2, inv2))):
        keep = listed(struct, blocks, n_row)
        flat = base[:, p].astype(jnp.float32).reshape(slices * blocks * slab, width).astype(jnp.bfloat16)
        product = split_dot(flat, inverse[...]).reshape(slices, blocks, slab, width)
        rows[:, p] = jnp.where(keep[None], product, 0.0).astype(jnp.bfloat16)


def sum_kernel(last_bit, rows, total_low, total_high, linked, after, out):
    _, _, half, slab, width = total_low.shape
    mine = (lax.axis_index("col") >> last_bit) & 1

    def gathered(p):
        parts = [total[place, p].reshape(half * slab, width) for place in (mine, 1 - mine) for total in (total_low, total_high)]
        return jnp.concatenate(parts, axis=0)

    def factor(p):
        return rows[:, p].astype(jnp.float32).reshape(-1, width).astype(jnp.bfloat16)

    link = linked[...]
    sum1 = gathered(0)
    u2 = factor(1)
    first = split_dot(factor(0), sum1, 0)
    cross = split_dot(u2, sum1, 0)
    top = cross.T - split_dot(first, link)
    second = split_dot(u2, gathered(1), 0) - split_dot(cross, link) - split_dot(link, top, 0)
    across = width // 2
    for i, part in enumerate((first, top, second)):
        part = part.reshape(width // slab, slab, width)
        for h in range(2):
            out[h, :, i] = part[:, :, h * across : (h + 1) * across]


def column_kernel(n_row, struct1, struct2, kept_low, came_low, kept_high, came_high, linked, column1, column2):
    blocks, slab, width = column1.shape
    sums = []
    for p in range(2):
        parts = [k[p] + c[p].astype(jnp.float32) for k, c in ((kept_low, came_low), (kept_high, came_high))]
        sums.append(jnp.concatenate(parts, axis=0))
    col1 = jnp.where(listed(struct1, blocks, n_row), -sums[0], 0.0)
    column1[...] = col1
    carried = split_dot(col1.reshape(blocks * slab, width), linked[...]).reshape(col1.shape)
    column2[...] = jnp.where(listed(struct2, blocks, n_row), -(sums[1] + carried), 0.0)


def swapped(value, axis, size, mask):
    return lax.ppermute(value, axis, [(i, i ^ mask) for i in range(size)])


def halves(value, axis, ways):
    kept, sent = (lax.dynamic_index_in_dim(value, way, axis, keepdims=False) for way in ways)
    return kept, sent


def body(stored_inverse, panel_first, panel_second, panel_link, inv_first, inv_second, struct_first, struct_second):
    n_row, n_col = lax.axis_size("row"), lax.axis_size("col")
    here_col = lax.axis_index("col")
    row_blocks, _, col_blocks, _, width, _ = stored_inverse.shape
    slab = width // n_col
    cycle = n_col // n_row
    n_bits = n_col.bit_length() - 1
    f32, bf16 = jnp.float32, jnp.bfloat16
    shape = jax.ShapeDtypeStruct
    big = pltpu.CompilerParams(vmem_limit_bytes=12 * 1024 * 1024)
    stored = stored_inverse.reshape(row_blocks, col_blocks, width, width)
    panel = (row_blocks, slab, width)

    panels = [panel_first.reshape(panel), panel_second.reshape(panel)]
    _, turn = place_of(here_col, n_row)
    picks = [((s + 1 - turn + cycle) % cycle).astype(jnp.uint32) for s in range(cycle)]
    ways = [(here_col >> bit) & 1 for bit in range(n_bits)]
    ways = [(way.astype(jnp.uint32), (1 - way).astype(jnp.uint32)) for way in ways]
    core = lax.axis_index("row") & 1
    cores = (core.astype(jnp.uint32), (1 - core).astype(jnp.uint32))
    quads = [(here_col & 3) ^ m for m in range(4)]
    quads = [quad.astype(jnp.uint32) for quad in quads]
    panels, picks, ways, cores, quads = lax.optimization_barrier((panels, picks, ways, cores, quads))

    raw = lax.optimization_barrier(jnp.stack(panels))
    turns = raw.reshape(2, col_blocks, cycle, slab, width)
    got = []
    for s in range(cycle):
        moves = []
        for r in range(n_row):
            for c in range(n_col):
                row, t = place_of(c, n_row)
                moves.append((r * n_col + c, row * n_col + r + (s + 1 - t) % cycle * n_row))
        part = lax.dynamic_index_in_dim(turns, picks[s], 2, keepdims=False)
        got.append(lax.ppermute(part, ("row", "col"), moves))
    base = jnp.stack([raw, swapped(raw, "col", n_col, n_col // 2)])

    pieces = {0: got}
    bit = n_row // 2
    while bit > 1:
        for m, parts in list(pieces.items()):
            pieces[m ^ bit] = [swapped(part, "row", n_row, bit) for part in parts]
        bit //= 2
    pieces = jnp.stack([jnp.stack(pieces[m]) for m in sorted(pieces)])
    pieces, base = lax.optimization_barrier((pieces, base))
    rows = pl.pallas_call(
        functools.partial(form_kernel, n_row),
        out_shape=shape(base.shape, bf16),
        in_specs=[SMEM, SMEM] + [VMEM] * 3,
        out_specs=VMEM,
        compiler_params=big,
        name="form",
        cost_estimate=pl.CostEstimate(flops=8 * width**3, bytes_accessed=4 * width**2, transcendentals=0),
    )(struct_first, struct_second, inv_first, inv_second, base)
    beside, rows = lax.optimization_barrier((swapped(pieces, "row", n_row, 1), rows))
    pieces = jnp.stack([pieces, beside], axis=1).reshape((n_row,) + pieces.shape[1:])

    orders = (list(range(n_bits)), [1, 0] + list(range(2, n_bits)))
    half = row_blocks // 2
    block = (2, half, slab, width)
    kept = (n_col // 2,) + block
    split = pl.pallas_call(
        functools.partial(product_kernel, n_row, n_col, (orders[0][0], orders[1][0])),
        out_shape=[shape(kept, f32)] * 2 + [shape(kept, bf16)] * 2,
        in_specs=[SMEM, SMEM] + [VMEM] * 4,
        out_specs=[VMEM] * 4,
        scratch_shapes=[
            pltpu.VMEM((col_blocks * width, 2 * width), bf16),
        ],
        compiler_params=big,
        name="products",
    )(struct_first, struct_second, inv_first, inv_second, stored, pieces)

    linked, consts = pl.pallas_call(
        prepare_kernel,
        out_shape=[shape((width, width), f32), shape((3, slab, width), f32)],
        in_specs=[VMEM] * 3 + [ANY],
        out_specs=[VMEM] * 2,
        scratch_shapes=[pltpu.VMEM((3, width, width), f32)],
        compiler_params=big,
        name="prepare",
        cost_estimate=pl.CostEstimate(flops=6 * 10 * width**3, bytes_accessed=8 * width**2, transcendentals=0),
    )(panel_link, inv_first, inv_second, split[0])

    state = [(split[g], swapped(split[2 + g], "col", n_col, 1 << orders[g][0])) for g in range(2)]
    left = [sorted(set(range(n_bits)) - {order[0]}) for order in orders]
    for i in range(1, n_bits):
        totals, last = [], []
        for g in range(2):
            keep, came = state[g]
            bit = orders[g][i]
            inner = 1 << left[g].index(bit)
            left[g].remove(bit)
            totals.append(keep + came.astype(f32))
            keep, send = halves(totals[g].reshape((-1, 2, inner) + block), 1, ways[bit])
            keep, send = keep.reshape((-1,) + block), send.astype(bf16).reshape((-1,) + block)
            last.append((keep, send))
        if i < n_bits - 1 and orders[0][i] != orders[1][i]:
            state = [(keep, swapped(send, "col", n_col, 1 << order[i])) for (keep, send), order in zip(last, orders)]
        else:
            came = swapped(jnp.stack([send for _, send in last]), "col", n_col, 1 << orders[0][i])
            state = [(keep, came[g]) for g, (keep, _) in enumerate(last)]

    sums = pl.pallas_call(
        functools.partial(sum_kernel, n_bits - 1),
        out_shape=shape((2, n_col, 3, slab, width // 2), f32),
        in_specs=[VMEM] * 4 + [ANY],
        out_specs=VMEM,
        compiler_params=big,
        name="sums",
    )(rows, *totals, linked, consts)
    keep, send = halves(sums, 0, cores)
    sums = keep + swapped(send, "row", n_row, 1)
    tail = (3, slab, width // 2)
    parts = [lax.dynamic_index_in_dim(sums.reshape((-1, 4) + tail), quad, 1, keepdims=False) for quad in quads]
    sums = parts[0]
    for m in range(1, 4):
        sums = sums + swapped(parts[m].astype(bf16), "col", n_col, m).astype(f32)
    for bit in range(2, n_bits - 1):
        keep, send = halves(sums.reshape((-1, 2) + tail), 1, ways[bit])
        sums = keep + swapped(send.astype(bf16), "col", n_col, 1 << bit).astype(f32)
    keep, send = (part.astype(bf16) for part in halves(sums.reshape((2,) + tail), 0, ways[n_bits - 1]))
    across = [(r * n_col + c, (r ^ 2) * n_col + (c ^ (n_col // 2))) for r in range(n_row) for c in range(n_col)]
    near = keep.astype(f32) + swapped(send, "col", n_col, n_col // 2).astype(f32)
    far = swapped(keep, "row", n_row, 2).astype(f32) + lax.ppermute(send, ("row", "col"), across).astype(f32)
    mine = near + far
    for bit in range(2, n_row.bit_length() - 1):
        mine = mine + swapped(mine, "row", n_row, 1 << bit)

    mine, state = lax.optimization_barrier((mine, state))
    column_first, column_second = pl.pallas_call(
        functools.partial(column_kernel, n_row),
        out_shape=[shape(panel, f32)] * 2,
        in_specs=[SMEM, SMEM] + [VMEM] * 5,
        out_specs=[VMEM] * 2,
        compiler_params=big,
        name="columns",
    )(struct_first, struct_second, *[part[0] for pair in state for part in pair], linked)

    pair = jnp.stack([mine, swapped(mine, "row", n_row, 1)])
    total = jnp.concatenate([lax.dynamic_index_in_dim(pair, way, 0, keepdims=False) for way in cores], axis=-1)
    diag_first, link_block, diag_second = consts + total
    out = (row_blocks, 1, slab, width)
    return column_first.reshape(out), column_second.reshape(out), diag_first, link_block, diag_second


def solution(mesh):
    placed = (
        P(None, "row", None, "col", None, None),
        P(None, "row", "col", None),
        P(None, "row", "col", None),
        P(),
        P(),
        P(),
        P(),
        P(),
    )
    return jax.shard_map(
        body,
        mesh=mesh,
        in_specs=placed,
        out_specs=(
            P(None, "row", "col", None),
            P(None, "row", "col", None),
            P("col", None),
            P("col", None),
            P("col", None),
        ),
        check_vma=False,
    )
```

```python
import functools

import jax
import jax.numpy as jnp
from jax import lax
from jax.experimental import pallas as pl
from jax.experimental.pallas import tpu as pltpu
from jax.sharding import PartitionSpec as P

precise = lax.Precision.HIGHEST
SMEM = pl.BlockSpec(memory_space=pltpu.SMEM)
VMEM = pl.BlockSpec(memory_space=pltpu.VMEM)
HBM = pl.BlockSpec(memory_space=pltpu.HBM)
ANY = pl.BlockSpec(memory_space=pl.ANY)


def exact_dot(left, right, left_dim=1):
    dims = (((left_dim,), (0,)), ((), ()))
    return lax.dot_general(left, right, dims, precision=precise, preferred_element_type=jnp.float32)


def split_dot(left, right, left_dim=1):
    def halves(value):
        if value.dtype == jnp.bfloat16:
            return [value]
        high = value.astype(jnp.bfloat16)
        return [high, (value - high.astype(jnp.float32)).astype(jnp.bfloat16)]

    dims = (((left_dim,), (0,)), ((), ()))
    total = None
    for i, a in enumerate(halves(left)):
        for j, b in enumerate(halves(right)):
            if i + j < 2:
                term = lax.dot_general(a, b, dims, preferred_element_type=jnp.float32)
                total = term if total is None else total + term
    return total


def listed(struct_ref, blocks, n_row):
    ids = lax.broadcasted_iota(jnp.int32, (blocks, 1, 1), 0) * n_row + lax.axis_index("row")

    def look(place, found):
        return jnp.where(ids == struct_ref[place], 1, found)

    found = lax.fori_loop(0, struct_ref.shape[0], look, jnp.zeros((blocks, 1, 1), jnp.int32))
    return found == 1


def place_of(piece, n_row):
    return piece % n_row, piece // n_row


def product_kernel(n_row, n_col, first_bits, struct1, struct2, inv1, inv2, stored, pieces, *rest):
    cycle = n_col // n_row
    keeps, sends = rest[:2], rest[2:4]
    (factor,) = rest[4:]
    row_blocks = stored.shape[0]
    _, _, _, col_blocks, slab, width = pieces.shape
    packed = jnp.bfloat16 if slab % 16 == 0 else jnp.float32
    here_row, here_col = lax.axis_index("row"), lax.axis_index("col")

    group = here_col // n_row
    places = [(row ^ here_row, lax.rem(turn + group + cycle - 1, cycle)) for turn in range(cycle) for row in range(n_row)]
    for p, (struct, inverse) in enumerate(((struct1, inv1), (struct2, inv2))):

        def look(place, found):
            return tuple(f | (struct[place] == b * n_col + here_col).astype(jnp.int32) for b, f in enumerate(found))

        found = lax.fori_loop(0, struct.shape[0], look, (jnp.int32(0),) * col_blocks)
        slices = [pieces[m, s, p, b].astype(packed) for b in range(col_blocks) for m, s in places]
        blocks = jnp.concatenate(slices, axis=0).astype(jnp.bfloat16)
        product = split_dot(blocks, inverse[...])
        for b in range(col_blocks):
            place = slice(b * width, (b + 1) * width)
            factor[place, p * width : (p + 1) * width] = jnp.where(found[b] == 1, product[place], 0.0).astype(jnp.bfloat16)

    half = row_blocks // 2
    step = 2 if row_blocks % 2 == 0 else 1
    for a in range(0, row_blocks, step):
        wide = [jnp.concatenate([stored[a + i, b] for b in range(col_blocks)], axis=1) for i in range(step)]
        totals = jnp.dot(jnp.concatenate(wide, axis=0), factor[...], preferred_element_type=jnp.float32)
        for i in range(step):
            total = totals[i * width : (i + 1) * width]
            group, place = divmod(a + i, half)
            bit = first_bits[group]
            upper = ((here_col >> bit) & 1) == 1
            for p in range(2):
                for j in range(n_col // 2):
                    low = ((j >> bit) << (bit + 1)) | (j & ((1 << bit) - 1))
                    high = low | (1 << bit)
                    x = total[low * slab : (low + 1) * slab, p * width : (p + 1) * width]
                    y = total[high * slab : (high + 1) * slab, p * width : (p + 1) * width]
                    keeps[group][j, p, place] = jnp.where(upper, y, x)
                    sends[group][j, p, place] = jnp.where(upper, x, y).astype(jnp.bfloat16)


def prepare_kernel(link, inv1, inv2, after, linked, out, whole):
    slab = out.shape[1]
    linked[...] = exact_dot(link[...].astype(jnp.float32), inv2[...])
    link = linked[...]
    gram1 = exact_dot(inv1[...], inv1[...], 0)
    across = exact_dot(gram1, link)
    whole[0] = gram1
    whole[1] = -across
    whole[2] = exact_dot(inv2[...], inv2[...], 0) + exact_dot(link, across, 0)
    place = pl.ds(pl.multiple_of(lax.axis_index("col") * slab, slab), slab)
    out[...] = whole[:, place, :]


def form_kernel(n_row, struct1, struct2, inv1, inv2, base, rows):
    slices, _, blocks, slab, width = base.shape
    for p, (struct, inverse) in enumerate(((struct1, inv1), (struct2, inv2))):
        keep = listed(struct, blocks, n_row)
        flat = base[:, p].astype(jnp.float32).reshape(slices * blocks * slab, width).astype(jnp.bfloat16)
        product = split_dot(flat, inverse[...]).reshape(slices, blocks, slab, width)
        rows[:, p] = jnp.where(keep[None], product, 0.0).astype(jnp.bfloat16)


def sum_kernel(last_bit, rows, total_low, total_high, linked, after, out):
    _, _, half, slab, width = total_low.shape
    mine = (lax.axis_index("col") >> last_bit) & 1

    def gathered(p):
        parts = [total[place, p].reshape(half * slab, width) for place in (mine, 1 - mine) for total in (total_low, total_high)]
        return jnp.concatenate(parts, axis=0)

    def factor(p):
        return rows[:, p].astype(jnp.float32).reshape(-1, width).astype(jnp.bfloat16)

    link = linked[...]
    sum1 = gathered(0)
    u2 = factor(1)
    first = split_dot(factor(0), sum1, 0)
    cross = split_dot(u2, sum1, 0)
    top = cross.T - split_dot(first, link)
    second = split_dot(u2, gathered(1), 0) - split_dot(cross, link) - split_dot(link, top, 0)
    across = width // 2
    for i, part in enumerate((first, top, second)):
        part = part.reshape(width // slab, slab, width)
        for h in range(2):
            out[h, :, i] = part[:, :, h * across : (h + 1) * across]


def column_kernel(n_row, struct1, struct2, kept_low, came_low, kept_high, came_high, linked, column1, column2):
    blocks, slab, width = column1.shape
    sums = []
    for p in range(2):
        parts = [k[p] + c[p].astype(jnp.float32) for k, c in ((kept_low, came_low), (kept_high, came_high))]
        sums.append(jnp.concatenate(parts, axis=0))
    col1 = jnp.where(listed(struct1, blocks, n_row), -sums[0], 0.0)
    column1[...] = col1
    carried = split_dot(col1.reshape(blocks * slab, width), linked[...]).reshape(col1.shape)
    column2[...] = jnp.where(listed(struct2, blocks, n_row), -(sums[1] + carried), 0.0)


def swapped(value, axis, size, mask):
    return lax.ppermute(value, axis, [(i, i ^ mask) for i in range(size)])


def halves(value, axis, ways):
    kept, sent = (lax.dynamic_index_in_dim(value, way, axis, keepdims=False) for way in ways)
    return kept, sent


def body(stored_inverse, panel_first, panel_second, panel_link, inv_first, inv_second, struct_first, struct_second):
    n_row, n_col = lax.axis_size("row"), lax.axis_size("col")
    here_col = lax.axis_index("col")
    row_blocks, _, col_blocks, _, width, _ = stored_inverse.shape
    slab = width // n_col
    cycle = n_col // n_row
    n_bits = n_col.bit_length() - 1
    f32, bf16 = jnp.float32, jnp.bfloat16
    shape = jax.ShapeDtypeStruct
    big = pltpu.CompilerParams(vmem_limit_bytes=12 * 1024 * 1024)
    stored = stored_inverse.reshape(row_blocks, col_blocks, width, width)
    panel = (row_blocks, slab, width)

    panels = [panel_first.reshape(panel), panel_second.reshape(panel)]
    _, turn = place_of(here_col, n_row)
    picks = [((s + 1 - turn + cycle) % cycle).astype(jnp.uint32) for s in range(cycle)]
    ways = [(here_col >> bit) & 1 for bit in range(n_bits)]
    ways = [(way.astype(jnp.uint32), (1 - way).astype(jnp.uint32)) for way in ways]
    core = lax.axis_index("row") & 1
    cores = (core.astype(jnp.uint32), (1 - core).astype(jnp.uint32))
    quads = [(here_col & 3) ^ m for m in range(4)]
    quads = [quad.astype(jnp.uint32) for quad in quads]
    panels, picks, ways, cores, quads = lax.optimization_barrier((panels, picks, ways, cores, quads))

    raw = lax.optimization_barrier(jnp.stack(panels))
    turns = raw.reshape(2, col_blocks, cycle, slab, width)
    got = []
    for s in range(cycle):
        moves = []
        for r in range(n_row):
            for c in range(n_col):
                row, t = place_of(c, n_row)
                moves.append((r * n_col + c, row * n_col + r + (s + 1 - t) % cycle * n_row))
        part = lax.dynamic_index_in_dim(turns, picks[s], 2, keepdims=False)
        got.append(lax.ppermute(part, ("row", "col"), moves))
    base = jnp.stack([raw, swapped(raw, "col", n_col, n_col // 2)])

    pieces = {0: got}
    bit = n_row // 2
    while bit > 1:
        for m, parts in list(pieces.items()):
            pieces[m ^ bit] = [swapped(part, "row", n_row, bit) for part in parts]
        bit //= 2
    pieces = jnp.stack([jnp.stack(pieces[m]) for m in sorted(pieces)])
    pieces, base = lax.optimization_barrier((pieces, base))
    rows = pl.pallas_call(
        functools.partial(form_kernel, n_row),
        out_shape=shape(base.shape, bf16),
        in_specs=[SMEM, SMEM] + [VMEM] * 3,
        out_specs=VMEM,
        compiler_params=big,
        name="form",
        cost_estimate=pl.CostEstimate(flops=8 * width**3, bytes_accessed=4 * width**2, transcendentals=0),
    )(struct_first, struct_second, inv_first, inv_second, base)
    beside, rows = lax.optimization_barrier((swapped(pieces, "row", n_row, 1), rows))
    pieces = jnp.stack([pieces, beside], axis=1).reshape((n_row,) + pieces.shape[1:])

    orders = (list(range(n_bits)), [1, 0] + list(range(2, n_bits)))
    half = row_blocks // 2
    block = (2, half, slab, width)
    kept = (n_col // 2,) + block
    split = pl.pallas_call(
        functools.partial(product_kernel, n_row, n_col, (orders[0][0], orders[1][0])),
        out_shape=[shape(kept, f32)] * 2 + [shape(kept, bf16)] * 2,
        in_specs=[SMEM, SMEM] + [VMEM] * 4,
        out_specs=[VMEM] * 4,
        scratch_shapes=[
            pltpu.VMEM((col_blocks * width, 2 * width), bf16),
        ],
        compiler_params=big,
        name="products",
    )(struct_first, struct_second, inv_first, inv_second, stored, pieces)

    linked, consts = pl.pallas_call(
        prepare_kernel,
        out_shape=[shape((width, width), f32), shape((3, slab, width), f32)],
        in_specs=[VMEM] * 3 + [ANY],
        out_specs=[VMEM] * 2,
        scratch_shapes=[pltpu.VMEM((3, width, width), f32)],
        compiler_params=big,
        name="prepare",
        cost_estimate=pl.CostEstimate(flops=6 * 10 * width**3, bytes_accessed=8 * width**2, transcendentals=0),
    )(panel_link, inv_first, inv_second, split[0])

    state = [(split[g], swapped(split[2 + g], "col", n_col, 1 << orders[g][0])) for g in range(2)]
    left = [sorted(set(range(n_bits)) - {order[0]}) for order in orders]
    for i in range(1, n_bits):
        totals, last = [], []
        for g in range(2):
            keep, came = state[g]
            bit = orders[g][i]
            inner = 1 << left[g].index(bit)
            left[g].remove(bit)
            totals.append(keep + came.astype(f32))
            keep, send = halves(totals[g].reshape((-1, 2, inner) + block), 1, ways[bit])
            keep, send = keep.reshape((-1,) + block), send.astype(bf16).reshape((-1,) + block)
            last.append((keep, send))
        if i < n_bits - 1 and orders[0][i] != orders[1][i]:
            state = [(keep, swapped(send, "col", n_col, 1 << order[i])) for (keep, send), order in zip(last, orders)]
        else:
            came = swapped(jnp.stack([send for _, send in last]), "col", n_col, 1 << orders[0][i])
            state = [(keep, came[g]) for g, (keep, _) in enumerate(last)]

    sums = pl.pallas_call(
        functools.partial(sum_kernel, n_bits - 1),
        out_shape=shape((2, n_col, 3, slab, width // 2), f32),
        in_specs=[VMEM] * 4 + [ANY],
        out_specs=VMEM,
        compiler_params=big,
        name="sums",
    )(rows, *totals, linked, consts)
    keep, send = halves(sums, 0, cores)
    sums = keep + swapped(send, "row", n_row, 1)
    tail = (3, slab, width // 2)
    parts = [lax.dynamic_index_in_dim(sums.reshape((-1, 4) + tail), quad, 1, keepdims=False) for quad in quads]
    sums = parts[0]
    for m in (3, 2, 1):
        sums = sums + swapped(parts[m].astype(bf16), "col", n_col, m).astype(f32)
    for bit in range(2, n_bits - 1):
        keep, send = halves(sums.reshape((-1, 2) + tail), 1, ways[bit])
        sums = keep + swapped(send.astype(bf16), "col", n_col, 1 << bit).astype(f32)
    keep, send = (part.astype(bf16) for part in halves(sums.reshape((2,) + tail), 0, ways[n_bits - 1]))
    across = [(r * n_col + c, (r ^ 2) * n_col + (c ^ (n_col // 2))) for r in range(n_row) for c in range(n_col)]
    far = lax.ppermute(send, ("row", "col"), across).astype(f32)
    near = keep.astype(f32) + swapped(send, "col", n_col, n_col // 2).astype(f32)
    mine = near + (swapped(keep, "row", n_row, 2).astype(f32) + far)
    for bit in range(2, n_row.bit_length() - 1):
        mine = mine + swapped(mine, "row", n_row, 1 << bit)

    mine, state = lax.optimization_barrier((mine, state))
    column_first, column_second = pl.pallas_call(
        functools.partial(column_kernel, n_row),
        out_shape=[shape(panel, f32)] * 2,
        in_specs=[SMEM, SMEM] + [VMEM] * 5,
        out_specs=[VMEM] * 2,
        compiler_params=big,
        name="columns",
    )(struct_first, struct_second, *[part[0] for pair in state for part in pair], linked)

    pair = jnp.stack([mine, swapped(mine, "row", n_row, 1)])
    total = jnp.concatenate([lax.dynamic_index_in_dim(pair, way, 0, keepdims=False) for way in cores], axis=-1)
    diag_first, link_block, diag_second = consts + total
    out = (row_blocks, 1, slab, width)
    return column_first.reshape(out), column_second.reshape(out), diag_first, link_block, diag_second


def solution(mesh):
    placed = (
        P(None, "row", None, "col", None, None),
        P(None, "row", "col", None),
        P(None, "row", "col", None),
        P(),
        P(),
        P(),
        P(),
        P(),
    )
    return jax.shard_map(
        body,
        mesh=mesh,
        in_specs=placed,
        out_specs=(
            P(None, "row", "col", None),
            P(None, "row", "col", None),
            P("col", None),
            P("col", None),
            P("col", None),
        ),
        check_vma=False,
    )
```

```python
import functools

import jax
import jax.numpy as jnp
from jax import lax
from jax.experimental import pallas as pl
from jax.experimental.pallas import tpu as pltpu
from jax.sharding import PartitionSpec as P

precise = lax.Precision.HIGHEST
SMEM = pl.BlockSpec(memory_space=pltpu.SMEM)
VMEM = pl.BlockSpec(memory_space=pltpu.VMEM)
HBM = pl.BlockSpec(memory_space=pltpu.HBM)
ANY = pl.BlockSpec(memory_space=pl.ANY)


def exact_dot(left, right, left_dim=1):
    dims = (((left_dim,), (0,)), ((), ()))
    return lax.dot_general(left, right, dims, precision=precise, preferred_element_type=jnp.float32)


def split_dot(left, right, left_dim=1):
    def halves(value):
        if value.dtype == jnp.bfloat16:
            return [value]
        high = value.astype(jnp.bfloat16)
        return [high, (value - high.astype(jnp.float32)).astype(jnp.bfloat16)]

    dims = (((left_dim,), (0,)), ((), ()))
    total = None
    for i, a in enumerate(halves(left)):
        for j, b in enumerate(halves(right)):
            if i + j < 2:
                term = lax.dot_general(a, b, dims, preferred_element_type=jnp.float32)
                total = term if total is None else total + term
    return total


def listed(struct_ref, blocks, n_row):
    ids = lax.broadcasted_iota(jnp.int32, (blocks, 1, 1), 0) * n_row + lax.axis_index("row")

    def look(place, found):
        return jnp.where(ids == struct_ref[place], 1, found)

    found = lax.fori_loop(0, struct_ref.shape[0], look, jnp.zeros((blocks, 1, 1), jnp.int32))
    return found == 1


def place_of(piece, n_row):
    return piece % n_row, piece // n_row


def product_kernel(n_row, n_col, first_bits, struct1, struct2, inv1, inv2, stored, pieces, *rest):
    cycle = n_col // n_row
    keeps, sends = rest[:2], rest[2:4]
    (factor,) = rest[4:]
    row_blocks = stored.shape[0]
    _, _, _, col_blocks, slab, width = pieces.shape
    packed = jnp.bfloat16 if slab % 16 == 0 else jnp.float32
    here_row, here_col = lax.axis_index("row"), lax.axis_index("col")

    group = here_col // n_row
    places = [(row ^ here_row, lax.rem(turn + group + cycle - 1, cycle)) for turn in range(cycle) for row in range(n_row)]
    for p, (struct, inverse) in enumerate(((struct1, inv1), (struct2, inv2))):

        def look(place, found):
            return tuple(f | (struct[place] == b * n_col + here_col).astype(jnp.int32) for b, f in enumerate(found))

        found = lax.fori_loop(0, struct.shape[0], look, (jnp.int32(0),) * col_blocks)
        slices = [pieces[m, s, p, b].astype(packed) for b in range(col_blocks) for m, s in places]
        blocks = jnp.concatenate(slices, axis=0).astype(jnp.bfloat16)
        product = split_dot(blocks, inverse[...])
        for b in range(col_blocks):
            place = slice(b * width, (b + 1) * width)
            factor[place, p * width : (p + 1) * width] = jnp.where(found[b] == 1, product[place], 0.0).astype(jnp.bfloat16)

    half = row_blocks // 2
    step = 2 if row_blocks % 2 == 0 else 1
    for a in range(0, row_blocks, step):
        wide = [jnp.concatenate([stored[a + i, b] for b in range(col_blocks)], axis=1) for i in range(step)]
        totals = jnp.dot(jnp.concatenate(wide, axis=0), factor[...], preferred_element_type=jnp.float32)
        for i in range(step):
            total = totals[i * width : (i + 1) * width]
            group, place = divmod(a + i, half)
            bit = first_bits[group]
            upper = ((here_col >> bit) & 1) == 1
            for p in range(2):
                for j in range(n_col // 2):
                    low = ((j >> bit) << (bit + 1)) | (j & ((1 << bit) - 1))
                    high = low | (1 << bit)
                    x = total[low * slab : (low + 1) * slab, p * width : (p + 1) * width]
                    y = total[high * slab : (high + 1) * slab, p * width : (p + 1) * width]
                    keeps[group][j, p, place] = jnp.where(upper, y, x)
                    sends[group][j, p, place] = jnp.where(upper, x, y).astype(jnp.bfloat16)


def prepare_kernel(link, inv1, inv2, after, linked, out, whole):
    slab = out.shape[1]
    linked[...] = exact_dot(link[...].astype(jnp.float32), inv2[...])
    link = linked[...]
    gram1 = exact_dot(inv1[...], inv1[...], 0)
    across = exact_dot(gram1, link)
    whole[0] = gram1
    whole[1] = -across
    whole[2] = exact_dot(inv2[...], inv2[...], 0) + exact_dot(link, across, 0)
    place = pl.ds(pl.multiple_of(lax.axis_index("col") * slab, slab), slab)
    out[...] = whole[:, place, :]


def form_kernel(n_row, struct1, struct2, inv1, inv2, base, rows):
    slices, _, blocks, slab, width = base.shape
    for p, (struct, inverse) in enumerate(((struct1, inv1), (struct2, inv2))):
        keep = listed(struct, blocks, n_row)
        flat = base[:, p].astype(jnp.float32).reshape(slices * blocks * slab, width).astype(jnp.bfloat16)
        product = split_dot(flat, inverse[...]).reshape(slices, blocks, slab, width)
        rows[:, p] = jnp.where(keep[None], product, 0.0).astype(jnp.bfloat16)


def sum_kernel(last_bit, rows, total_low, total_high, linked, after, out):
    _, _, half, slab, width = total_low.shape
    mine = (lax.axis_index("col") >> last_bit) & 1

    def gathered(p):
        parts = [total[place, p].reshape(half * slab, width) for place in (mine, 1 - mine) for total in (total_low, total_high)]
        return jnp.concatenate(parts, axis=0)

    def factor(p):
        return rows[:, p].astype(jnp.float32).reshape(-1, width).astype(jnp.bfloat16)

    link = linked[...]
    sum1 = gathered(0)
    u2 = factor(1)
    first = split_dot(factor(0), sum1, 0)
    cross = split_dot(u2, sum1, 0)
    top = cross.T - split_dot(first, link)
    second = split_dot(u2, gathered(1), 0) - split_dot(cross, link) - split_dot(link, top, 0)
    across = width // 2
    for i, part in enumerate((first, top, second)):
        part = part.reshape(width // slab, slab, width)
        for h in range(2):
            out[h, :, i] = part[:, :, h * across : (h + 1) * across]


def column_kernel(n_row, struct1, struct2, kept_low, came_low, kept_high, came_high, linked, column1, column2):
    blocks, slab, width = column1.shape
    sums = []
    for p in range(2):
        parts = [k[p] + c[p].astype(jnp.float32) for k, c in ((kept_low, came_low), (kept_high, came_high))]
        sums.append(jnp.concatenate(parts, axis=0))
    col1 = jnp.where(listed(struct1, blocks, n_row), -sums[0], 0.0)
    column1[...] = col1
    carried = split_dot(col1.reshape(blocks * slab, width), linked[...]).reshape(col1.shape)
    column2[...] = jnp.where(listed(struct2, blocks, n_row), -(sums[1] + carried), 0.0)


def swapped(value, axis, size, mask):
    return lax.ppermute(value, axis, [(i, i ^ mask) for i in range(size)])


def halves(value, axis, ways):
    kept, sent = (lax.dynamic_index_in_dim(value, way, axis, keepdims=False) for way in ways)
    return kept, sent


def body(stored_inverse, panel_first, panel_second, panel_link, inv_first, inv_second, struct_first, struct_second):
    n_row, n_col = lax.axis_size("row"), lax.axis_size("col")
    here_col = lax.axis_index("col")
    row_blocks, _, col_blocks, _, width, _ = stored_inverse.shape
    slab = width // n_col
    cycle = n_col // n_row
    n_bits = n_col.bit_length() - 1
    f32, bf16 = jnp.float32, jnp.bfloat16
    shape = jax.ShapeDtypeStruct
    big = pltpu.CompilerParams(vmem_limit_bytes=12 * 1024 * 1024)
    stored = stored_inverse.reshape(row_blocks, col_blocks, width, width)
    panel = (row_blocks, slab, width)

    panels = [panel_first.reshape(panel), panel_second.reshape(panel)]
    _, turn = place_of(here_col, n_row)
    picks = [((s + 1 - turn + cycle) % cycle).astype(jnp.uint32) for s in range(cycle)]
    ways = [(here_col >> bit) & 1 for bit in range(n_bits)]
    ways = [(way.astype(jnp.uint32), (1 - way).astype(jnp.uint32)) for way in ways]
    core = lax.axis_index("row") & 1
    cores = (core.astype(jnp.uint32), (1 - core).astype(jnp.uint32))
    quads = [(here_col & 3) ^ m for m in range(4)]
    quads = [quad.astype(jnp.uint32) for quad in quads]
    panels, picks, ways, cores, quads = lax.optimization_barrier((panels, picks, ways, cores, quads))

    raw = lax.optimization_barrier(jnp.stack(panels))
    turns = raw.reshape(2, col_blocks, cycle, slab, width)
    got = []
    for s in range(cycle):
        moves = []
        for r in range(n_row):
            for c in range(n_col):
                row, t = place_of(c, n_row)
                moves.append((r * n_col + c, row * n_col + r + (s + 1 - t) % cycle * n_row))
        part = lax.dynamic_index_in_dim(turns, picks[s], 2, keepdims=False)
        got.append(lax.ppermute(part, ("row", "col"), moves))
    base = jnp.stack([raw, swapped(raw, "col", n_col, n_col // 2)])

    pieces = {0: got}
    bit = n_row // 2
    while bit > 1:
        for m, parts in list(pieces.items()):
            pieces[m ^ bit] = [swapped(part, "row", n_row, bit) for part in parts]
        bit //= 2
    pieces = jnp.stack([jnp.stack(pieces[m]) for m in sorted(pieces)])
    pieces, base = lax.optimization_barrier((pieces, base))
    rows = pl.pallas_call(
        functools.partial(form_kernel, n_row),
        out_shape=shape(base.shape, bf16),
        in_specs=[SMEM, SMEM] + [VMEM] * 3,
        out_specs=VMEM,
        compiler_params=big,
        name="form",
        cost_estimate=pl.CostEstimate(flops=8 * width**3, bytes_accessed=4 * width**2, transcendentals=0),
    )(struct_first, struct_second, inv_first, inv_second, base)
    beside, rows = lax.optimization_barrier((swapped(pieces, "row", n_row, 1), rows))
    pieces = jnp.stack([pieces, beside], axis=1).reshape((n_row,) + pieces.shape[1:])

    orders = (list(range(n_bits)), [1, 0] + list(range(2, n_bits)))
    half = row_blocks // 2
    block = (2, half, slab, width)
    kept = (n_col // 2,) + block
    split = pl.pallas_call(
        functools.partial(product_kernel, n_row, n_col, (orders[0][0], orders[1][0])),
        out_shape=[shape(kept, f32)] * 2 + [shape(kept, bf16)] * 2,
        in_specs=[SMEM, SMEM] + [VMEM] * 4,
        out_specs=[VMEM] * 4,
        scratch_shapes=[
            pltpu.VMEM((col_blocks * width, 2 * width), bf16),
        ],
        compiler_params=big,
        name="products",
    )(struct_first, struct_second, inv_first, inv_second, stored, pieces)

    linked, consts = pl.pallas_call(
        prepare_kernel,
        out_shape=[shape((width, width), f32), shape((3, slab, width), f32)],
        in_specs=[VMEM] * 3 + [ANY],
        out_specs=[VMEM] * 2,
        scratch_shapes=[pltpu.VMEM((3, width, width), f32)],
        compiler_params=big,
        name="prepare",
        cost_estimate=pl.CostEstimate(flops=6 * 10 * width**3, bytes_accessed=8 * width**2, transcendentals=0),
    )(panel_link, inv_first, inv_second, split[0])

    state = [(split[g], swapped(split[2 + g], "col", n_col, 1 << orders[g][0])) for g in range(2)]
    left = [sorted(set(range(n_bits)) - {order[0]}) for order in orders]
    for i in range(1, n_bits):
        totals, last = [], []
        for g in range(2):
            keep, came = state[g]
            bit = orders[g][i]
            inner = 1 << left[g].index(bit)
            left[g].remove(bit)
            totals.append(keep + came.astype(f32))
            keep, send = halves(totals[g].reshape((-1, 2, inner) + block), 1, ways[bit])
            keep, send = keep.reshape((-1,) + block), send.astype(bf16).reshape((-1,) + block)
            last.append((keep, send))
        if i < n_bits - 1 and orders[0][i] != orders[1][i]:
            state = [(keep, swapped(send, "col", n_col, 1 << order[i])) for (keep, send), order in zip(last, orders)]
        else:
            came = swapped(jnp.stack([send for _, send in last]), "col", n_col, 1 << orders[0][i])
            state = [(keep, came[g]) for g, (keep, _) in enumerate(last)]

    sums = pl.pallas_call(
        functools.partial(sum_kernel, n_bits - 1),
        out_shape=shape((2, n_col, 3, slab, width // 2), f32),
        in_specs=[VMEM] * 4 + [ANY],
        out_specs=VMEM,
        compiler_params=big,
        name="sums",
    )(rows, *totals, linked, consts)
    keep, send = halves(sums, 0, cores)
    sums = keep + swapped(send, "row", n_row, 1)
    tail = (3, slab, width // 2)
    parts = [lax.dynamic_index_in_dim(sums.reshape((-1, 4) + tail), quad, 1, keepdims=False) for quad in quads]
    sums = parts[0]
    for m in range(1, 4):
        sums = sums + swapped(parts[m], "col", n_col, m)
    for bit in range(2, n_bits - 1):
        keep, send = halves(sums.reshape((-1, 2) + tail), 1, ways[bit])
        sums = keep + swapped(send.astype(bf16), "col", n_col, 1 << bit).astype(f32)
    keep, send = (part.astype(bf16) for part in halves(sums.reshape((2,) + tail), 0, ways[n_bits - 1]))
    across = [(r * n_col + c, (r ^ 2) * n_col + (c ^ (n_col // 2))) for r in range(n_row) for c in range(n_col)]
    near = keep.astype(f32) + swapped(send, "col", n_col, n_col // 2).astype(f32)
    far = swapped(keep, "row", n_row, 2).astype(f32) + lax.ppermute(send, ("row", "col"), across).astype(f32)
    mine = near + far
    for bit in range(2, n_row.bit_length() - 1):
        mine = mine + swapped(mine, "row", n_row, 1 << bit)

    mine, state = lax.optimization_barrier((mine, state))
    column_first, column_second = pl.pallas_call(
        functools.partial(column_kernel, n_row),
        out_shape=[shape(panel, f32)] * 2,
        in_specs=[SMEM, SMEM] + [VMEM] * 5,
        out_specs=[VMEM] * 2,
        compiler_params=big,
        name="columns",
    )(struct_first, struct_second, *[part[0] for pair in state for part in pair], linked)

    pair = jnp.stack([mine, swapped(mine, "row", n_row, 1)])
    total = jnp.concatenate([lax.dynamic_index_in_dim(pair, way, 0, keepdims=False) for way in cores], axis=-1)
    diag_first, link_block, diag_second = consts + total
    out = (row_blocks, 1, slab, width)
    return column_first.reshape(out), column_second.reshape(out), diag_first, link_block, diag_second


def solution(mesh):
    placed = (
        P(None, "row", None, "col", None, None),
        P(None, "row", "col", None),
        P(None, "row", "col", None),
        P(),
        P(),
        P(),
        P(),
        P(),
    )
    return jax.shard_map(
        body,
        mesh=mesh,
        in_specs=placed,
        out_specs=(
            P(None, "row", "col", None),
            P(None, "row", "col", None),
            P("col", None),
            P("col", None),
            P("col", None),
        ),
        check_vma=False,
    )
```

```python
import functools

import jax
import jax.numpy as jnp
from jax import lax
from jax.experimental import pallas as pl
from jax.experimental.pallas import tpu as pltpu
from jax.sharding import PartitionSpec as P

precise = lax.Precision.HIGHEST
SMEM = pl.BlockSpec(memory_space=pltpu.SMEM)
VMEM = pl.BlockSpec(memory_space=pltpu.VMEM)
HBM = pl.BlockSpec(memory_space=pltpu.HBM)
ANY = pl.BlockSpec(memory_space=pl.ANY)


def exact_dot(left, right, left_dim=1):
    dims = (((left_dim,), (0,)), ((), ()))
    return lax.dot_general(left, right, dims, precision=precise, preferred_element_type=jnp.float32)


def split_dot(left, right, left_dim=1):
    def halves(value):
        if value.dtype == jnp.bfloat16:
            return [value]
        high = value.astype(jnp.bfloat16)
        return [high, (value - high.astype(jnp.float32)).astype(jnp.bfloat16)]

    dims = (((left_dim,), (0,)), ((), ()))
    total = None
    for i, a in enumerate(halves(left)):
        for j, b in enumerate(halves(right)):
            if i + j < 2:
                term = lax.dot_general(a, b, dims, preferred_element_type=jnp.float32)
                total = term if total is None else total + term
    return total


def listed(struct_ref, blocks, n_row):
    ids = lax.broadcasted_iota(jnp.int32, (blocks, 1, 1), 0) * n_row + lax.axis_index("row")

    def look(place, found):
        return jnp.where(ids == struct_ref[place], 1, found)

    found = lax.fori_loop(0, struct_ref.shape[0], look, jnp.zeros((blocks, 1, 1), jnp.int32))
    return found == 1


def place_of(piece, n_row):
    return piece % n_row, piece // n_row


def product_kernel(n_row, n_col, first_bits, struct1, struct2, inv1, inv2, stored, pieces, *rest):
    cycle = n_col // n_row
    keeps, sends = rest[:2], rest[2:4]
    (factor,) = rest[4:]
    row_blocks = stored.shape[0]
    _, _, _, col_blocks, slab, width = pieces.shape
    packed = jnp.bfloat16 if slab % 16 == 0 else jnp.float32
    here_row, here_col = lax.axis_index("row"), lax.axis_index("col")

    group = here_col // n_row
    places = [(row ^ here_row, lax.rem(turn + group + cycle - 1, cycle)) for turn in range(cycle) for row in range(n_row)]
    for p, (struct, inverse) in enumerate(((struct1, inv1), (struct2, inv2))):

        def look(place, found):
            return tuple(f | (struct[place] == b * n_col + here_col).astype(jnp.int32) for b, f in enumerate(found))

        found = lax.fori_loop(0, struct.shape[0], look, (jnp.int32(0),) * col_blocks)
        slices = [pieces[m, s, p, b].astype(packed) for b in range(col_blocks) for m, s in places]
        blocks = jnp.concatenate(slices, axis=0).astype(jnp.bfloat16)
        product = split_dot(blocks, inverse[...])
        for b in range(col_blocks):
            place = slice(b * width, (b + 1) * width)
            factor[place, p * width : (p + 1) * width] = jnp.where(found[b] == 1, product[place], 0.0).astype(jnp.bfloat16)

    half = row_blocks // 2
    step = 2 if row_blocks % 2 == 0 else 1
    for a in range(0, row_blocks, step):
        wide = [jnp.concatenate([stored[a + i, b] for b in range(col_blocks)], axis=1) for i in range(step)]
        totals = jnp.dot(jnp.concatenate(wide, axis=0), factor[...], preferred_element_type=jnp.float32)
        for i in range(step):
            total = totals[i * width : (i + 1) * width]
            group, place = divmod(a + i, half)
            bit = first_bits[group]
            upper = ((here_col >> bit) & 1) == 1
            for p in range(2):
                for j in range(n_col // 2):
                    low = ((j >> bit) << (bit + 1)) | (j & ((1 << bit) - 1))
                    high = low | (1 << bit)
                    x = total[low * slab : (low + 1) * slab, p * width : (p + 1) * width]
                    y = total[high * slab : (high + 1) * slab, p * width : (p + 1) * width]
                    keeps[group][j, p, place] = jnp.where(upper, y, x)
                    sends[group][j, p, place] = jnp.where(upper, x, y).astype(jnp.bfloat16)


def prepare_kernel(link, inv1, inv2, after, linked, out, whole):
    slab = out.shape[1]
    linked[...] = exact_dot(link[...].astype(jnp.float32), inv2[...])
    link = linked[...]
    gram1 = exact_dot(inv1[...], inv1[...], 0)
    across = exact_dot(gram1, link)
    whole[0] = gram1
    whole[1] = -across
    whole[2] = exact_dot(inv2[...], inv2[...], 0) + exact_dot(link, across, 0)
    place = pl.ds(pl.multiple_of(lax.axis_index("col") * slab, slab), slab)
    out[...] = whole[:, place, :]


def form_kernel(n_row, struct1, struct2, inv1, inv2, base, rows):
    slices, _, blocks, slab, width = base.shape
    for p, (struct, inverse) in enumerate(((struct1, inv1), (struct2, inv2))):
        keep = listed(struct, blocks, n_row)
        flat = base[:, p].astype(jnp.float32).reshape(slices * blocks * slab, width).astype(jnp.bfloat16)
        product = split_dot(flat, inverse[...]).reshape(slices, blocks, slab, width)
        rows[:, p] = jnp.where(keep[None], product, 0.0).astype(jnp.bfloat16)


def sum_kernel(last_bit, rows, total_low, total_high, linked, after, out):
    _, _, half, slab, width = total_low.shape
    mine = (lax.axis_index("col") >> last_bit) & 1

    def gathered(p):
        parts = [total[place, p].reshape(half * slab, width) for place in (mine, 1 - mine) for total in (total_low, total_high)]
        return jnp.concatenate(parts, axis=0)

    def factor(p):
        return rows[:, p].astype(jnp.float32).reshape(-1, width).astype(jnp.bfloat16)

    link = linked[...]
    sum1 = gathered(0)
    u2 = factor(1)
    first = split_dot(factor(0), sum1, 0)
    cross = split_dot(u2, sum1, 0)
    top = cross.T - split_dot(first, link)
    second = split_dot(u2, gathered(1), 0) - split_dot(cross, link) - split_dot(link, top, 0)
    across = width // 2
    for i, part in enumerate((first, top, second)):
        part = part.reshape(width // slab, slab, width)
        for h in range(2):
            out[h, :, i] = part[:, :, h * across : (h + 1) * across]


def column_kernel(n_row, struct1, struct2, kept_low, came_low, kept_high, came_high, linked, column1, column2):
    blocks, slab, width = column1.shape
    sums = []
    for p in range(2):
        parts = [k[p] + c[p].astype(jnp.float32) for k, c in ((kept_low, came_low), (kept_high, came_high))]
        sums.append(jnp.concatenate(parts, axis=0))
    col1 = jnp.where(listed(struct1, blocks, n_row), -sums[0], 0.0)
    column1[...] = col1
    carried = split_dot(col1.reshape(blocks * slab, width), linked[...]).reshape(col1.shape)
    column2[...] = jnp.where(listed(struct2, blocks, n_row), -(sums[1] + carried), 0.0)


def swapped(value, axis, size, mask):
    return lax.ppermute(value, axis, [(i, i ^ mask) for i in range(size)])


def halves(value, axis, ways):
    kept, sent = (lax.dynamic_index_in_dim(value, way, axis, keepdims=False) for way in ways)
    return kept, sent


def body(stored_inverse, panel_first, panel_second, panel_link, inv_first, inv_second, struct_first, struct_second):
    n_row, n_col = lax.axis_size("row"), lax.axis_size("col")
    here_col = lax.axis_index("col")
    row_blocks, _, col_blocks, _, width, _ = stored_inverse.shape
    slab = width // n_col
    cycle = n_col // n_row
    n_bits = n_col.bit_length() - 1
    f32, bf16 = jnp.float32, jnp.bfloat16
    shape = jax.ShapeDtypeStruct
    big = pltpu.CompilerParams(vmem_limit_bytes=12 * 1024 * 1024)
    stored = stored_inverse.reshape(row_blocks, col_blocks, width, width)
    panel = (row_blocks, slab, width)

    panels = [panel_first.reshape(panel), panel_second.reshape(panel)]
    _, turn = place_of(here_col, n_row)
    picks = [((s + 1 - turn + cycle) % cycle).astype(jnp.uint32) for s in range(cycle)]
    ways = [(here_col >> bit) & 1 for bit in range(n_bits)]
    ways = [(way.astype(jnp.uint32), (1 - way).astype(jnp.uint32)) for way in ways]
    core = lax.axis_index("row") & 1
    cores = (core.astype(jnp.uint32), (1 - core).astype(jnp.uint32))
    quads = [(here_col & 3) ^ m for m in range(4)]
    quads = [quad.astype(jnp.uint32) for quad in quads]
    panels, picks, ways, cores, quads = lax.optimization_barrier((panels, picks, ways, cores, quads))

    raw = lax.optimization_barrier(jnp.stack(panels))
    turns = raw.reshape(2, col_blocks, cycle, slab, width)
    got = []
    for s in range(cycle):
        moves = []
        for r in range(n_row):
            for c in range(n_col):
                row, t = place_of(c, n_row)
                moves.append((r * n_col + c, row * n_col + r + (s + 1 - t) % cycle * n_row))
        part = lax.dynamic_index_in_dim(turns, picks[s], 2, keepdims=False)
        got.append(lax.ppermute(part, ("row", "col"), moves))
    base = jnp.stack([raw, swapped(raw, "col", n_col, n_col // 2)])

    pieces = {0: got}
    bit = n_row // 2
    while bit > 1:
        for m, parts in list(pieces.items()):
            pieces[m ^ bit] = [swapped(part, "row", n_row, bit) for part in parts]
        bit //= 2
    pieces = jnp.stack([jnp.stack(pieces[m]) for m in sorted(pieces)])
    pieces, base = lax.optimization_barrier((pieces, base))
    rows = pl.pallas_call(
        functools.partial(form_kernel, n_row),
        out_shape=shape(base.shape, bf16),
        in_specs=[SMEM, SMEM] + [VMEM] * 3,
        out_specs=VMEM,
        compiler_params=big,
        name="form",
        cost_estimate=pl.CostEstimate(flops=8 * width**3, bytes_accessed=4 * width**2, transcendentals=0),
    )(struct_first, struct_second, inv_first, inv_second, base)
    beside, rows = lax.optimization_barrier((swapped(pieces, "row", n_row, 1), rows))
    pieces = jnp.stack([pieces, beside], axis=1).reshape((n_row,) + pieces.shape[1:])

    orders = (list(range(n_bits)), [1, 0] + list(range(2, n_bits)))
    half = row_blocks // 2
    block = (2, half, slab, width)
    kept = (n_col // 2,) + block
    split = pl.pallas_call(
        functools.partial(product_kernel, n_row, n_col, (orders[0][0], orders[1][0])),
        out_shape=[shape(kept, f32)] * 2 + [shape(kept, bf16)] * 2,
        in_specs=[SMEM, SMEM] + [VMEM] * 4,
        out_specs=[VMEM] * 4,
        scratch_shapes=[
            pltpu.VMEM((col_blocks * width, 2 * width), bf16),
        ],
        compiler_params=big,
        name="products",
    )(struct_first, struct_second, inv_first, inv_second, stored, pieces)

    linked, consts = pl.pallas_call(
        prepare_kernel,
        out_shape=[shape((width, width), f32), shape((3, slab, width), f32)],
        in_specs=[VMEM] * 3 + [ANY],
        out_specs=[VMEM] * 2,
        scratch_shapes=[pltpu.VMEM((3, width, width), f32)],
        compiler_params=big,
        name="prepare",
        cost_estimate=pl.CostEstimate(flops=6 * 10 * width**3, bytes_accessed=8 * width**2, transcendentals=0),
    )(panel_link, inv_first, inv_second, split[0])

    state = [(split[g], swapped(split[2 + g], "col", n_col, 1 << orders[g][0])) for g in range(2)]
    left = [sorted(set(range(n_bits)) - {order[0]}) for order in orders]
    for i in range(1, n_bits):
        totals, last = [], []
        for g in range(2):
            keep, came = state[g]
            bit = orders[g][i]
            inner = 1 << left[g].index(bit)
            left[g].remove(bit)
            totals.append(keep + came.astype(f32))
            keep, send = halves(totals[g].reshape((-1, 2, inner) + block), 1, ways[bit])
            keep, send = keep.reshape((-1,) + block), send.astype(bf16).reshape((-1,) + block)
            last.append((keep, send))
        if i < n_bits - 1 and orders[0][i] != orders[1][i]:
            state = [(keep, swapped(send, "col", n_col, 1 << order[i])) for (keep, send), order in zip(last, orders)]
        else:
            came = swapped(jnp.stack([send for _, send in last]), "col", n_col, 1 << orders[0][i])
            state = [(keep, came[g]) for g, (keep, _) in enumerate(last)]

    sums = pl.pallas_call(
        functools.partial(sum_kernel, n_bits - 1),
        out_shape=shape((2, n_col, 3, slab, width // 2), f32),
        in_specs=[VMEM] * 4 + [ANY],
        out_specs=VMEM,
        compiler_params=big,
        name="sums",
    )(rows, *totals, linked, consts)
    keep, send = halves(sums, 0, cores)
    sums = keep + swapped(send, "row", n_row, 1)
    tail = (3, slab, width // 2)
    parts = [lax.dynamic_index_in_dim(sums.reshape((-1, 4) + tail), quad, 1, keepdims=False) for quad in quads]
    sums = parts[0]
    for m in range(1, 4):
        sums = sums + swapped(parts[m].astype(bf16), "col", n_col, m).astype(f32)
    for bit in range(2, n_bits - 1):
        keep, send = halves(sums.reshape((-1, 2) + tail), 1, ways[bit])
        sums = keep + swapped(send.astype(bf16), "col", n_col, 1 << bit).astype(f32)
    sums, state = lax.optimization_barrier((sums, state))
    keep, send = (part.astype(bf16) for part in halves(sums.reshape((2,) + tail), 0, ways[n_bits - 1]))
    across = [(r * n_col + c, (r ^ 2) * n_col + (c ^ (n_col // 2))) for r in range(n_row) for c in range(n_col)]
    near = keep.astype(f32) + swapped(send, "col", n_col, n_col // 2).astype(f32)
    far = swapped(keep, "row", n_row, 2).astype(f32) + lax.ppermute(send, ("row", "col"), across).astype(f32)
    mine = near + far
    for bit in range(2, n_row.bit_length() - 1):
        mine = mine + swapped(mine, "row", n_row, 1 << bit)

    column_first, column_second = pl.pallas_call(
        functools.partial(column_kernel, n_row),
        out_shape=[shape(panel, f32)] * 2,
        in_specs=[SMEM, SMEM] + [VMEM] * 5,
        out_specs=[VMEM] * 2,
        compiler_params=big,
        name="columns",
    )(struct_first, struct_second, *[part[0] for pair in state for part in pair], linked)

    pair = jnp.stack([mine, swapped(mine, "row", n_row, 1)])
    total = jnp.concatenate([lax.dynamic_index_in_dim(pair, way, 0, keepdims=False) for way in cores], axis=-1)
    diag_first, link_block, diag_second = consts + total
    out = (row_blocks, 1, slab, width)
    return column_first.reshape(out), column_second.reshape(out), diag_first, link_block, diag_second


def solution(mesh):
    placed = (
        P(None, "row", None, "col", None, None),
        P(None, "row", "col", None),
        P(None, "row", "col", None),
        P(),
        P(),
        P(),
        P(),
        P(),
    )
    return jax.shard_map(
        body,
        mesh=mesh,
        in_specs=placed,
        out_specs=(
            P(None, "row", "col", None),
            P(None, "row", "col", None),
            P("col", None),
            P("col", None),
            P("col", None),
        ),
        check_vma=False,
    )
```
